32 devices in a mesh: wide: 8 (over z, x), narrow: 4 (over y, core).
Axes of the slice: x: 2, y: 2, z: 4, core: 2. Of those that a mesh axis runs over, the one named last changes fastest.
Arguments:
- block: float32 [4, 1024, 512], P(None, 'wide', 'narrow'), may hold values from -6 to 6
- east_weight: float32 [1024, 512], P('wide', 'narrow'), may hold values from 0.2 to 5
- north_weight: float32 [1024, 512], P('wide', 'narrow'), may hold values from 0.2 to 5
- fine_groups: int32 [1024, 512], P('wide', 'narrow'), may hold values from 0 to 2047
- tiles_one: float32 [512, 4, 128, 128], P(('wide', 'narrow')), as said below
- columns_one: int32 [512, 3], P(('wide', 'narrow')), may hold values from 0 to 79
- live_one: int32 [512, 3], P(('wide', 'narrow')), may hold values 0 or 1
- coarse_groups: int32 [65536], P(('wide', 'narrow')), may hold values from 0 to 255
- tiles_two: float32 [128, 4, 64, 64], P(('wide', 'narrow')), as said below
- columns_two: int32 [128, 3], P(('wide', 'narrow')), may hold values from 0 to 19
- live_two: int32 [128, 3], P(('wide', 'narrow')), may hold values 0 or 1
- coarser_groups: int32 [8192], P(('wide', 'narrow')), may hold values from 0 to 31
- chain_forward: float32 [8, 128, 128], P('wide')
- chain_gain: float32 [8, 128, 128], P('wide')
- chain_backward: float32 [8, 128, 128], P('wide')
Outputs:
- corrected: float32 [4, 1024, 512], P(None, 'wide', 'narrow')
The draws below stay inside these ranges and needn't reach their ends.
Inputs may be any that keep to these rules, and one draw needn't show every extreme that they name: `tiles_one`: in every row tile, slot 0 is the tile of that row tile with itself, and its diagonal entries lie in 1 to 2. `tiles_two`: in every row tile, slot 0 is the tile of that row tile with itself, and its diagonal entries lie in 1 to 2.
All inputs are finite; a program needn't handle non-finite values. No bound on the sum of `live_one` or of `live_two` on one device may be relied on, other than what follows from the above.
Results may differ from the reference program's by a relative error of at most 0.0001.
Values sent between devices are 32-bit elements; how exact they have to be, the bound alone decides.
No kernel may reach another device: no remote copies, remote signals or barrier semaphores. Data moves between devices by JAX's collectives and lax.ppermute only.
A program may use at most 128 MiB of HBM per device.

```python
import math
import jax
import jax.numpy as jnp
from jax import lax

GX = 128
GY = 128
COLS = 4
SLOTS = 4
TB1 = 128
TB2 = 64
NX0 = 1024
NY0 = 512
C1 = 2048
C2 = 256
C3L = 32
NT1 = 16
NT2 = 4
M3 = 128
CHAIN = 8
ROWS1 = 65536
ROWS2 = 8192
ROWS3 = 1024
TILES1 = 512
TILES2 = 128
N_WIDE = 8
N_NARROW = 4


def build_tiles(key, noise, tile_rows, tile_size):
    diagonal = jax.random.uniform(jax.random.fold_in(key, 7), (tile_rows, tile_size), jnp.float32, 1.0, 2.0)
    identity = jnp.eye(tile_size, dtype=jnp.float32)
    first_slot = (lax.broadcasted_iota(jnp.int32, (1, SLOTS, 1, 1), 1) == 0).astype(jnp.float32)
    marker = first_slot * identity
    return noise * (1.0 - marker) + marker * diagonal[:, None, :, None]


def draw_tiles_one(key, part):
    spread = 0.35 / math.sqrt(SLOTS * TB1)
    shape = (TILES1, SLOTS, TB1, TB1)
    noise = jax.random.normal(key, shape, jnp.float32) * spread
    return build_tiles(key, noise, TILES1, TB1)


def draw_tiles_two(key, part):
    spread = 0.35 / math.sqrt(SLOTS * TB2)
    shape = (TILES2, SLOTS, TB2, TB2)
    noise = jax.random.normal(key, shape, jnp.float32) * spread
    return build_tiles(key, noise, TILES2, TB2)


def coupling_draw(key):
    decay = 0.3 ** (1.0 / CHAIN)
    shape = (CHAIN, M3, M3)
    noise = jax.random.normal(key, shape, jnp.float32)
    return decay * noise / math.sqrt(M3)


def draw_chain_forward(key, part):
    return coupling_draw(jax.random.fold_in(key, 11))


def draw_chain_backward(key, part):
    return coupling_draw(jax.random.fold_in(key, 13))


def draw_chain_gain(key, part):
    shape = (CHAIN, M3, M3)
    noise = jax.random.normal(key, shape, jnp.float32)
    diagonal = jax.random.uniform(jax.random.fold_in(key, 5), (CHAIN, M3), jnp.float32, 0.5, 1.5)
    identity = jnp.eye(M3, dtype=jnp.float32)
    return identity[None] * diagonal[:, :, None] + 0.5 * noise / math.sqrt(M3)


def plant(values, rng, low, top_value):
    dims = values.shape
    spot = [jax.random.randint(jax.random.fold_in(rng, axis), (), 0, dims[axis]) for axis in range(len(dims))]
    values = values.at[tuple(spot)].set(low)
    longest = dims.index(max(dims))
    spot[longest] = (spot[longest] + 1) % dims[longest]
    return values.at[tuple(spot)].set(top_value)


def block_scale(key, extent, split, low, largest):
    gain, own = 1.0, jax.random.fold_in(key, 6)
    for position, shards_of in split:
        steps = jnp.exp(jax.random.uniform(jax.random.fold_in(own, position), (shards_of,), jnp.float32, low / len(split), largest / len(split)))
        gain = gain * jnp.repeat(steps, extent[position] // shards_of).reshape([-1 if axis == position else 1 for axis in range(len(extent))])
    return gain


def scatter_about(stream_key, extent, deviation, reach, split=(), kind=jnp.bfloat16):
    loudness = block_scale(stream_key, extent, split, -0.22, 0.18) if split else 1.0
    entries = jax.random.normal(stream_key, extent, jnp.float32) * deviation * loudness
    return jnp.minimum(jnp.maximum(entries, -reach), reach).astype(kind)


def setup_inputs(seed: int = 0) -> dict:
    arg_keys = jax.random.split(jax.random.key(seed), 16)
    block = scatter_about(arg_keys[0], (COLS, NX0, NY0), 1.0, 6.0, ((1, 8), (2, 4)), jnp.float32)
    east_weight = jnp.clip(jnp.exp(math.log(5.0) - 3.218876 * jax.random.uniform(arg_keys[1], (NX0, NY0), jnp.float32) ** block_scale(arg_keys[1], (NX0, NY0), ((0, 8), (1, 4)), -0.2, 0.2)), 0.2, 5.0)
    north_weight = jnp.clip(jnp.exp(math.log(5.0) - 3.218876 * jax.random.uniform(arg_keys[2], (NX0, NY0), jnp.float32) ** block_scale(arg_keys[2], (NX0, NY0), ((0, 8), (1, 4)), -0.2, 0.2)), 0.2, 5.0)
    fine_groups = plant(jax.random.randint(arg_keys[3], (NX0, NY0), 0, C1), jax.random.fold_in(arg_keys[3], 1), 0, C1 - 1).astype(jnp.int32)
    tiles_one = draw_tiles_one(jax.random.fold_in(arg_keys[15], 71), 0)
    columns_one = plant(jax.random.randint(arg_keys[5], (TILES1, SLOTS - 1), 0, 5 * NT1), jax.random.fold_in(arg_keys[5], 1), 0, (5 * NT1) - 1).astype(jnp.int32)
    live_one = plant((jax.random.randint(arg_keys[6], (TILES1, SLOTS - 1), 0, 3) < 2).astype(jnp.int32), jax.random.fold_in(arg_keys[6], 1), 0, 1)
    coarse_groups = plant(jax.random.randint(arg_keys[7], (ROWS1,), 0, C2), jax.random.fold_in(arg_keys[7], 1), 0, C2 - 1).astype(jnp.int32)
    tiles_two = draw_tiles_two(jax.random.fold_in(arg_keys[15], 71), 0)
    columns_two = plant(jax.random.randint(arg_keys[9], (TILES2, SLOTS - 1), 0, 5 * NT2), jax.random.fold_in(arg_keys[9], 1), 0, (5 * NT2) - 1).astype(jnp.int32)
    live_two = plant((jax.random.randint(arg_keys[10], (TILES2, SLOTS - 1), 0, 3) < 2).astype(jnp.int32), jax.random.fold_in(arg_keys[10], 1), 0, 1)
    coarser_groups = plant(jax.random.randint(arg_keys[11], (ROWS2,), 0, C3L), jax.random.fold_in(arg_keys[11], 1), 0, C3L - 1).astype(jnp.int32)
    chain_forward = draw_chain_forward(jax.random.fold_in(arg_keys[15], 71), 0)
    chain_gain = draw_chain_gain(jax.random.fold_in(arg_keys[15], 71), 0)
    chain_backward = draw_chain_backward(jax.random.fold_in(arg_keys[15], 71), 0)
    return dict(block=block, east_weight=east_weight, north_weight=north_weight, fine_groups=fine_groups, tiles_one=tiles_one, columns_one=columns_one, live_one=live_one, coarse_groups=coarse_groups, tiles_two=tiles_two, columns_two=columns_two, live_two=live_two, coarser_groups=coarser_groups, chain_forward=chain_forward, chain_gain=chain_gain, chain_backward=chain_backward)


shift_value = 0.1
jacobi_weight = 0.6
smooth_weight = 0.5


def fine_weights(east_weight, north_weight):
    row_index = lax.broadcasted_iota(jnp.int32, east_weight.shape, 0)
    column_index = lax.broadcasted_iota(jnp.int32, east_weight.shape, 1)
    east_live = jnp.where(row_index < NX0 - 1, east_weight, 0.0)
    north_live = jnp.where(column_index < NY0 - 1, north_weight, 0.0)
    west_live = jnp.pad(east_live, ((1, 0), (0, 0)))[:-1]
    south_live = jnp.pad(north_live, ((0, 0), (1, 0)))[:, :-1]
    diagonal = shift_value + east_live + west_live + north_live + south_live
    return east_live, west_live, north_live, south_live, diagonal


def combine_fine(field, padded, east_live, west_live, north_live, south_live):
    east_side = padded[:, 2:, 1:-1]
    west_side = padded[:, :-2, 1:-1]
    north_side = padded[:, 1:-1, 2:]
    south_side = padded[:, 1:-1, :-2]
    result = shift_value * field + east_live * (field - east_side) + west_live * (field - west_side)
    return result + north_live * (field - north_side) + south_live * (field - south_side)


def tile_product(tiles, blocks, picked):
    own_part = jnp.einsum("rab,crb->cra", tiles[:, 0], blocks, precision=lax.Precision.HIGHEST)
    other_part = jnp.einsum("rkab,crkb->cra", tiles[:, 1:], picked, precision=lax.Precision.HIGHEST)
    return (own_part + other_part).reshape(blocks.shape[0], -1)


def neighbour_targets(columns, tile_count):
    owner = lax.broadcasted_iota(jnp.int32, columns.shape, 0) // tile_count
    wide_pos = owner // N_NARROW
    narrow_pos = owner % N_NARROW
    slot_code = columns // tile_count
    local_tile = columns % tile_count
    step_wide = jnp.where(slot_code == 1, -1, jnp.where(slot_code == 2, 1, 0))
    step_narrow = jnp.where(slot_code == 3, -1, jnp.where(slot_code == 4, 1, 0))
    wide_to = wide_pos + step_wide
    narrow_to = narrow_pos + step_narrow
    inside = (wide_to >= 0) & (wide_to < N_WIDE) & (narrow_to >= 0) & (narrow_to < N_NARROW)
    target = (wide_to * N_NARROW + narrow_to) * tile_count + local_tile
    target = jnp.where(inside, target, 0).astype(jnp.int32)
    return target, inside


def coarse_apply(field, tiles, columns, live, tile_count):
    tile_size = tiles.shape[2]
    blocks = field.reshape(COLS, -1, tile_size)
    target, inside = neighbour_targets(columns, tile_count)
    picked = jnp.take(blocks, target.reshape(-1), axis=1)
    picked = picked.reshape(COLS, columns.shape[0], columns.shape[1], tile_size)
    usable = (inside & (live == 1)).astype(jnp.float32)
    picked = picked * usable[None, :, :, None]
    return tile_product(tiles, blocks, picked)


def segment_total(values, indices, segment_count):
    return jax.ops.segment_sum(values.T, indices, num_segments=segment_count).T


def smooth_cycle(level, right, levels, coarsest):
    if level == len(levels):
        return coarsest(right)
    apply_op, diagonal, restrict_op, prolong_op = levels[level]
    first_iter = jacobi_weight * right / diagonal
    second_iter = first_iter + jacobi_weight * (right - apply_op(first_iter)) / diagonal
    leftover = right - apply_op(second_iter)
    scaled = leftover / diagonal
    coarse_right = restrict_op(leftover - smooth_weight * apply_op(scaled))
    coarse_answer = smooth_cycle(level + 1, coarse_right, levels, coarsest)
    spread = prolong_op(coarse_answer)
    third_iter = second_iter + (spread - smooth_weight * apply_op(spread) / diagonal)
    fourth_iter = third_iter + jacobi_weight * (right - apply_op(third_iter)) / diagonal
    return fourth_iter + jacobi_weight * (right - apply_op(fourth_iter)) / diagonal


def reference(block, east_weight, north_weight, fine_groups, tiles_one, columns_one, live_one, coarse_groups, tiles_two, columns_two, live_two, coarser_groups, chain_forward, chain_gain, chain_backward):
    weights = fine_weights(east_weight, north_weight)
    row_index = lax.broadcasted_iota(jnp.int32, (NX0, NY0), 0)
    column_index = lax.broadcasted_iota(jnp.int32, (NX0, NY0), 1)
    owner = (row_index // GX) * N_NARROW + column_index // GY
    fine_ids = (owner * C1 + fine_groups).reshape(-1).astype(jnp.int32)
    ids_one = ((jnp.arange(ROWS1, dtype=jnp.int32) // C1) * C2 + coarse_groups).astype(jnp.int32)
    ids_two = ((jnp.arange(ROWS2, dtype=jnp.int32) // C2) * C3L + coarser_groups).astype(jnp.int32)

    def apply_fine(field):
        padded = jnp.pad(field, ((0, 0), (1, 1), (1, 1)))
        return combine_fine(field, padded, weights[0], weights[1], weights[2], weights[3])

    def restrict_fine(field):
        return segment_total(field.reshape(COLS, -1), fine_ids, ROWS1)

    def prolong_fine(coarse):
        return jnp.take(coarse, fine_ids, axis=1).reshape(COLS, NX0, NY0)

    def apply_one(field):
        return coarse_apply(field, tiles_one, columns_one, live_one, NT1)

    def restrict_one(field):
        return segment_total(field, ids_one, ROWS2)

    def prolong_one(coarse):
        return jnp.take(coarse, ids_one, axis=1)

    def apply_two(field):
        return coarse_apply(field, tiles_two, columns_two, live_two, NT2)

    def restrict_two(field):
        return segment_total(field, ids_two, ROWS3)

    def prolong_two(coarse):
        return jnp.take(coarse, ids_two, axis=1)

    def chain_solve(right):
        blocks = right.reshape(COLS, N_WIDE, M3).transpose(1, 2, 0)

        def forward(carry, items):
            forward_map, gain_map, piece_now = items
            result = jnp.dot(forward_map, carry, precision=lax.Precision.HIGHEST) + jnp.dot(gain_map, piece_now, precision=lax.Precision.HIGHEST)
            return result, result

        unused, ahead_all = lax.scan(forward, jnp.zeros((M3, COLS), jnp.float32), (chain_forward, chain_gain, blocks))

        def backward(carry, items):
            back_map, piece_now = items
            result = jnp.dot(back_map, carry, precision=lax.Precision.HIGHEST) + piece_now
            return result, result

        unused_two, behind_all = lax.scan(backward, jnp.zeros((M3, COLS), jnp.float32), (chain_backward, ahead_all), reverse=True)
        return behind_all.transpose(2, 0, 1).reshape(COLS, -1)

    diag_one = jnp.diagonal(tiles_one[:, 0], axis1=1, axis2=2).reshape(-1)
    diag_two = jnp.diagonal(tiles_two[:, 0], axis1=1, axis2=2).reshape(-1)
    levels = ((apply_fine, weights[4], restrict_fine, prolong_fine), (apply_one, diag_one, restrict_one, prolong_one), (apply_two, diag_two, restrict_two, prolong_two))
    return smooth_cycle(0, block, levels, chain_solve)
```

```python
import functools

import jax
import jax.numpy as jnp
from jax import lax
from jax.experimental import pallas as pl
from jax.experimental.pallas import tpu as pltpu
from jax.sharding import PartitionSpec as P

F32 = jnp.float32
BF16 = jnp.bfloat16
SHIFT = 0.1
JACOBI = 0.6
LANES = 128
RIM = 4
PAD = 16
VMEM = pl.BlockSpec(memory_space=pltpu.VMEM)
SMEM = pl.BlockSpec(memory_space=pltpu.SMEM)
W_ODD, N_ODD, HAS_WEST, HAS_EAST, HAS_SOUTH, HAS_NORTH, W_AT, N_AT = range(8)


def sds(shape, dtype=F32):
    return jax.ShapeDtypeStruct(shape, dtype)


def call(kernel, outs, ins, scratch=(), specs=None, name=None):
    specs = specs or [VMEM] * len(ins)
    return pl.pallas_call(
        kernel,
        out_shape=outs,
        in_specs=specs,
        out_specs=jax.tree.map(lambda _: VMEM, outs),
        scratch_shapes=list(scratch),
        compiler_params=pltpu.CompilerParams(vmem_limit_bytes=48 * 1024 * 1024),
        name=name,
    )(*ins)


def parts_of(x):
    hi = x.astype(BF16).astype(F32)
    rest = x - hi
    mid = rest.astype(BF16).astype(F32)
    return hi, mid, rest - mid


def rows_of(x):
    return jnp.concatenate([*parts_of(x), jnp.zeros_like(x)], axis=0)


def rows_sum(s, cols):
    return s[0:cols] + s[cols : 2 * cols] + s[2 * cols : 3 * cols]


def dot_nt(a, b):
    return lax.dot_general(a, b, (((1,), (1,)), ((), ())), preferred_element_type=F32)


def store_parts(xs, base, x):
    count, cols, _ = x.shape
    for i, part in enumerate(parts_of(x)):
        xs[pl.ds(base, count), i * cols : (i + 1) * cols, :] = part


def tiles_kernel(tiles_ref, t_ref, d_ref):
    slots, size = tiles_ref.shape[1], tiles_ref.shape[2]
    if size < LANES:
        t_ref[...] = jnp.zeros_like(t_ref)
    for r in range(tiles_ref.shape[0]):
        for k in range(slots):
            tile = tiles_ref[r, k]
            if size < LANES:
                tile = jnp.concatenate([tile, jnp.zeros((size, LANES - size), F32)], axis=1)
            hi = tile.astype(BF16)
            lo = (tile - hi.astype(F32)).astype(BF16)
            t_ref[r, 0:size, k * LANES : (k + 1) * LANES] = hi
            t_ref[r, LANES : LANES + size, k * LANES : (k + 1) * LANES] = lo
            if k == 0:
                row = lax.broadcasted_iota(jnp.int32, tile.shape, 0)
                col = lax.broadcasted_iota(jnp.int32, tile.shape, 1)
                diag = jnp.sum(jnp.where(row == col, tile, 0.0), axis=0, keepdims=True)
                lane = lax.broadcasted_iota(jnp.int32, diag.shape, 1)
                d_ref[r] = jnp.where(lane < size, diag, 1.0)


def split_tiles(tiles):
    count, slots, size, _ = tiles.shape
    step = min(count, 4)
    return pl.pallas_call(
        tiles_kernel,
        grid=(count // step,),
        in_specs=[pl.BlockSpec((step, slots, size, size), lambda i: (i, 0, 0, 0))],
        out_specs=[
            pl.BlockSpec((step, 2 * LANES, slots * LANES), lambda i: (i, 0, 0)),
            pl.BlockSpec((step, 1, LANES), lambda i: (i, 0, 0)),
        ],
        out_shape=[sds((count, 2 * LANES, slots * LANES), BF16), sds((count, 1, LANES))],
        compiler_params=pltpu.CompilerParams(vmem_limit_bytes=32 * 1024 * 1024),
        name="split_tiles",
    )(tiles)


def index_kernel(flags, *refs):
    half = len(refs) // 2
    w_odd, n_odd = flags[W_ODD], flags[N_ODD]
    region = (0, 3 + (1 - w_odd), 3 + w_odd, 1 + (1 - n_odd), 1 + n_odd)
    there = (1, flags[HAS_WEST], flags[HAS_EAST], flags[HAS_SOUTH], flags[HAS_NORTH])
    for level in range(2):
        columns, live, out = refs[2 * level], refs[2 * level + 1], refs[4 + level]
        count, slots = out.shape
        code = columns[...]
        place = jnp.full(code.shape, 5 * count, jnp.int32)
        for s in range(5):
            at = code - s * count
            ok = (at >= 0) & (at < count) & (live[...] == 1) & (there[s] == 1)
            place = jnp.where(ok, at + region[s] * count, place)
        out[:, 1:] = place
        out[:, 0:1] = lax.broadcasted_iota(jnp.int32, (count, 1), 0)


def apply_tiles(t_ref, xs, idx):
    count, slots = idx.shape
    cols = 4
    out = []
    for r in range(count):
        lhs = jnp.concatenate([xs[idx[r, k]] for k in range(slots)], axis=1).astype(BF16)
        both = dot_nt(lhs, t_ref[r])
        out.append(rows_sum(both[:, :LANES] + both[:, LANES:], cols))
    return out


def fill_blocks(xs, own, others, count):
    xs[:, 12:16, :] = jnp.zeros((xs.shape[0], 4, LANES), F32)
    xs[5 * count] = jnp.zeros((16, LANES), F32)
    store_parts(xs, 0, own[0:count])
    for i, other in enumerate(others):
        store_parts(xs, (i + 1) * count, other[0:count])


def smooth_kernel(idx, t, d, b, own, o1, o2, o3, o4, out, xs):
    count = b.shape[0]
    fill_blocks(xs, own, (o1, o2, o3, o4), count)
    for r, ax in enumerate(apply_tiles(t, xs, idx)):
        out[r] = own[r] + JACOBI * (b[r] - ax) / d[r]


def residual_kernel(idx, t, d, b, own, o1, o2, o3, o4, left, scaled, xs):
    count = b.shape[0]
    fill_blocks(xs, own, (o1, o2, o3, o4), count)
    for r, ax in enumerate(apply_tiles(t, xs, idx)):
        rest = b[r] - ax
        left[r] = rest
        scaled[r] = rest / d[r]


def restrict_one_kernel(idx, t, left, groups, d2, own, o1, o2, o3, o4, b2, first, xs):
    count = left.shape[0]
    fill_blocks(xs, own, (o1, o2, o3, o4), count)
    total = None
    coarse_tiles, _, lanes = b2.shape
    size = coarse_tiles * lanes // 2
    for r, ax in enumerate(apply_tiles(t, xs, idx)):
        rows = rows_of(left[r] - 0.5 * ax).astype(BF16)
        hot = lax.broadcasted_iota(jnp.int32, (size, LANES), 0) == groups[r : r + 1, :]
        term = dot_nt(rows, hot.astype(F32).astype(BF16))
        total = term if total is None else total + term
    total = rows_sum(total, 4)
    half = LANES // 2
    lane = lax.broadcasted_iota(jnp.int32, (4, LANES), 1)
    for tile in range(coarse_tiles):
        pair = total[:, (tile // 2) * LANES : (tile // 2 + 1) * LANES]
        if tile % 2:
            pair = pltpu.roll(pair, half, 1)
        value = jnp.where(lane < half, pair, 0.0)
        b2[tile] = value
        first[tile] = JACOBI * value / d2[tile]


def restrict_two_kernel(flags, idx, t, left, groups, own, o1, o2, o3, o4, out, xs):
    count = left.shape[0]
    fill_blocks(xs, own, (o1, o2, o3, o4), count)
    offset = flags[N_AT] * flags[8]
    total = None
    for r, ax in enumerate(apply_tiles(t, xs, idx)):
        rows = rows_of(left[r] - 0.5 * ax).astype(BF16)
        hot = lax.broadcasted_iota(jnp.int32, (LANES, LANES), 0) == groups[r : r + 1, :] + offset
        term = dot_nt(rows, hot.astype(F32).astype(BF16))
        total = term if total is None else total + term
    total = rows_sum(total, 4)
    out[...] = jnp.broadcast_to(total[None], out.shape)


def chain_maps_kernel(flags, maps, out):
    count = maps.shape[0]
    at = flags[W_AT]
    for v in range(count):
        for i in range(3):
            piece = maps[v ^ at, i]
            hi = piece.astype(BF16)
            out[v, i, 0:LANES] = hi
            out[v, i, LANES : 2 * LANES] = (piece - hi.astype(F32)).astype(BF16)


def map_product(m, x):
    both = dot_nt(rows_of(x).astype(BF16), m)
    return rows_sum(both[:, :LANES] + both[:, LANES:], 4)


def take_lanes(table, lanes):
    return jnp.take_along_axis(table, jnp.broadcast_to(lanes, table.shape), axis=1)


def chain_kernel(flags, maps, pieces, idx, t, d, x2, groups, g1, g2, g3, g4, out, xs, ys):
    blocks = maps.shape[0]
    narrow = pieces.shape[0] // blocks
    carry = None
    for v in range(blocks):
        b = pieces[v * narrow]
        for k in range(1, narrow):
            b = b + pieces[v * narrow + k]
        now = map_product(maps[v, 1], b)
        if carry is not None:
            now = now + map_product(maps[v, 0], carry)
        ys[v] = now
        carry = now
    for v in range(blocks - 2, -1, -1):
        carry = ys[v] + map_product(maps[v, 2], carry)
        ys[v] = carry
    count = x2.shape[0]
    xs[5 * count] = jnp.zeros((16, LANES), F32)
    size = flags[8]
    w, n, w_odd, n_odd = flags[W_AT], flags[N_AT], flags[W_ODD], flags[N_ODD]
    n_first = n + 1 - 2 * n_odd
    n_second = jnp.clip(n - 1 + 2 * n_odd, 0, narrow - 1)
    w_first = w + 1 - 2 * w_odd
    w_second = jnp.clip(w - 1 + 2 * w_odd, 0, blocks - 1)
    where = ((w, n), (w, n_first), (w, n_second), (w_first, n), (w_second, n))
    lane = lax.broadcasted_iota(jnp.int32, (16, LANES), 1)
    for p, ((pw, pn), group) in enumerate(zip(where, (groups, g1, g2, g3, g4))):
        table = rows_of(ys[pw])
        for tile in range(count):
            index = (group[tile : tile + 1, :] + pn * size) & (LANES - 1)
            got = take_lanes(table, index)
            xs[p * count + tile] = jnp.where(lane < LANES // 2, got, 0.0)
    for r, ax in enumerate(apply_tiles(t, xs, idx)):
        out[r] = x2[r] + (rows_sum(xs[r], 4) - 0.5 * ax / d[r])


def prolong_one_kernel(idx, t, d, x2, groups, g1, g2, g3, g4, own, o1, o2, o3, o4, out, xs):
    count = x2.shape[0]
    xs[5 * count] = jnp.zeros((16, LANES), F32)
    half = LANES // 2
    lane = lax.broadcasted_iota(jnp.int32, (4, LANES), 1)
    for p, (u, group) in enumerate(
        zip((own, o1, o2, o3, o4), (groups, g1, g2, g3, g4))
    ):
        tables = []
        for i in range(u.shape[0] // 2):
            wide = jnp.where(lane < half, u[2 * i], pltpu.roll(u[2 * i + 1], half, 1))
            tables.append(rows_of(wide))
        for tile in range(count):
            index = group[tile : tile + 1, :]
            got = take_lanes(tables[0], index & (LANES - 1))
            for i in range(1, len(tables)):
                more = take_lanes(tables[i], index & (LANES - 1))
                got = jnp.where((index >> 7) == i, more, got)
            xs[p * count + tile] = got
    for r, ax in enumerate(apply_tiles(t, xs, idx)):
        out[r] = x2[r] + (rows_sum(xs[r], 4) - 0.5 * ax / d[r])


def live_weights(flags, east, north):
    row = lax.broadcasted_iota(jnp.int32, east.shape, 0)
    col = lax.broadcasted_iota(jnp.int32, east.shape, 1)
    east = jnp.where((flags[HAS_EAST] == 1) | (row < east.shape[0] - 1), east, 0.0)
    north = jnp.where((flags[HAS_NORTH] == 1) | (col < north.shape[1] - 1), north, 0.0)
    return east, north


def narrow_rims(flags, fields, first, second):
    odd = flags[N_ODD] == 1
    for i, field in enumerate(fields):
        turned = field.T
        low, high = turned[0:RIM], turned[-RIM:]
        first[i] = jnp.where(odd, low, high)
        second[i] = jnp.where(odd, high, low)


def narrow_sides(flags, first, second, i):
    odd = flags[N_ODD] == 1
    low = jnp.where(odd, first[i], second[i]) * flags[HAS_SOUTH].astype(F32)
    high = jnp.where(odd, second[i], first[i]) * flags[HAS_NORTH].astype(F32)
    return low, high


def with_sides(flags, field, first, second, i):
    low, high = narrow_sides(flags, first, second, i)
    side = jnp.concatenate([high, jnp.zeros((LANES - 2 * RIM, LANES), F32), low], axis=0)
    return jnp.concatenate([field, side.T], axis=1)


def wide_rims(flags, field, i, first, second):
    odd = flags[W_ODD] == 1
    low, high = field[0:RIM], field[-RIM:]
    first[i] = jnp.where(odd, low, high)
    second[i] = jnp.where(odd, high, low)


def with_rows(flags, field, first, second, i):
    odd = flags[W_ODD] == 1
    low = jnp.where(odd, first[i], second[i]) * flags[HAS_WEST].astype(F32)
    high = jnp.where(odd, second[i], first[i]) * flags[HAS_EAST].astype(F32)
    rim = jnp.concatenate([high, jnp.zeros((PAD - 2 * RIM, field.shape[1]), F32), low], axis=0)
    return jnp.concatenate([field, rim], axis=0)


def fine_first_kernel(flags, block, east, north, first, second):
    e, n = live_weights(flags, east[...], north[...])
    narrow_rims(flags, [*(block[c] for c in range(block.shape[0])), e, n], first, second)


def fine_second_kernel(flags, block, east, north, o1, o2, ext, first, second):
    e, n = live_weights(flags, east[...], north[...])
    for i, field in enumerate([*(block[c] for c in range(block.shape[0])), e, n]):
        wider = with_sides(flags, field, o1, o2, i)
        ext[i] = wider
        wide_rims(flags, wider, i, first, second)


def beside(field, e, n):
    rows, lanes = field.shape
    return (
        e * pltpu.roll(field, rows - 1, 0)
        + pltpu.roll(e * field, 1, 0)
        + n * pltpu.roll(field, lanes - 1, 1)
        + pltpu.roll(n * field, 1, 1)
    )


def fine_down_kernel(flags, ext, o1, o2, groups, d1, keep, b1, first, q_ref):
    cols = ext.shape[0] - 2
    rows = ext.shape[1]
    e = with_rows(flags, ext[cols], o1, o2, cols)
    n = with_rows(flags, ext[cols + 1], o1, o2, cols + 1)
    inv = 1.0 / (SHIFT + e + pltpu.roll(e, 1, 0) + n + pltpu.roll(n, 1, 1))
    diag = SHIFT + e + pltpu.roll(e, 1, 0) + n + pltpu.roll(n, 1, 1)
    keep[2 * cols] = e
    keep[2 * cols + 1] = n
    keep[2 * cols + 2] = inv
    for c in range(cols):
        b = with_rows(flags, ext[c], o1, o2, c)
        x1 = JACOBI * b * inv
        x2 = x1 + JACOBI * ((1.0 - JACOBI) * b + beside(x1, e, n)) * inv
        keep[c] = x2
        keep[cols + c] = b
        rest = b - diag * x2 + beside(x2, e, n)
        q = 0.5 * (rest + beside(rest * inv, e, n))
        for i, part in enumerate(parts_of(q[:rows, :LANES])):
            q_ref[i * cols + c] = part
    count = b1.shape[0]
    step = 4

    def add_rows(j, total):
        left, right = [], []
        for k in range(step):
            row = j * step + k
            group = groups[pl.ds(row, 1), :]
            high, low = group >> 7, group & (LANES - 1)
            mask = lax.broadcasted_iota(jnp.int32, (count, LANES), 0) == high
            left.append(
                jnp.concatenate(
                    [
                        jnp.where(mask, q_ref[i, pl.ds(row, 1), :], 0.0).astype(BF16)
                        for i in range(3 * cols)
                    ],
                    axis=0,
                )
            )
            hot = lax.broadcasted_iota(jnp.int32, (LANES, LANES), 0) == low
            right.append(hot.astype(F32).astype(BF16))
        return total + dot_nt(jnp.concatenate(left, axis=1), jnp.concatenate(right, axis=1))

    total = lax.fori_loop(
        0, rows // step, add_rows, jnp.zeros((3 * cols * count, LANES), F32)
    )
    size = cols * count
    total = total[0:size] + total[size : 2 * size] + total[2 * size : 3 * size]
    for c in range(cols):
        value = total[c * count : (c + 1) * count]
        b1[:, c, :] = value
        first[:, c, :] = JACOBI * value / d1[:, 0, :]


def fine_spread_kernel(flags, t, idx, d, b, groups, own, o1, o2, o3, o4, spread, first, second, xs, us):
    count, cols, _ = b.shape
    fill_blocks(xs, own, (o1, o2, o3, o4), count)
    for r, ax in enumerate(apply_tiles(t, xs, idx)):
        us[r] = own[r] + JACOBI * (b[r] - ax) / d[r]
    rows = groups.shape[0]
    for c in range(cols):
        for j in range(rows // 8):
            group = groups[8 * j : 8 * j + 8, :]
            high, low = group >> 7, group & (LANES - 1)
            value = jnp.zeros((8, LANES), F32)
            for h in range(count):
                table = jnp.broadcast_to(us[h, c : c + 1, :], (8, LANES))
                got = jnp.take_along_axis(table, low, axis=1)
                value = jnp.where(high == h, got, value)
            spread[c, 8 * j : 8 * j + 8, :] = value
    narrow_rims(flags, [spread[c] for c in range(cols)], first, second)


def fine_sides_kernel(flags, spread, o1, o2, ext, first, second):
    for c in range(spread.shape[0]):
        wider = with_sides(flags, spread[c], o1, o2, c)
        ext[c] = wider
        wide_rims(flags, wider, c, first, second)


def fine_up_kernel(flags, keep, ext, o1, o2, out):
    cols = out.shape[0]
    e, n, inv = keep[2 * cols], keep[2 * cols + 1], keep[2 * cols + 2]
    for c in range(cols):
        b = keep[cols + c]
        spread = with_rows(flags, ext[c], o1, o2, c)
        x = keep[c] + 0.5 * (spread + beside(spread, e, n) * inv)
        for _ in range(2):
            x = (1.0 - JACOBI) * x + JACOBI * (b + beside(x, e, n)) * inv
        out[c] = x[: out.shape[1], :LANES]


def pairs(start, count):
    out = []
    for i in range(start, count - 1, 2):
        out += [(i, i + 1), (i + 1, i)]
    return out


def routes(wide, narrow):
    narrow_first = pairs(0, narrow)
    narrow_second = pairs(1, narrow) + [(0, narrow - 1), (narrow - 1, 0)]
    wide_first = pairs(0, wide)
    both = [(a * narrow + k, b * narrow + k) for a, b in pairs(1, wide) for k in range(narrow)]
    for a in (0, wide - 1):
        both += [(a * narrow + k, a * narrow + (k ^ 1)) for k in range(narrow)]
    return narrow_first, narrow_second, wide_first, both


def exchange_narrow(first, second, route):
    return lax.ppermute(first, "narrow", route[0]), lax.ppermute(second, "narrow", route[1])


def exchange_wide(first, second, route):
    return (
        lax.ppermute(first, "wide", route[2]),
        lax.ppermute(second, ("wide", "narrow"), route[3]),
    )


def exchange(x, route):
    return (*exchange_narrow(x, x, route), *exchange_wide(x, x, route))


def body(
    sizes,
    block,
    east,
    north,
    fine_groups,
    tiles_one,
    columns_one,
    live_one,
    coarse_groups,
    tiles_two,
    columns_two,
    live_two,
    coarser_groups,
    chain_forward,
    chain_gain,
    chain_backward,
):
    wide, narrow = sizes
    route = routes(wide, narrow)
    w, n = lax.axis_index("wide"), lax.axis_index("narrow")
    cols = block.shape[0]
    rows = block.shape[1]
    count1, slots = tiles_one.shape[:2]
    count2, _, size2, _ = tiles_two.shape
    level3 = chain_forward.shape[-1] // narrow
    flags = jnp.stack(
        [w % 2, n % 2, w > 0, w < wide - 1, n > 0, n < narrow - 1, w, n, jnp.int32(level3)]
    ).astype(jnp.int32)

    rim = sds((cols + 2, RIM, LANES))
    first, second = call(
        fine_first_kernel, [rim, rim], (flags, block, east, north), specs=[SMEM] + [VMEM] * 3
    )
    o1, o2 = exchange_narrow(first, second, route)

    tiles1, d1 = split_tiles(tiles_one)
    tiles2, d2 = split_tiles(tiles_two)
    idx1, idx2 = call(
        index_kernel,
        [sds((count1, slots), jnp.int32), sds((count2, slots), jnp.int32)],
        (flags, columns_one, live_one, columns_two, live_two),
        specs=[SMEM] + [VMEM] * 4,
    )
    maps = jnp.stack([chain_forward, chain_gain, chain_backward], axis=1)
    step = 1
    while step < wide:
        maps = jnp.concatenate(
            [maps, lax.ppermute(maps, "wide", [(i, i ^ step) for i in range(wide)])], axis=0
        )
        step *= 2
    chain = call(
        chain_maps_kernel,
        sds((wide, 3, 2 * LANES, LANES), BF16),
        (flags, maps),
        specs=[SMEM, VMEM],
    )

    rim = sds((cols + 2, RIM, 2 * LANES))
    ext, first, second = call(
        fine_second_kernel,
        [sds((cols + 2, rows, 2 * LANES)), rim, rim],
        (flags, block, east, north, o1, o2),
        specs=[SMEM] + [VMEM] * 5,
    )
    o1, o2 = exchange_wide(first, second, route)
    field1 = sds((count1, cols, LANES))
    field2 = sds((count2, cols, LANES))
    keep, b1, x1 = call(
        fine_down_kernel,
        [sds((2 * cols + 3, rows + PAD, 2 * LANES)), field1, field1],
        (flags, ext, o1, o2, fine_groups, d1),
        scratch=[pltpu.VMEM((3 * cols, rows, LANES), F32)],
        specs=[SMEM] + [VMEM] * 5,
    )

    groups1 = coarse_groups.reshape(count1, LANES)
    groups2 = jnp.pad(coarser_groups.reshape(count2, size2), ((0, 0), (0, LANES - size2)))
    xs1 = [pltpu.VMEM((5 * count1 + 1, 16, LANES), F32)]
    xs2 = [pltpu.VMEM((5 * count2 + 1, 16, LANES), F32)]
    lead = [SMEM]
    near_groups = exchange(jnp.concatenate([groups1, groups2], axis=0), route)
    near1 = tuple(g[:count1] for g in near_groups)
    near2 = tuple(g[count1:] for g in near_groups)

    def smooth(idx, t, d, b, x, xs, like):
        return call(
            smooth_kernel, like, (idx, t, d, b, x, *exchange(x, route)), xs, lead + [VMEM] * 8
        )

    x2 = smooth(idx1, tiles1, d1, b1, x1, xs1, field1)
    left, scaled = call(
        residual_kernel,
        [field1, field1],
        (idx1, tiles1, d1, b1, x2, *exchange(x2, route)),
        xs1,
        lead + [VMEM] * 8,
    )
    b2, y1 = call(
        restrict_one_kernel,
        [field2, field2],
        (idx1, tiles1, left, groups1, d2, scaled, *exchange(scaled, route)),
        xs1,
        lead + [VMEM] * 9,
    )

    y2 = smooth(idx2, tiles2, d2, b2, y1, xs2, field2)
    left, scaled = call(
        residual_kernel,
        [field2, field2],
        (idx2, tiles2, d2, b2, y2, *exchange(y2, route)),
        xs2,
        lead + [VMEM] * 8,
    )
    out3 = call(
        restrict_two_kernel,
        sds((wide * narrow, cols, LANES)),
        (flags, idx2, tiles2, left, groups2, scaled, *exchange(scaled, route)),
        xs2,
        [SMEM, SMEM] + [VMEM] * 8,
    )
    pieces = lax.all_to_all(out3, ("wide", "narrow"), 0, 0)
    y3 = call(
        chain_kernel,
        field2,
        (flags, chain, pieces, idx2, tiles2, d2, y2, groups2, *near2),
        xs2 + [pltpu.VMEM((wide, cols, LANES), F32)],
        [SMEM, VMEM, VMEM, SMEM] + [VMEM] * 8,
    )
    y4 = smooth(idx2, tiles2, d2, b2, y3, xs2, field2)
    y5 = smooth(idx2, tiles2, d2, b2, y4, xs2, field2)

    x3 = call(
        prolong_one_kernel,
        field1,
        (idx1, tiles1, d1, x2, groups1, *near1, y5, *exchange(y5, route)),
        xs1,
        lead + [VMEM] * 13,
    )
    x4 = smooth(idx1, tiles1, d1, b1, x3, xs1, field1)
    rim = sds((cols, RIM, LANES))
    spread, first, second = call(
        fine_spread_kernel,
        [sds((cols, rows, LANES)), rim, rim],
        (flags, tiles1, idx1, d1, b1, fine_groups, x4, *exchange(x4, route)),
        xs1 + [pltpu.VMEM((count1, cols, LANES), F32)],
        [SMEM, VMEM, SMEM] + [VMEM] * 8,
    )
    o1, o2 = exchange_narrow(first, second, route)
    rim = sds((cols, RIM, 2 * LANES))
    ext, first, second = call(
        fine_sides_kernel,
        [sds((cols, rows, 2 * LANES)), rim, rim],
        (flags, spread, o1, o2),
        specs=[SMEM] + [VMEM] * 3,
    )
    o1, o2 = exchange_wide(first, second, route)
    return call(
        fine_up_kernel,
        sds((cols, rows, LANES)),
        (flags, keep, ext, o1, o2),
        specs=[SMEM] + [VMEM] * 4,
    )


def solution(mesh):
    tile = P(("wide", "narrow"), None, None, None)
    pair = P(("wide", "narrow"), None)
    line = P(("wide", "narrow"))
    grid = P("wide", "narrow")
    chain = P("wide", None, None)
    field = P(None, "wide", "narrow")
    in_specs = (
        field, grid, grid, grid, tile, pair, pair, line, tile, pair, pair, line, chain, chain, chain,
    )
    sizes = (mesh.shape["wide"], mesh.shape["narrow"])
    return jax.shard_map(
        functools.partial(body, sizes), mesh=mesh, in_specs=in_specs, out_specs=field, check_vma=False
    )
```

```python
import functools

import jax
import jax.numpy as jnp
from jax import lax
from jax.experimental import pallas as pl
from jax.experimental.pallas import tpu as pltpu
from jax.sharding import PartitionSpec as P

F32 = jnp.float32
BF16 = jnp.bfloat16
SHIFT = 0.1
JACOBI = 0.6
LANES = 128
RIM = 4
PAD = 16
VMEM = pl.BlockSpec(memory_space=pltpu.VMEM)
PLAIN = pl.BlockSpec(memory_space=pltpu.VMEM)
HBM = pl.BlockSpec(memory_space=pl.ANY)
SMEM = pl.BlockSpec(memory_space=pltpu.SMEM)
W_ODD, N_ODD, HAS_WEST, HAS_EAST, HAS_SOUTH, HAS_NORTH, W_AT, N_AT = range(8)


def sds(shape, dtype=F32):
    return jax.ShapeDtypeStruct(shape, dtype)


def constrain(x, spec):
    if spec is VMEM:
        return pltpu.with_memory_space_constraint(x, pltpu.VMEM)
    if spec is HBM or spec is SMEM:
        return pltpu.with_memory_space_constraint(x, pltpu.HBM)
    return x


def call(kernel, outs, ins, scratch=(), specs=None, mib=12, us=2, hold=None, far=(), loose=()):
    hold = {} if hold is None else hold
    outs, tree = jax.tree.flatten(outs)
    specs = specs or [VMEM] * len(ins)
    places = {x: i for i, x in enumerate(ins) if isinstance(x, str)}
    rest = [name for name in hold if name not in places]
    places |= {name: len(ins) + i for i, name in enumerate(rest)}
    inputs = [hold[x] if isinstance(x, str) else x for x in ins] + [hold[name] for name in rest]
    specs = list(specs) + [VMEM] * len(rest)
    inputs = [constrain(x, spec) for x, spec in zip(inputs, specs)]
    count_in, count_out = len(ins), len(outs)
    shapes = [
        o if o in loose else (pltpu.HBM if o in far else pltpu.VMEM)(o.shape, o.dtype) for o in outs
    ]
    shapes += [pltpu.VMEM(hold[name].shape, hold[name].dtype) for name in hold]

    def inner(*refs):
        first = len(inputs)
        kernel(
            *refs[:count_in],
            *refs[first : first + count_out],
            *refs[first + count_out + len(hold) :],
        )

    results = pl.pallas_call(
        inner,
        out_shape=shapes,
        in_specs=specs,
        out_specs=[HBM if o in far else VMEM for o in outs] + [VMEM] * len(hold),
        scratch_shapes=list(scratch),
        input_output_aliases={places[name]: count_out + i for i, name in enumerate(hold)},
        compiler_params=pltpu.CompilerParams(vmem_limit_bytes=mib * 1024 * 1024),
        cost_estimate=pl.CostEstimate(flops=0, bytes_accessed=int(us * 3.5e6), transcendentals=0),
    )(*inputs)
    for name, value in zip(list(hold), results[count_out:]):
        hold[name] = value
    return jax.tree.unflatten(tree, results[:count_out])


def parts_of(x):
    hi = x.astype(BF16).astype(F32)
    rest = x - hi
    mid = rest.astype(BF16).astype(F32)
    return hi, mid, rest - mid


def rows_of(x):
    return jnp.concatenate([*parts_of(x), jnp.zeros_like(x)], axis=0)


def rows_sum(s, cols):
    return s[0:cols] + s[cols : 2 * cols] + s[2 * cols : 3 * cols]


def dot_nt(a, b):
    return lax.dot_general(a, b, (((1,), (1,)), ((), ())), preferred_element_type=F32)


def store_parts(xs, base, x):
    count, cols, _ = x.shape
    for i, part in enumerate(parts_of(x)):
        xs[pl.ds(base, count), i * cols : (i + 1) * cols, :] = part


def tiles_kernel(tiles_ref, t_ref, d_ref, *again):
    slots, size = tiles_ref.shape[1], tiles_ref.shape[2]
    if size < LANES:
        t_ref[...] = jnp.zeros_like(t_ref)
    for r in range(tiles_ref.shape[0]):
        for k in range(slots):
            tile = tiles_ref[r, k]
            if size < LANES:
                tile = jnp.concatenate([tile, jnp.zeros((size, LANES - size), F32)], axis=1)
            hi = tile.astype(BF16)
            lo = (tile - hi.astype(F32)).astype(BF16)
            t_ref[r, 0:size, k * LANES : (k + 1) * LANES] = hi
            t_ref[r, LANES : LANES + size, k * LANES : (k + 1) * LANES] = lo
            if k == 0:
                row = lax.broadcasted_iota(jnp.int32, tile.shape, 0)
                col = lax.broadcasted_iota(jnp.int32, tile.shape, 1)
                diag = jnp.sum(jnp.where(row == col, tile, 0.0), axis=0, keepdims=True)
                lane = lax.broadcasted_iota(jnp.int32, diag.shape, 1)
                d_ref[r] = jnp.where(lane < size, diag, 1.0)
    for ref in again:
        ref[...] = t_ref[...]


def split_tiles(tiles, again):
    count, slots, size, _ = tiles.shape
    step = min(count, 4)
    spec = pl.BlockSpec((step, 2 * LANES, slots * LANES), lambda i: (i, 0, 0))
    shape = (count, 2 * LANES, slots * LANES)
    return pl.pallas_call(
        tiles_kernel,
        grid=(count // step,),
        in_specs=[pl.BlockSpec((step, slots, size, size), lambda i: (i, 0, 0, 0))],
        out_specs=[spec, pl.BlockSpec((step, 1, LANES), lambda i: (i, 0, 0))] + [spec] * again,
        out_shape=[pltpu.VMEM(shape, BF16), pltpu.VMEM((count, 1, LANES), F32)]
        + [pltpu.HBM(shape, BF16)] * again,
        compiler_params=pltpu.CompilerParams(vmem_limit_bytes=16 * 1024 * 1024),
        cost_estimate=pl.CostEstimate(flops=0, bytes_accessed=2 * 4 * tiles.size, transcendentals=0),
        name="split_tiles",
    )(pltpu.with_memory_space_constraint(tiles, pltpu.HBM))


def index_kernel(flags, *refs):
    half = len(refs) // 2
    w_odd, n_odd = flags[W_ODD], flags[N_ODD]
    region = (0, 3 + (1 - w_odd), 3 + w_odd, 1 + (1 - n_odd), 1 + n_odd)
    there = (1, flags[HAS_WEST], flags[HAS_EAST], flags[HAS_SOUTH], flags[HAS_NORTH])
    for level in range(2):
        columns, live, out = refs[2 * level], refs[2 * level + 1], refs[4 + level]
        count, slots = out.shape
        code = columns[...]
        place = jnp.full(code.shape, 5 * count, jnp.int32)
        for s in range(5):
            at = code - s * count
            ok = (at >= 0) & (at < count) & (live[...] == 1) & (there[s] == 1)
            place = jnp.where(ok, at + region[s] * count, place)
        out[:, 1:] = place
        out[:, 0:1] = lax.broadcasted_iota(jnp.int32, (count, 1), 0)


def apply_tiles(t_ref, xs, idx):
    count, slots = idx.shape
    cols = 4
    out = []
    for r in range(count):
        lhs = jnp.concatenate([xs[idx[r, k]] for k in range(slots)], axis=1).astype(BF16)
        both = dot_nt(lhs, t_ref[r])
        out.append(rows_sum(both[:, :LANES] + both[:, LANES:], cols))
    return out


def fill_blocks(xs, own, others, count):
    xs[:, 12:16, :] = jnp.zeros((xs.shape[0], 4, LANES), F32)
    xs[5 * count] = jnp.zeros((16, LANES), F32)
    store_parts(xs, 0, own[0:count])
    for i, other in enumerate(others):
        store_parts(xs, (i + 1) * count, other[0:count])


def smooth_kernel(idx, t, d, b, own, o1, o2, o3, o4, out, xs):
    count = b.shape[0]
    fill_blocks(xs, own, (o1, o2, o3, o4), count)
    for r, ax in enumerate(apply_tiles(t, xs, idx)):
        out[r] = own[r] + JACOBI * (b[r] - ax) / d[r]


def residual_kernel(idx, t, d, b, own, o1, o2, o3, o4, left, scaled, xs):
    count = b.shape[0]
    fill_blocks(xs, own, (o1, o2, o3, o4), count)
    for r, ax in enumerate(apply_tiles(t, xs, idx)):
        rest = b[r] - ax
        left[r] = rest
        scaled[r] = rest / d[r]


def restrict_one_kernel(idx, t, left, groups, d2, own, o1, o2, o3, o4, b2, first, xs):
    count = left.shape[0]
    fill_blocks(xs, own, (o1, o2, o3, o4), count)
    total = None
    coarse_tiles, _, lanes = b2.shape
    size = coarse_tiles * lanes // 2
    for r, ax in enumerate(apply_tiles(t, xs, idx)):
        rows = rows_of(left[r] - 0.5 * ax).astype(BF16)
        hot = lax.broadcasted_iota(jnp.int32, (size, LANES), 0) == groups[r : r + 1, :]
        term = dot_nt(rows, hot.astype(F32).astype(BF16))
        total = term if total is None else total + term
    total = rows_sum(total, 4)
    half = LANES // 2
    lane = lax.broadcasted_iota(jnp.int32, (4, LANES), 1)
    for tile in range(coarse_tiles):
        pair = total[:, (tile // 2) * LANES : (tile // 2 + 1) * LANES]
        if tile % 2:
            pair = pltpu.roll(pair, half, 1)
        value = jnp.where(lane < half, pair, 0.0)
        b2[tile] = value
        first[tile] = JACOBI * value / d2[tile]


def restrict_two_kernel(flags, idx, t, left, groups, own, o1, o2, o3, o4, out, xs):
    count = left.shape[0]
    fill_blocks(xs, own, (o1, o2, o3, o4), count)
    offset = flags[N_AT] * flags[8]
    total = None
    for r, ax in enumerate(apply_tiles(t, xs, idx)):
        rows = rows_of(left[r] - 0.5 * ax).astype(BF16)
        hot = lax.broadcasted_iota(jnp.int32, (LANES, LANES), 0) == groups[r : r + 1, :] + offset
        term = dot_nt(rows, hot.astype(F32).astype(BF16))
        total = term if total is None else total + term
    total = rows_sum(total, 4)
    out[...] = jnp.broadcast_to(total[None], out.shape)


def chain_maps_kernel(order, flags, *refs):
    *pieces, out = refs
    position = -1
    for piece in pieces:
        rows = piece.shape[2]
        for k in range(piece.shape[0]):
            position += 1
            v, q = flags[W_AT], flags[N_AT]
            for bit, (axis, step) in enumerate(order):
                if position >> bit & 1:
                    v, q = (v ^ step, q) if axis == "wide" else (v, q ^ step)
            for i in range(3):
                value = piece[k, i]
                hi = value.astype(BF16)
                at = pl.multiple_of(q * rows, rows)
                out[v, i, pl.ds(at, rows), :] = hi
                at = pl.multiple_of(LANES + q * rows, rows)
                out[v, i, pl.ds(at, rows), :] = (value - hi.astype(F32)).astype(BF16)


def map_product(m, x):
    both = dot_nt(rows_of(x).astype(BF16), m)
    return rows_sum(both[:, :LANES] + both[:, LANES:], 4)


def take_lanes(table, lanes):
    return jnp.take_along_axis(table, jnp.broadcast_to(lanes, table.shape), axis=1)


def groups_kernel(own1, own2, o1, o2, o3, o4, out):
    count1, count2 = own1.shape[0], own2.shape[0]
    out[0, 0:count1] = own1[...]
    out[0, count1:] = own2[...]
    for p, ref in enumerate((o1, o2, o3, o4)):
        cols = ref.shape[1]
        for i in range(count1 + count2):
            row = ref[count1 + i // cols, i % cols : i % cols + 1, :]
            out[p + 1, i : i + 1] = row.astype(jnp.int32)


def chain_kernel(flags, maps, pieces, idx, t, d, x2, groups, out, xs, ys):
    blocks = maps.shape[0]
    narrow = pieces.shape[0] // blocks
    carry = None
    for v in range(blocks):
        b = pieces[v * narrow]
        for k in range(1, narrow):
            b = b + pieces[v * narrow + k]
        now = map_product(maps[v, 1], b)
        if carry is not None:
            now = now + map_product(maps[v, 0], carry)
        ys[v] = now
        carry = now
    for v in range(blocks - 2, -1, -1):
        carry = ys[v] + map_product(maps[v, 2], carry)
        ys[v] = carry
    count = x2.shape[0]
    xs[5 * count] = jnp.zeros((16, LANES), F32)
    size = flags[8]
    w, n, w_odd, n_odd = flags[W_AT], flags[N_AT], flags[W_ODD], flags[N_ODD]
    n_first = n + 1 - 2 * n_odd
    n_second = jnp.clip(n - 1 + 2 * n_odd, 0, narrow - 1)
    w_first = w + 1 - 2 * w_odd
    w_second = jnp.clip(w - 1 + 2 * w_odd, 0, blocks - 1)
    where = ((w, n), (w, n_first), (w, n_second), (w_first, n), (w_second, n))
    lane = lax.broadcasted_iota(jnp.int32, (16, LANES), 1)
    first = groups.shape[1] - count
    for p, (pw, pn) in enumerate(where):
        table = rows_of(ys[pw])
        for tile in range(count):
            index = groups[p, first + tile : first + tile + 1, :]
            index = (index + pn * size) & (LANES - 1)
            got = take_lanes(table, index)
            xs[p * count + tile] = jnp.where(lane < LANES // 2, got, 0.0)
    for r, ax in enumerate(apply_tiles(t, xs, idx)):
        out[r] = x2[r] + (rows_sum(xs[r], 4) - 0.5 * ax / d[r])


def prolong_one_kernel(idx, t, d, x2, groups, own, o1, o2, o3, o4, out, xs):
    count = x2.shape[0]
    xs[5 * count] = jnp.zeros((16, LANES), F32)
    half = LANES // 2
    lane = lax.broadcasted_iota(jnp.int32, (4, LANES), 1)
    for p, u in enumerate((own, o1, o2, o3, o4)):
        tables = []
        for i in range(u.shape[0] // 2):
            wide = jnp.where(lane < half, u[2 * i], pltpu.roll(u[2 * i + 1], half, 1))
            tables.append(rows_of(wide))
        for tile in range(count):
            index = groups[p, tile : tile + 1, :]
            got = take_lanes(tables[0], index & (LANES - 1))
            for i in range(1, len(tables)):
                more = take_lanes(tables[i], index & (LANES - 1))
                got = jnp.where((index >> 7) == i, more, got)
            xs[p * count + tile] = got
    for r, ax in enumerate(apply_tiles(t, xs, idx)):
        out[r] = x2[r] + (rows_sum(xs[r], 4) - 0.5 * ax / d[r])


def live_weights(flags, east, north):
    row = lax.broadcasted_iota(jnp.int32, east.shape, 0)
    col = lax.broadcasted_iota(jnp.int32, east.shape, 1)
    east = jnp.where((flags[HAS_EAST] == 1) | (row < east.shape[0] - 1), east, 0.0)
    north = jnp.where((flags[HAS_NORTH] == 1) | (col < north.shape[1] - 1), north, 0.0)
    return east, north


def narrow_rims(flags, fields, first, second):
    odd = flags[N_ODD] == 1
    for i, field in enumerate(fields):
        turned = field.T
        low, high = turned[0:RIM], turned[-RIM:]
        first[i] = jnp.where(odd, low, high)
        second[i] = jnp.where(odd, high, low)


def narrow_sides(flags, first, second, i):
    odd = flags[N_ODD] == 1
    low = jnp.where(odd, first[i], second[i]) * flags[HAS_SOUTH].astype(F32)
    high = jnp.where(odd, second[i], first[i]) * flags[HAS_NORTH].astype(F32)
    return low, high


def with_sides(flags, field, first, second, i):
    low, high = narrow_sides(flags, first, second, i)
    side = jnp.concatenate([high, jnp.zeros((LANES - 2 * RIM, LANES), F32), low], axis=0)
    return jnp.concatenate([field, side.T], axis=1)


def wide_rims(flags, field, i, first, second):
    odd = flags[W_ODD] == 1
    low, high = field[0:RIM], field[-RIM:]
    first[i] = jnp.where(odd, low, high)
    second[i] = jnp.where(odd, high, low)


def with_rows(flags, field, first, second, i):
    odd = flags[W_ODD] == 1
    low = jnp.where(odd, first[i], second[i]) * flags[HAS_WEST].astype(F32)
    high = jnp.where(odd, second[i], first[i]) * flags[HAS_EAST].astype(F32)
    rim = jnp.concatenate([high, jnp.zeros((PAD - 2 * RIM, field.shape[1]), F32), low], axis=0)
    return jnp.concatenate([field, rim], axis=0)


def fine_first_kernel(
    flags, block, east, north, forward, gain, backward, fields, first, second, piece, edges, sems
):
    cols = block.shape[0]
    rows = piece.shape[2]
    at = pl.multiple_of(flags[N_AT] * rows, rows)
    copies = [
        (block, fields.at[0:cols]),
        (east, edges.at[0]),
        (north, edges.at[1]),
        *((m.at[0, pl.ds(at, rows)], piece.at[0, i]) for i, m in enumerate((forward, gain, backward))),
    ]
    copies = [pltpu.make_async_copy(a, b, sems.at[i]) for i, (a, b) in enumerate(copies)]
    for copy in copies:
        copy.start()
    for copy in copies:
        copy.wait()
    fields[cols], fields[cols + 1] = live_weights(flags, edges[0], edges[1])
    narrow_rims(flags, [fields[c] for c in range(cols + 2)], first, second)


def fine_second_kernel(flags, fields, o1, o2, ext, first, second):
    for i in range(fields.shape[0]):
        wider = with_sides(flags, fields[i], o1, o2, i)
        ext[i] = wider
        wide_rims(flags, wider, i, first, second)


def beside(field, e, n):
    rows, lanes = field.shape
    return (
        e * pltpu.roll(field, rows - 1, 0)
        + pltpu.roll(e * field, 1, 0)
        + n * pltpu.roll(field, lanes - 1, 1)
        + pltpu.roll(n * field, 1, 1)
    )


def fine_down_kernel(flags, ext, o1, o2, groups, d1, near1, near2, far, b1, first, q_ref, keep, sem):
    cols = ext.shape[0] - 2
    rows = ext.shape[1]
    e = with_rows(flags, ext[cols], o1, o2, cols)
    n = with_rows(flags, ext[cols + 1], o1, o2, cols + 1)
    inv = 1.0 / (SHIFT + e + pltpu.roll(e, 1, 0) + n + pltpu.roll(n, 1, 1))
    diag = SHIFT + e + pltpu.roll(e, 1, 0) + n + pltpu.roll(n, 1, 1)
    keep[2 * cols] = e
    keep[2 * cols + 1] = n
    keep[2 * cols + 2] = inv
    for c in range(cols):
        b = with_rows(flags, ext[c], o1, o2, c)
        x1 = JACOBI * b * inv
        x2 = x1 + JACOBI * ((1.0 - JACOBI) * b + beside(x1, e, n)) * inv
        keep[c] = x2
        keep[cols + c] = b
        rest = b - diag * x2 + beside(x2, e, n)
        q = 0.5 * (rest + beside(rest * inv, e, n))
        for i, part in enumerate(parts_of(q[:rows, :LANES])):
            q_ref[i * cols + c] = part
    copy = pltpu.make_async_copy(keep, far, sem.at[0])
    copy.start()
    count = b1.shape[0]
    step = 4

    def add_rows(j, total):
        left, right = [], []
        for k in range(step):
            row = j * step + k
            group = groups[pl.ds(row, 1), :]
            high, low = group >> 7, group & (LANES - 1)
            mask = lax.broadcasted_iota(jnp.int32, (count, LANES), 0) == high
            left.append(
                jnp.concatenate(
                    [
                        jnp.where(mask, q_ref[i, pl.ds(row, 1), :], 0.0).astype(BF16)
                        for i in range(3 * cols)
                    ],
                    axis=0,
                )
            )
            hot = lax.broadcasted_iota(jnp.int32, (LANES, LANES), 0) == low
            right.append(hot.astype(F32).astype(BF16))
        return total + dot_nt(jnp.concatenate(left, axis=1), jnp.concatenate(right, axis=1))

    total = lax.fori_loop(
        0, rows // step, add_rows, jnp.zeros((3 * cols * count, LANES), F32)
    )
    size = cols * count
    total = total[0:size] + total[size : 2 * size] + total[2 * size : 3 * size]
    for c in range(cols):
        value = total[c * count : (c + 1) * count]
        b1[:, c, :] = value
        first[0:count, c, :] = JACOBI * value / d1[:, 0, :]
    groups = [near1[i : i + 1, :] for i in range(count)] + [
        near2[i : i + 1, :] for i in range(near2.shape[0])
    ]
    for i, group in enumerate(groups):
        first[count + i // cols, i % cols : i % cols + 1, :] = group.astype(F32)
    copy.wait()


def fine_spread_kernel(flags, t, idx, d, b, groups, own, o1, o2, o3, o4, spread, first, second, xs, us):
    count, cols, _ = b.shape
    fill_blocks(xs, own, (o1, o2, o3, o4), count)
    for r, ax in enumerate(apply_tiles(t, xs, idx)):
        us[r] = own[r] + JACOBI * (b[r] - ax) / d[r]
    rows = groups.shape[0]
    for c in range(cols):
        for j in range(rows // 8):
            group = groups[8 * j : 8 * j + 8, :]
            high, low = group >> 7, group & (LANES - 1)
            value = jnp.zeros((8, LANES), F32)
            for h in range(count):
                table = jnp.broadcast_to(us[h, c : c + 1, :], (8, LANES))
                got = jnp.take_along_axis(table, low, axis=1)
                value = jnp.where(high == h, got, value)
            spread[c, 8 * j : 8 * j + 8, :] = value
    narrow_rims(flags, [spread[c] for c in range(cols)], first, second)


def fine_up_kernel(flags, keep, ext, o1, o2, far, out, sems):
    cols = out.shape[0]
    copies = []
    e, n, inv = keep[2 * cols], keep[2 * cols + 1], keep[2 * cols + 2]
    for c in range(cols):
        b = keep[cols + c]
        spread = with_rows(flags, ext[c], o1, o2, c)
        x = keep[c] + 0.5 * (spread + beside(spread, e, n) * inv)
        for _ in range(2):
            x = (1.0 - JACOBI) * x + JACOBI * (b + beside(x, e, n)) * inv
        out[c] = x[: out.shape[1], :LANES]
        copies.append(pltpu.make_async_copy(out.at[c], far.at[c], sems.at[c]))
        copies[-1].start()
    for copy in copies:
        copy.wait()


def pairs(start, count):
    out = []
    for i in range(start, count - 1, 2):
        out += [(i, i + 1), (i + 1, i)]
    return out


def routes(wide, narrow):
    narrow_first = pairs(0, narrow)
    narrow_second = pairs(1, narrow) + [(0, narrow - 1), (narrow - 1, 0)]
    wide_first = pairs(0, wide)
    both = [(a * narrow + k, b * narrow + k) for a, b in pairs(1, wide) for k in range(narrow)]
    for a in (0, wide - 1):
        both += [(a * narrow + k, a * narrow + (k ^ 1)) for k in range(narrow)]
    return narrow_first, narrow_second, wide_first, both


def exchange_narrow(first, second, route):
    return lax.ppermute(first, "narrow", route[0]), lax.ppermute(second, "narrow", route[1])


def exchange_wide(first, second, route):
    return (
        lax.ppermute(first, "wide", route[2]),
        lax.ppermute(second, ("wide", "narrow"), route[3]),
    )


def exchange(x, route):
    return (*exchange_narrow(x, x, route), *exchange_wide(x, x, route))


def body(
    sizes,
    block,
    east,
    north,
    fine_groups,
    tiles_one,
    columns_one,
    live_one,
    coarse_groups,
    tiles_two,
    columns_two,
    live_two,
    coarser_groups,
    chain_forward,
    chain_gain,
    chain_backward,
):
    wide, narrow = sizes
    route = routes(wide, narrow)
    w, n = lax.axis_index("wide"), lax.axis_index("narrow")
    cols = block.shape[0]
    rows = block.shape[1]
    count1, slots = tiles_one.shape[:2]
    count2, _, size2, _ = tiles_two.shape
    level3 = chain_forward.shape[-1] // narrow
    flags = jnp.stack(
        [w % 2, n % 2, w > 0, w < wide - 1, n > 0, n < narrow - 1, w, n, jnp.int32(level3)]
    ).astype(jnp.int32)

    order = [("wide", 1 << i) for i in reversed(range((wide - 1).bit_length()))]
    order += [("narrow", 1 << i) for i in reversed(range((narrow - 1).bit_length()))]
    share = chain_forward.shape[1] // narrow
    held = []
    done = []

    def swap(x, axis, step):
        return lax.ppermute(x, axis, [(i, i ^ step) for i in range(lax.axis_size(axis))])

    def gather_step(*anchor):
        step = order[len(done)]
        merged = held if len(done) == len(order) - 1 or len(held) == 1 else [jnp.concatenate(held, axis=0)]
        merged, anchor = lax.optimization_barrier((merged, anchor))
        held[:] = merged + [swap(m, *step) for m in merged]
        done.append(step)
        return anchor

    rim = sds((cols + 2, RIM, LANES))
    fields, first, second, piece = call(
        fine_first_kernel,
        [sds((cols + 2, rows, LANES)), rim, rim, sds((1, 3, share, LANES))],
        (flags, block, east, north, chain_forward, chain_gain, chain_backward),
        scratch=[pltpu.VMEM((2, rows, LANES), F32), pltpu.SemaphoreType.DMA((6,))],
        specs=[SMEM] + [HBM] * 6,
    )
    held.append(piece)
    first, second = gather_step(first, second)
    o1, o2 = exchange_narrow(first, second, route)

    idx1, idx2 = call(
        index_kernel,
        [sds((count1, slots), jnp.int32), sds((count2, slots), jnp.int32)],
        (flags, columns_one, live_one, columns_two, live_two),
        specs=[SMEM] + [VMEM] * 4,
        us=0.5,
    )
    tiles2, d2 = split_tiles(tiles_two, 0)
    groups1 = coarse_groups.reshape(count1, LANES)
    groups2 = jnp.pad(coarser_groups.reshape(count2, size2), ((0, 0), (0, LANES - size2)))
    o1, idx1, idx2, tiles2, d2, groups1, groups2 = lax.optimization_barrier(
        (o1, idx1, idx2, tiles2, d2, groups1, groups2)
    )

    rim = sds((cols + 2, RIM, 2 * LANES))
    ext, first, second = call(
        fine_second_kernel,
        [sds((cols + 2, rows, 2 * LANES)), rim, rim],
        (flags, fields, o1, o2),
        specs=[SMEM] + [VMEM] * 3,
    )
    first, second = gather_step(first, second)
    o1, o2 = exchange_wide(first, second, route)
    field1 = sds((count1, cols, LANES))
    field2 = sds((count2, cols, LANES))
    tiles1, d1, tiles1_far = split_tiles(tiles_one, 1)
    more = -(-(count1 + count2) // cols)
    hold = {"t1": tiles1, "d1": d1}
    kept = sds((2 * cols + 3, rows + PAD, 2 * LANES))
    keep, b1, x1 = call(
        fine_down_kernel,
        [kept, field1, sds((count1 + more, cols, LANES))],
        (flags, ext, o1, o2, fine_groups, "d1", groups1, groups2),
        scratch=[
            pltpu.VMEM((3 * cols, rows, LANES), F32),
            pltpu.VMEM(kept.shape, F32),
            pltpu.SemaphoreType.DMA((1,)),
        ],
        specs=[SMEM] + [VMEM] * 7,
        mib=16,
        us=7,
        hold=hold,
        far=(kept,),
    )
    hold["b1"] = b1

    xs1 = [pltpu.VMEM((5 * count1 + 1, 16, LANES), F32)]
    xs2 = [pltpu.VMEM((5 * count2 + 1, 16, LANES), F32)]
    lead = [SMEM]

    def smooth(level, x):
        idx, like, xs = (idx1, field1, xs1) if level == 1 else (idx2, field2, xs2)
        near = exchange(x, route)
        ins = (idx, f"t{level}", f"d{level}", f"b{level}", x, *near)
        return call(smooth_kernel, like, ins, xs, lead + [VMEM] * 8, hold=hold), near

    (x1,) = gather_step(x1)
    x2, near = smooth(1, x1)
    groups = call(
        groups_kernel,
        sds((5, count1 + count2, LANES), jnp.int32),
        (groups1, groups2, *near),
        specs=[VMEM] * 6,
        us=1,
    )
    (x2,) = gather_step(x2)
    near = exchange(x2, route)
    hold |= {"x2": x2, "groups": groups, "d2": d2}
    left, scaled = call(
        residual_kernel,
        [field1, field1],
        (idx1, "t1", "d1", "b1", "x2", *near),
        xs1,
        lead + [VMEM] * 8,
        hold=hold,
    )
    while len(done) < len(order):
        (scaled,) = gather_step(scaled)
    b2, y1 = call(
        restrict_one_kernel,
        [field2, field2],
        (idx1, "t1", left, groups1, "d2", scaled, *exchange(scaled, route)),
        xs1,
        lead + [VMEM] * 9,
        hold=hold,
    )

    del hold["t1"]
    hold |= {"b2": b2, "t2": tiles2}
    y2, _ = smooth(2, y1)
    maps, y2 = lax.optimization_barrier((held, y2))
    near = exchange(y2, route)
    chain_shape = sds((wide, 3, 2 * LANES, LANES), BF16)
    big = wide > 16
    chain = call(
        functools.partial(chain_maps_kernel, order),
        chain_shape,
        (flags, *maps),
        specs=[SMEM] + [PLAIN if big else VMEM] * len(maps),
        mib=48 if big else 12,
        us=0.7,
        loose=(chain_shape,) if big else (),
    )
    if not big:
        hold["chain"] = chain
    hold["y2"] = y2
    left, scaled = call(
        residual_kernel,
        [field2, field2],
        (idx2, "t2", "d2", "b2", "y2", *near),
        xs2,
        lead + [VMEM] * 8,
        us=1,
        hold=hold,
    )
    out3 = call(
        restrict_two_kernel,
        sds((wide * narrow, cols, LANES)),
        (flags, idx2, "t2", left, groups2, scaled, *exchange(scaled, route)),
        xs2,
        [SMEM, SMEM] + [VMEM] * 8,
        hold=hold,
    )
    pieces = lax.all_to_all(out3, ("wide", "narrow"), 0, 0)
    y3 = call(
        chain_kernel,
        field2,
        (flags, chain if big else "chain", pieces, idx2, "t2", "d2", "y2", "groups"),
        xs2 + [pltpu.VMEM((wide, cols, LANES), F32)],
        [SMEM, PLAIN if big else VMEM, VMEM, SMEM] + [VMEM] * 4,
        mib=32 if big else 12,
        us=3,
        hold=hold,
    )
    hold.pop("chain", None)
    y4, _ = smooth(2, y3)
    y5, _ = smooth(2, y4)

    for name in ("t2", "d2", "b2", "y2"):
        del hold[name]
    hold["t1"] = tiles1_far
    x3 = call(
        prolong_one_kernel,
        field1,
        (idx1, "t1", "d1", "x2", "groups", y5, *exchange(y5, route)),
        xs1,
        lead + [VMEM] * 9,
        hold=hold,
    )
    del hold["x2"], hold["groups"]
    x4, _ = smooth(1, x3)
    rim = sds((cols, RIM, LANES))
    spread, first, second = call(
        fine_spread_kernel,
        [sds((cols, rows, LANES)), rim, rim],
        (flags, "t1", idx1, "d1", "b1", fine_groups, x4, *exchange(x4, route)),
        xs1 + [pltpu.VMEM((count1, cols, LANES), F32)],
        [SMEM, VMEM, SMEM] + [VMEM] * 8,
        us=3,
        hold=hold,
    )
    o1, o2 = exchange_narrow(first, second, route)
    rim = sds((cols, RIM, 2 * LANES))
    for name in ("t1", "d1", "b1"):
        del hold[name]
    ext, first, second = call(
        fine_second_kernel,
        [sds((cols, rows, 2 * LANES)), rim, rim],
        (flags, spread, o1, o2),
        specs=[SMEM] + [VMEM] * 3,
        us=1,
        hold=hold,
    )
    o1, o2 = exchange_wide(first, second, route)
    whole = sds((cols, rows, LANES))
    return call(
        fine_up_kernel,
        whole,
        (flags, keep, ext, o1, o2),
        scratch=[pltpu.VMEM(whole.shape, F32), pltpu.SemaphoreType.DMA((cols,))],
        specs=[SMEM] + [VMEM] * 4,
        far=(whole,),
    )


def solution(mesh):
    tile = P(("wide", "narrow"), None, None, None)
    pair = P(("wide", "narrow"), None)
    line = P(("wide", "narrow"))
    grid = P("wide", "narrow")
    chain = P("wide", None, None)
    field = P(None, "wide", "narrow")
    in_specs = (
        field, grid, grid, grid, tile, pair, pair, line, tile, pair, pair, line, chain, chain, chain,
    )
    sizes = (mesh.shape["wide"], mesh.shape["narrow"])
    return jax.shard_map(
        functools.partial(body, sizes), mesh=mesh, in_specs=in_specs, out_specs=field, check_vma=False
    )
```

```python
import functools

import jax
import jax.numpy as jnp
from jax import lax
from jax.experimental import pallas as pl
from jax.experimental.pallas import tpu as pltpu
from jax.sharding import PartitionSpec as P

F32 = jnp.float32
BF16 = jnp.bfloat16
SHIFT = 0.1
JACOBI = 0.6
LANES = 128
RIM = 4
PAD = 16
VMEM = pl.BlockSpec(memory_space=pltpu.VMEM)
PLAIN = pl.BlockSpec(memory_space=pltpu.VMEM)
HBM = pl.BlockSpec(memory_space=pl.ANY)
SMEM = pl.BlockSpec(memory_space=pltpu.SMEM)
W_ODD, N_ODD, HAS_WEST, HAS_EAST, HAS_SOUTH, HAS_NORTH, W_AT, N_AT, LEVEL3 = range(9)


def sds(shape, dtype=F32):
    return jax.ShapeDtypeStruct(shape, dtype)


def constrain(x, spec):
    if spec is VMEM:
        return pltpu.with_memory_space_constraint(x, pltpu.VMEM)
    if spec is HBM:
        return pltpu.with_memory_space_constraint(x, pltpu.HBM)
    if spec is SMEM:
        return pltpu.with_memory_space_constraint(x, pltpu.SMEM)
    return x


def call(kernel, outs, ins, scratch=(), specs=None, mib=12, us=2, hold=None, far=(), loose=(), scalars=()):
    hold = {} if hold is None else hold
    outs, tree = jax.tree.flatten(outs)
    specs = specs or [VMEM] * len(ins)
    places = {x: i for i, x in enumerate(ins) if isinstance(x, str)}
    rest = [name for name in hold if name not in places]
    places |= {name: len(ins) + i for i, name in enumerate(rest)}
    inputs = [hold[x] if isinstance(x, str) else x for x in ins] + [hold[name] for name in rest]
    specs = list(specs) + [VMEM] * len(rest)
    inputs = [constrain(x, spec) for x, spec in zip(inputs, specs)]
    count_in, count_out = len(ins), len(outs)
    spaces = [pltpu.HBM if i in far else pltpu.SMEM if i in scalars else pltpu.VMEM for i in range(len(outs))]
    shapes = [o if i in loose else spaces[i](o.shape, o.dtype) for i, o in enumerate(outs)]
    shapes += [pltpu.VMEM(hold[name].shape, hold[name].dtype) for name in hold]

    def inner(*refs):
        first = len(inputs)
        kernel(
            *refs[:count_in],
            *refs[first : first + count_out],
            *refs[first + count_out + len(hold) :],
        )

    results = pl.pallas_call(
        inner,
        out_shape=shapes,
        in_specs=specs,
        out_specs=[{pltpu.HBM: HBM, pltpu.SMEM: SMEM, pltpu.VMEM: VMEM}[space] for space in spaces]
        + [VMEM] * len(hold),
        scratch_shapes=list(scratch),
        input_output_aliases={places[name]: count_out + i for i, name in enumerate(hold)},
        compiler_params=pltpu.CompilerParams(vmem_limit_bytes=mib * 1024 * 1024),
        cost_estimate=pl.CostEstimate(flops=0, bytes_accessed=int(us * 3.5e6), transcendentals=0),
    )(*inputs)
    for name, value in zip(list(hold), results[count_out:]):
        hold[name] = value
    return jax.tree.unflatten(tree, results[:count_out])


def parts_of(x):
    hi = x.astype(BF16).astype(F32)
    return hi, x - hi


def rows_of(x):
    return jnp.concatenate(parts_of(x), axis=0)


def twice(x):
    return jnp.concatenate([x, x], axis=0).astype(BF16)


def rows_sum(s):
    return s[0:4] + s[4:8]


def dot_nt(a, b):
    return lax.dot_general(a, b, (((1,), (1,)), ((), ())), preferred_element_type=F32)


def store_parts(xs, base, x):
    count, cols, _ = x.shape
    for i, part in enumerate(parts_of(x)):
        xs[pl.ds(base, count), i * cols : (i + 1) * cols, :] = part


def split_map(m):
    hi = m.astype(BF16)
    return hi, (m - hi.astype(F32)).astype(BF16)


def split_tile(tile, r, k, t_ref, d_ref):
    size = tile.shape[0]
    if size < LANES:
        tile = jnp.concatenate([tile, jnp.zeros((size, LANES - size), F32)], axis=1)
    hi, lo = split_map(tile)
    t_ref[r, 0:size, k * LANES : (k + 1) * LANES] = hi
    t_ref[r, LANES : LANES + size, k * LANES : (k + 1) * LANES] = lo
    if k == 0:
        row = lax.broadcasted_iota(jnp.int32, tile.shape, 0)
        col = lax.broadcasted_iota(jnp.int32, tile.shape, 1)
        diag = jnp.sum(jnp.where(row == col, tile, 0.0), axis=0, keepdims=True)
        lane = lax.broadcasted_iota(jnp.int32, diag.shape, 1)
        d_ref[r] = jnp.where(lane < size, diag, 1.0)


def tiles_kernel(parts, tiles, t_ref, d_ref, far, held, sems, far_sems):
    count, slots = tiles.shape[:2]
    step = count // parts
    spans = [pl.ds(i * step, step) for i in range(parts)]
    loads = [pltpu.make_async_copy(tiles.at[a], held.at[a], sems.at[i]) for i, a in enumerate(spans)]
    stores = [pltpu.make_async_copy(t_ref.at[a], far.at[a], far_sems.at[i]) for i, a in enumerate(spans)]
    for load in loads:
        load.start()
    for i in range(parts):
        loads[i].wait()
        for r in range(i * step, (i + 1) * step):
            for k in range(slots):
                split_tile(held[r, k], r, k, t_ref, d_ref)
        stores[i].start()
    for store in stores:
        store.wait()


def small_tiles_kernel(tiles, t_ref, d_ref):
    t_ref[...] = jnp.zeros_like(t_ref)
    for r in range(tiles.shape[0]):
        for k in range(tiles.shape[1]):
            split_tile(tiles[r, k], r, k, t_ref, d_ref)


def index_kernel(flags, columns1, live1, columns2, live2, idx1, idx2, held1, held2, turned, sems):
    w_odd, n_odd = flags[W_ODD], flags[N_ODD]
    region = (0, 1 + w_odd, 2 - w_odd, 3 + n_odd, 4 - n_odd)
    there = (1, flags[HAS_WEST], flags[HAS_EAST], flags[HAS_SOUTH], flags[HAS_NORTH])
    for columns, live, held, dim in ((columns1, live1, held1, 1), (columns2, live2, held2, 0)):
        code = columns[...]
        count = code.shape[dim]
        place = jnp.full(code.shape, 5 * count, jnp.int32)
        for s in range(5):
            at = code - s * count
            ok = (at >= 0) & (at < count) & (live[...] == 1) & (there[s] == 1)
            place = jnp.where(ok, at + region[s] * count, place)
        own = lax.broadcasted_iota(jnp.int32, held.shape, dim)
        held[...] = own
        if dim:
            held[1:, :] = place
        else:
            held[:, 1:] = place
    copies = [
        pltpu.make_async_copy(held1, idx1, sems.at[0]),
        pltpu.make_async_copy(held2, turned, sems.at[1]),
    ]
    for copy in copies:
        copy.start()
    for copy in copies:
        copy.wait()
    slots, count = idx2.shape
    for k in range(slots):
        for r in range(count):
            idx2[k, r] = turned[r, k]


def apply_tiles(t_ref, xs, idx):
    slots, count = idx.shape
    out = []
    for r in range(count):
        lhs = twice(jnp.concatenate([xs[idx[k, r]] for k in range(slots)], axis=1))
        both = dot_nt(lhs, t_ref[r])[0:8]
        out.append(rows_sum(both[:, :LANES] + both[:, LANES:]))
    return out


def fill_blocks(xs, own, others, count):
    xs[5 * count] = jnp.zeros((8, LANES), F32)
    store_parts(xs, 0, own[0:count])
    for i, other in enumerate(others):
        store_parts(xs, (i + 1) * count, other[0:count])


def smooth_kernel(idx, t, d, b, own, o1, o2, o3, o4, out, xs):
    count = b.shape[0]
    fill_blocks(xs, own, (o1, o2, o3, o4), count)
    for r, ax in enumerate(apply_tiles(t, xs, idx)):
        out[r] = own[r] + JACOBI * (b[r] - ax) / d[r]


def residual_kernel(idx, t, d, b, own, o1, o2, o3, o4, left, scaled, xs):
    count = b.shape[0]
    fill_blocks(xs, own, (o1, o2, o3, o4), count)
    for r, ax in enumerate(apply_tiles(t, xs, idx)):
        rest = b[r] - ax
        left[r] = rest
        scaled[r] = rest / d[r]


def restrict_one_kernel(idx, t, left, groups, d2, own, o1, o2, o3, o4, b2, first, xs):
    count = left.shape[0]
    fill_blocks(xs, own, (o1, o2, o3, o4), count)
    total = None
    coarse_tiles, _, lanes = b2.shape
    size = coarse_tiles * lanes // 2
    for r, ax in enumerate(apply_tiles(t, xs, idx)):
        rows = twice(rows_of(left[r] - 0.5 * ax))
        hot = lax.broadcasted_iota(jnp.int32, (size, LANES), 0) == groups[r : r + 1, :]
        term = dot_nt(rows, hot.astype(F32).astype(BF16))
        total = term if total is None else total + term
    total = rows_sum(total[0:8])
    half = LANES // 2
    lane = lax.broadcasted_iota(jnp.int32, (4, LANES), 1)
    for tile in range(coarse_tiles):
        pair = total[:, (tile // 2) * LANES : (tile // 2 + 1) * LANES]
        if tile % 2:
            pair = pltpu.roll(pair, half, 1)
        value = jnp.where(lane < half, pair, 0.0)
        b2[tile] = value
        first[tile] = JACOBI * value / d2[tile]


def restrict_two_kernel(flags, idx, t, left, groups, gain, own, o1, o2, o3, o4, out, xs):
    count = left.shape[0]
    fill_blocks(xs, own, (o1, o2, o3, o4), count)
    offset = flags[N_AT] * flags[LEVEL3]
    first = groups.shape[1] - count
    total = None
    for r, ax in enumerate(apply_tiles(t, xs, idx)):
        rows = twice(rows_of(left[r] - 0.5 * ax))
        group = groups[0, first + r : first + r + 1, :] + offset
        hot = lax.broadcasted_iota(jnp.int32, (LANES, LANES), 0) == group
        term = dot_nt(rows, hot.astype(F32).astype(BF16))
        total = term if total is None else total + term
    total = map_product(jnp.concatenate(split_map(gain[0]), axis=0), rows_sum(total[0:8]))
    out[...] = jnp.broadcast_to(total[None], out.shape)


def chain_maps_kernel(order, flags, *refs):
    *pieces, out = refs
    position = -1
    for piece in pieces:
        rows = piece.shape[2]
        for k in range(piece.shape[0]):
            position += 1
            v, q = flags[W_AT], flags[N_AT]
            for bit, (axis, step) in enumerate(order):
                if position >> bit & 1:
                    v, q = (v ^ step, q) if axis == "wide" else (v, q ^ step)
            for i in range(piece.shape[1]):
                value = piece[k, i]
                hi = value.astype(BF16)
                at = pl.multiple_of(q * rows, rows)
                out[v, i, pl.ds(at, rows), :] = hi
                at = pl.multiple_of(LANES + q * rows, rows)
                out[v, i, pl.ds(at, rows), :] = (value - hi.astype(F32)).astype(BF16)


def map_product(m, x):
    both = dot_nt(twice(rows_of(x)), m)[0:8]
    return rows_sum(both[:, :LANES] + both[:, LANES:])


def take_lanes(table, lanes):
    return jnp.take_along_axis(table, jnp.broadcast_to(lanes, table.shape), axis=1)


def groups_kernel(own1, own, o1, o2, o3, o4, out):
    count1 = own1.shape[0]
    for p, ref in enumerate((own, o1, o2, o3, o4)):
        cols = ref.shape[1]
        for i in range(out.shape[1]):
            row = ref[count1 + i // cols, i % cols : i % cols + 1, :]
            out[p, i : i + 1] = row.astype(jnp.int32)


def chain_kernel(flags, maps, pieces, idx, t, d, x2, groups, out, xs, ys):
    blocks = maps.shape[0]
    narrow = pieces.shape[0] // blocks
    carry = None
    for v in range(blocks):
        now = pieces[v * narrow]
        for k in range(1, narrow):
            now = now + pieces[v * narrow + k]
        if carry is not None:
            now = now + map_product(maps[v, 0], carry)
        ys[v] = now
        carry = now
    for v in range(blocks - 2, -1, -1):
        carry = ys[v] + map_product(maps[v, 1], carry)
        ys[v] = carry
    count = x2.shape[0]
    xs[5 * count] = jnp.zeros((8, LANES), F32)
    size = flags[LEVEL3]
    w, n, w_odd, n_odd = flags[W_AT], flags[N_AT], flags[W_ODD], flags[N_ODD]
    n_first = n + 1 - 2 * n_odd
    n_second = jnp.clip(n - 1 + 2 * n_odd, 0, narrow - 1)
    w_first = w + 1 - 2 * w_odd
    w_second = jnp.clip(w - 1 + 2 * w_odd, 0, blocks - 1)
    where = ((w, n), (w_second, n), (w_first, n), (w, n_second), (w, n_first))
    lane = lax.broadcasted_iota(jnp.int32, (8, LANES), 1)
    first = groups.shape[1] - count
    for p, (pw, pn) in enumerate(where):
        table = rows_of(ys[pw])
        for tile in range(count):
            index = groups[p, first + tile : first + tile + 1, :]
            index = (index + pn * size) & (LANES - 1)
            got = take_lanes(table, index)
            xs[p * count + tile] = jnp.where(lane < LANES // 2, got, 0.0)
    for r, ax in enumerate(apply_tiles(t, xs, idx)):
        out[r] = x2[r] + (rows_sum(xs[r]) - 0.5 * ax / d[r])


def prolong_one_kernel(idx, t, d, x2, groups, own, o1, o2, o3, o4, out, xs):
    count = x2.shape[0]
    xs[5 * count] = jnp.zeros((8, LANES), F32)
    half = LANES // 2
    lane = lax.broadcasted_iota(jnp.int32, (4, LANES), 1)
    for p, u in enumerate((own, o1, o2, o3, o4)):
        tables = []
        for i in range(u.shape[0] // 2):
            wide = jnp.where(lane < half, u[2 * i], pltpu.roll(u[2 * i + 1], half, 1))
            tables.append(rows_of(wide))
        for tile in range(count):
            index = groups[p, tile : tile + 1, :]
            got = take_lanes(tables[0], index & (LANES - 1))
            for i in range(1, len(tables)):
                more = take_lanes(tables[i], index & (LANES - 1))
                got = jnp.where((index >> 7) == i, more, got)
            xs[p * count + tile] = got
    for r, ax in enumerate(apply_tiles(t, xs, idx)):
        out[r] = x2[r] + (rows_sum(xs[r]) - 0.5 * ax / d[r])


def live_weights(flags, east, north):
    row = lax.broadcasted_iota(jnp.int32, east.shape, 0)
    col = lax.broadcasted_iota(jnp.int32, east.shape, 1)
    east = jnp.where((flags[HAS_EAST] == 1) | (row < east.shape[0] - 1), east, 0.0)
    north = jnp.where((flags[HAS_NORTH] == 1) | (col < north.shape[1] - 1), north, 0.0)
    return east, north


def narrow_rims(flags, fields, first, second):
    odd = flags[N_ODD] == 1
    for i, field in enumerate(fields):
        turned = field.T
        low, high = turned[0:RIM], turned[-RIM:]
        first[i] = jnp.where(odd, low, high)
        second[i] = jnp.where(odd, high, low)


def narrow_sides(flags, first, second, i):
    odd = flags[N_ODD] == 1
    low = jnp.where(odd, first[i], second[i]) * flags[HAS_SOUTH].astype(F32)
    high = jnp.where(odd, second[i], first[i]) * flags[HAS_NORTH].astype(F32)
    return low, high


def with_sides(flags, field, first, second, i):
    low, high = narrow_sides(flags, first, second, i)
    side = jnp.concatenate([high, jnp.zeros((LANES - 2 * RIM, LANES), F32), low], axis=0)
    return jnp.concatenate([field, side.T], axis=1)


def wide_rims(flags, field, i, first, second):
    odd = flags[W_ODD] == 1
    low, high = field[0:RIM], field[-RIM:]
    first[i] = jnp.where(odd, low, high)
    second[i] = jnp.where(odd, high, low)


def with_rows(flags, field, first, second, i):
    odd = flags[W_ODD] == 1
    low = jnp.where(odd, first[i], second[i]) * flags[HAS_WEST].astype(F32)
    high = jnp.where(odd, second[i], first[i]) * flags[HAS_EAST].astype(F32)
    rim = jnp.concatenate([high, jnp.zeros((PAD - 2 * RIM, field.shape[1]), F32), low], axis=0)
    return jnp.concatenate([field, rim], axis=0)


def fine_first_kernel(
    sizes, block, east, north, forward, backward, flags, fields, first, second, piece, edges, sems
):
    wide, narrow = sizes
    w, n = lax.axis_index("wide"), lax.axis_index("narrow")
    values = (
        w & 1, n & 1, w > 0, w < wide - 1, n > 0, n < narrow - 1, w, n, forward.shape[1] // narrow,
    )
    for i, value in enumerate(values):
        flags[i] = jnp.int32(value)
    cols = block.shape[0]
    rows = piece.shape[2]
    at = pl.multiple_of(flags[N_AT] * rows, rows)
    copies = [
        (block, fields.at[0:cols]),
        (east, edges.at[0]),
        (north, edges.at[1]),
        *((m.at[0, pl.ds(at, rows)], piece.at[0, i]) for i, m in enumerate((forward, backward))),
    ]
    copies = [pltpu.make_async_copy(a, b, sems.at[i]) for i, (a, b) in enumerate(copies)]
    for copy in copies:
        copy.start()
    for copy in copies:
        copy.wait()
    fields[cols], fields[cols + 1] = live_weights(flags, edges[0], edges[1])
    narrow_rims(flags, [fields[c] for c in range(cols + 2)], first, second)


def fine_second_kernel(flags, fields, o2, o1, ext, first, second):
    for i in range(fields.shape[0]):
        wider = with_sides(flags, fields[i], o1, o2, i)
        ext[i] = wider
        wide_rims(flags, wider, i, first, second)


def beside(field, e, n):
    rows, lanes = field.shape
    return (
        e * pltpu.roll(field, rows - 1, 0)
        + pltpu.roll(e * field, 1, 0)
        + n * pltpu.roll(field, lanes - 1, 1)
        + pltpu.roll(n * field, 1, 1)
    )


def fine_down_kernel(flags, ext, o2, o1, groups, d1, near1, near2, far, b1, first, q_ref, keep, sem):
    cols = ext.shape[0] - 2
    rows = ext.shape[1]
    e = with_rows(flags, ext[cols], o1, o2, cols)
    n = with_rows(flags, ext[cols + 1], o1, o2, cols + 1)
    inv = 1.0 / (SHIFT + e + pltpu.roll(e, 1, 0) + n + pltpu.roll(n, 1, 1))
    diag = SHIFT + e + pltpu.roll(e, 1, 0) + n + pltpu.roll(n, 1, 1)
    keep[2 * cols] = e
    keep[2 * cols + 1] = n
    keep[2 * cols + 2] = inv
    for c in range(cols):
        b = with_rows(flags, ext[c], o1, o2, c)
        x1 = JACOBI * b * inv
        x2 = x1 + JACOBI * ((1.0 - JACOBI) * b + beside(x1, e, n)) * inv
        keep[c] = x2
        keep[cols + c] = b
        rest = b - diag * x2 + beside(x2, e, n)
        q = 0.5 * (rest + beside(rest * inv, e, n))
        for i, part in enumerate(parts_of(q[:rows, :LANES])):
            q_ref[i * cols + c] = part
    copy = pltpu.make_async_copy(keep, far, sem.at[0])
    copy.start()
    count = b1.shape[0]
    step = 32
    one, zero = jnp.ones((), BF16), jnp.zeros((), BF16)
    lanes = lax.broadcasted_iota(jnp.int32, (LANES, LANES), 0).astype(F32).astype(BF16)

    def over_rows(x):
        return jnp.broadcast_to(x, (16, LANES)).astype(BF16)

    def add_rows(j, total):
        left, right = [], []
        for k in range(step):
            row = pl.ds(j * step + k, 1)
            group = groups[row, :]
            mask = lanes[0:count] == over_rows((group >> 7).astype(F32))
            low = over_rows((group & (LANES - 1)).astype(F32))
            picked = [jnp.where(mask, over_rows(q_ref[i, row, :]), zero) for i in range(2 * cols)]
            left.append(jnp.concatenate(picked, axis=0))
            low = jnp.concatenate([low] * (LANES // 16), axis=0)
            right.append(jnp.where(lanes == low, one, zero))
        return total + dot_nt(jnp.concatenate(left, axis=1), jnp.concatenate(right, axis=1))

    total = lax.fori_loop(
        0, rows // step, add_rows, jnp.zeros((2 * cols * count, LANES), F32)
    )
    size = cols * count
    total = total[0:size] + total[size : 2 * size]
    for c in range(cols):
        value = total[c * count : (c + 1) * count]
        b1[:, c, :] = value
        first[0:count, c, :] = JACOBI * value / d1[:, 0, :]
    groups = [near1[i : i + 1, :] for i in range(count)]
    for i in range(near2.shape[0]):
        row = near2[i : i + 1, :]
        groups += [row, pltpu.roll(row, LANES // 2, 1)]
    for i, group in enumerate(groups):
        first[count + i // cols, i % cols : i % cols + 1, :] = group.astype(F32)
    copy.wait()


def fine_spread_kernel(flags, t, idx, d, b, groups, own, o1, o2, o3, o4, spread, first, second, xs, us):
    count, cols, _ = b.shape
    fill_blocks(xs, own, (o1, o2, o3, o4), count)
    for r, ax in enumerate(apply_tiles(t, xs, idx)):
        us[r] = own[r] + JACOBI * (b[r] - ax) / d[r]
    rows = groups.shape[0]
    for c in range(cols):
        for j in range(rows // 8):
            group = groups[8 * j : 8 * j + 8, :]
            high, low = group >> 7, group & (LANES - 1)
            value = jnp.zeros((8, LANES), F32)
            for h in range(count):
                table = jnp.broadcast_to(us[h, c : c + 1, :], (8, LANES))
                got = jnp.take_along_axis(table, low, axis=1)
                value = jnp.where(high == h, got, value)
            spread[c, 8 * j : 8 * j + 8, :] = value
    narrow_rims(flags, [spread[c] for c in range(cols)], first, second)


def fine_up_kernel(flags, keep, ext, o2, o1, far, out, sems):
    cols = out.shape[0]
    copies = []
    e, n, inv = keep[2 * cols], keep[2 * cols + 1], keep[2 * cols + 2]
    for c in range(cols):
        b = keep[cols + c]
        spread = with_rows(flags, ext[c], o1, o2, c)
        x = keep[c] + 0.5 * (spread + beside(spread, e, n) * inv)
        for _ in range(2):
            x = (1.0 - JACOBI) * x + JACOBI * (b + beside(x, e, n)) * inv
        out[c] = x[: out.shape[1], :LANES]
        copies.append(pltpu.make_async_copy(out.at[c], far.at[c], sems.at[c]))
        copies[-1].start()
    for copy in copies:
        copy.wait()


def pairs(start, count):
    out = []
    for i in range(start, count - 1, 2):
        out += [(i, i + 1), (i + 1, i)]
    return out


def routes(wide, narrow):
    narrow_first = pairs(0, narrow)
    narrow_second = pairs(1, narrow) + [(0, narrow - 1), (narrow - 1, 0)]
    wide_first = pairs(0, wide)
    both = [(a * narrow + k, b * narrow + k) for a, b in pairs(1, wide) for k in range(narrow)]
    for a in (0, wide - 1):
        both += [(a * narrow + k, a * narrow + (k ^ 1)) for k in range(narrow)]
    return narrow_first, narrow_second, wide_first, both


def exchange_narrow(first, second, route):
    second = lax.ppermute(second, "narrow", route[1])
    return second, lax.ppermute(first, "narrow", route[0])


def exchange_wide(first, second, route):
    second = lax.ppermute(second, ("wide", "narrow"), route[3])
    return second, lax.ppermute(first, "wide", route[2])


def exchange(x, route):
    return (*exchange_wide(x, x, route), *exchange_narrow(x, x, route))


def body(
    sizes,
    block,
    east,
    north,
    fine_groups,
    tiles_one,
    columns_one,
    live_one,
    coarse_groups,
    tiles_two,
    columns_two,
    live_two,
    coarser_groups,
    chain_forward,
    chain_gain,
    chain_backward,
):
    wide, narrow = sizes
    route = routes(wide, narrow)
    cols = block.shape[0]
    rows = block.shape[1]
    count1, slots = tiles_one.shape[:2]
    count2 = tiles_two.shape[0]

    order = [("wide", 1 << i) for i in reversed(range((wide - 1).bit_length()))]
    order += [("narrow", 1 << i) for i in reversed(range((narrow - 1).bit_length()))]
    share = chain_forward.shape[1] // narrow
    held = []
    done = []

    def swap(x, axis, step):
        return lax.ppermute(x, axis, [(i, i ^ step) for i in range(lax.axis_size(axis))])

    def gather_step(*anchor):
        step = order[len(done)]
        merged = held if len(done) == len(order) - 1 or len(held) == 1 else [jnp.concatenate(held, axis=0)]
        merged, anchor = lax.optimization_barrier((merged, anchor))
        held[:] = merged + [swap(m, *step) for m in merged]
        done.append(step)
        return anchor

    rim = sds((cols + 2, RIM, LANES))
    flags = sds((LEVEL3 + 1,), jnp.int32)
    flags, fields, first, second, piece = call(
        functools.partial(fine_first_kernel, sizes),
        [flags, sds((cols + 2, rows, LANES)), rim, rim, sds((1, 2, share, LANES))],
        (block, east, north, chain_forward, chain_backward),
        scratch=[pltpu.VMEM((2, rows, LANES), F32), pltpu.SemaphoreType.DMA((5,))],
        specs=[HBM] * 5,
        scalars=(0,),
    )
    held.append(piece)
    first, second = gather_step(first, second)
    o2, o1 = exchange_narrow(first, second, route)

    shapes = (sds((slots, count1), jnp.int32), sds((slots, count2), jnp.int32))
    idx1, idx2 = call(
        index_kernel,
        list(shapes),
        (flags, columns_one.T, live_one.T, columns_two, live_two),
        scratch=[
            pltpu.VMEM((slots, count1), jnp.int32),
            pltpu.VMEM((count2, slots), jnp.int32),
            pltpu.SMEM((count2, slots), jnp.int32),
            pltpu.SemaphoreType.DMA((2,)),
        ],
        specs=[SMEM] + [VMEM] * 4,
        us=0.5,
        scalars=(0, 1),
    )
    tiles2, d2 = call(
        small_tiles_kernel,
        [sds((count2, 2 * LANES, slots * LANES), BF16), sds((count2, 1, LANES))],
        (tiles_two,),
        us=0.7,
    )
    groups1 = coarse_groups.reshape(count1, LANES)
    groups2 = coarser_groups.reshape(-1, LANES)
    o2, idx1, idx2, tiles2, d2 = lax.optimization_barrier((o2, idx1, idx2, tiles2, d2))

    rim = sds((cols + 2, RIM, 2 * LANES))
    ext, first, second = call(
        fine_second_kernel,
        [sds((cols + 2, rows, 2 * LANES)), rim, rim],
        (flags, fields, o2, o1),
        specs=[SMEM] + [VMEM] * 3,
    )
    first, second = gather_step(first, second)
    o2, o1 = exchange_wide(first, second, route)
    field1 = sds((count1, cols, LANES))
    field2 = sds((count2, cols, LANES))
    split = sds((count1, 2 * LANES, slots * LANES), BF16)
    tiles1, d1, tiles1_far = call(
        functools.partial(tiles_kernel, 4),
        [split, sds((count1, 1, LANES)), split],
        (tiles_one,),
        scratch=[
            pltpu.VMEM(tiles_one.shape, F32),
            pltpu.SemaphoreType.DMA((4,)),
            pltpu.SemaphoreType.DMA((4,)),
        ],
        specs=[HBM],
        us=3,
        far=(2,),
    )
    more = -(-(count1 + count2) // cols)
    hold = {"t1": tiles1, "d1": d1}
    kept = sds((2 * cols + 3, rows + PAD, 2 * LANES))
    keep, b1, x1 = call(
        fine_down_kernel,
        [kept, field1, sds((count1 + more, cols, LANES))],
        (flags, ext, o2, o1, fine_groups, "d1", groups1, groups2),
        scratch=[
            pltpu.VMEM((2 * cols, rows, LANES), F32),
            pltpu.VMEM(kept.shape, F32),
            pltpu.SemaphoreType.DMA((1,)),
        ],
        specs=[SMEM] + [VMEM] * 7,
        mib=16,
        us=7,
        hold=hold,
        far=(0,),
    )
    hold["b1"] = b1

    xs1 = [pltpu.VMEM((5 * count1 + 1, 8, LANES), F32)]
    xs2 = [pltpu.VMEM((5 * count2 + 1, 8, LANES), F32)]
    lead = [SMEM]

    def smooth(level, x):
        idx, like, xs = (idx1, field1, xs1) if level == 1 else (idx2, field2, xs2)
        near = exchange(x, route)
        ins = (idx, f"t{level}", f"d{level}", f"b{level}", x, *near)
        return call(smooth_kernel, like, ins, xs, lead + [VMEM] * 8, hold=hold), near

    (x1,) = gather_step(x1)
    x2, near = smooth(1, x1)
    groups = call(
        groups_kernel,
        sds((5, count1 + count2, LANES), jnp.int32),
        (groups1, x1, *near),
        specs=[VMEM] * 6,
        us=1,
    )
    (x2,) = gather_step(x2)
    near = exchange(x2, route)
    hold |= {"x2": x2, "groups": groups, "d2": d2}
    left, scaled = call(
        residual_kernel,
        [field1, field1],
        (idx1, "t1", "d1", "b1", "x2", *near),
        xs1,
        lead + [VMEM] * 8,
        hold=hold,
    )
    while len(done) < len(order):
        (scaled,) = gather_step(scaled)
    b2, y1 = call(
        restrict_one_kernel,
        [field2, field2],
        (idx1, "t1", left, groups1, "d2", scaled, *exchange(scaled, route)),
        xs1,
        lead + [VMEM] * 9,
        hold=hold,
    )

    del hold["t1"]
    hold |= {"b2": b2, "t2": tiles2}
    y2, _ = smooth(2, y1)
    maps, y2 = lax.optimization_barrier((held, y2))
    near = exchange(y2, route)
    chain_shape = sds((wide, 2, 2 * LANES, LANES), BF16)
    big = wide > 16
    chain = call(
        functools.partial(chain_maps_kernel, order),
        chain_shape,
        (flags, *maps),
        specs=[SMEM] + [PLAIN if big else VMEM] * len(maps),
        mib=48 if big else 12,
        us=0.7,
        loose=(0,) if big else (),
    )
    if not big:
        hold["chain"] = chain
    hold["y2"] = y2
    left, scaled = call(
        residual_kernel,
        [field2, field2],
        (idx2, "t2", "d2", "b2", "y2", *near),
        xs2,
        lead + [VMEM] * 8,
        us=1,
        hold=hold,
    )
    out3 = call(
        restrict_two_kernel,
        sds((wide * narrow, cols, LANES)),
        (flags, idx2, "t2", left, "groups", chain_gain, scaled, *exchange(scaled, route)),
        xs2,
        [SMEM, SMEM] + [VMEM] * 9,
        hold=hold,
    )
    pieces = lax.all_to_all(out3, ("wide", "narrow"), 0, 0)
    y3 = call(
        chain_kernel,
        field2,
        (flags, chain if big else "chain", pieces, idx2, "t2", "d2", "y2", "groups"),
        xs2 + [pltpu.VMEM((wide, cols, LANES), F32)],
        [SMEM, PLAIN if big else VMEM, VMEM, SMEM] + [VMEM] * 4,
        mib=32 if big else 12,
        us=3,
        hold=hold,
    )
    hold.pop("chain", None)
    y4, _ = smooth(2, y3)
    y5, _ = smooth(2, y4)

    for name in ("t2", "d2", "b2", "y2"):
        del hold[name]
    hold["t1"] = tiles1_far
    x3 = call(
        prolong_one_kernel,
        field1,
        (idx1, "t1", "d1", "x2", "groups", y5, *exchange(y5, route)),
        xs1,
        lead + [VMEM] * 9,
        hold=hold,
    )
    del hold["x2"], hold["groups"]
    x4, _ = smooth(1, x3)
    rim = sds((cols, RIM, LANES))
    spread, first, second = call(
        fine_spread_kernel,
        [sds((cols, rows, LANES)), rim, rim],
        (flags, "t1", idx1, "d1", "b1", fine_groups, x4, *exchange(x4, route)),
        xs1 + [pltpu.VMEM((count1, cols, LANES), F32)],
        [SMEM, VMEM, SMEM] + [VMEM] * 8,
        us=3,
        hold=hold,
    )
    o2, o1 = exchange_narrow(first, second, route)
    rim = sds((cols, RIM, 2 * LANES))
    for name in ("t1", "d1", "b1"):
        del hold[name]
    ext, first, second = call(
        fine_second_kernel,
        [sds((cols, rows, 2 * LANES)), rim, rim],
        (flags, spread, o2, o1),
        specs=[SMEM] + [VMEM] * 3,
        us=1,
        hold=hold,
    )
    o2, o1 = exchange_wide(first, second, route)
    whole = sds((cols, rows, LANES))
    return call(
        fine_up_kernel,
        whole,
        (flags, keep, ext, o2, o1),
        scratch=[pltpu.VMEM(whole.shape, F32), pltpu.SemaphoreType.DMA((cols,))],
        specs=[SMEM] + [VMEM] * 4,
        far=(0,),
    )


def solution(mesh):
    tile = P(("wide", "narrow"), None, None, None)
    pair = P(("wide", "narrow"), None)
    line = P(("wide", "narrow"))
    grid = P("wide", "narrow")
    chain = P("wide", None, None)
    field = P(None, "wide", "narrow")
    in_specs = (
        field, grid, grid, grid, tile, pair, pair, line, tile, pair, pair, line, chain, chain, chain,
    )
    sizes = (mesh.shape["wide"], mesh.shape["narrow"])
    return jax.shard_map(
        functools.partial(body, sizes), mesh=mesh, in_specs=in_specs, out_specs=field, check_vma=False
    )
```

```python
import functools

import jax
import jax.numpy as jnp
from jax import lax
from jax.experimental import pallas as pl
from jax.experimental.pallas import tpu as pltpu
from jax.sharding import PartitionSpec as P

F32 = jnp.float32
BF16 = jnp.bfloat16
SHIFT = 0.1
JACOBI = 0.6
LANES = 128
RIM = 4
PAD = 16
VMEM = pl.BlockSpec(memory_space=pltpu.VMEM)
PLAIN = pl.BlockSpec(memory_space=pltpu.VMEM)
HBM = pl.BlockSpec(memory_space=pl.ANY)
SMEM = pl.BlockSpec(memory_space=pltpu.SMEM)
W_ODD, N_ODD, HAS_WEST, HAS_EAST, HAS_SOUTH, HAS_NORTH, W_AT, N_AT, LEVEL3 = range(9)


def sds(shape, dtype=F32):
    return jax.ShapeDtypeStruct(shape, dtype)


def constrain(x, spec):
    if spec is VMEM:
        return pltpu.with_memory_space_constraint(x, pltpu.VMEM)
    if spec is HBM:
        return pltpu.with_memory_space_constraint(x, pltpu.HBM)
    if spec is SMEM:
        return pltpu.with_memory_space_constraint(x, pltpu.SMEM)
    return x


def call(kernel, outs, ins, scratch=(), specs=None, mib=12, us=2, hold=None, far=(), loose=(), scalars=()):
    hold = {} if hold is None else hold
    outs, tree = jax.tree.flatten(outs)
    specs = jax.tree.leaves([[spec] * len(x) if isinstance(x, tuple) else spec for x, spec in zip(ins, specs)])
    ins, shape_in = jax.tree.flatten(list(ins))
    places = {x: i for i, x in enumerate(ins) if isinstance(x, str)}
    rest = [name for name in hold if name not in places]
    places |= {name: len(ins) + i for i, name in enumerate(rest)}
    inputs = [hold[x] if isinstance(x, str) else x for x in ins] + [hold[name] for name in rest]
    specs = list(specs) + [VMEM] * len(rest)
    inputs = [constrain(x, spec) for x, spec in zip(inputs, specs)]
    count_in, count_out = len(ins), len(outs)
    spaces = [pltpu.HBM if i in far else pltpu.SMEM if i in scalars else pltpu.VMEM for i in range(len(outs))]
    shapes = [o if i in loose else spaces[i](o.shape, o.dtype) for i, o in enumerate(outs)]
    shapes += [pltpu.VMEM(hold[name].shape, hold[name].dtype) for name in hold]

    def inner(*refs):
        first = len(inputs)
        kernel(
            *jax.tree.unflatten(shape_in, refs[:count_in]),
            *refs[first : first + count_out],
            *refs[first + count_out + len(hold) :],
        )

    results = pl.pallas_call(
        inner,
        out_shape=shapes,
        in_specs=specs,
        out_specs=[{pltpu.HBM: HBM, pltpu.SMEM: SMEM, pltpu.VMEM: VMEM}[space] for space in spaces]
        + [VMEM] * len(hold),
        scratch_shapes=list(scratch),
        input_output_aliases={places[name]: count_out + i for i, name in enumerate(hold)},
        compiler_params=pltpu.CompilerParams(vmem_limit_bytes=mib * 1024 * 1024),
        cost_estimate=pl.CostEstimate(flops=0, bytes_accessed=int(us * 3.5e6), transcendentals=0),
    )(*inputs)
    for name, value in zip(list(hold), results[count_out:]):
        hold[name] = value
    return jax.tree.unflatten(tree, results[:count_out])


def parts_of(x):
    hi = x.astype(BF16).astype(F32)
    return hi, x - hi


def rows_of(x):
    return jnp.concatenate(parts_of(x), axis=0)


def twice(x):
    return jnp.concatenate([x, x], axis=0).astype(BF16)


def rows_sum(s):
    return s[0:4] + s[4:8]


def dot_nt(a, b):
    return lax.dot_general(a, b, (((1,), (1,)), ((), ())), preferred_element_type=F32)


def store_parts(xs, base, x):
    count, cols, _ = x.shape
    for i, part in enumerate(parts_of(x)):
        xs[pl.ds(base, count), i * cols : (i + 1) * cols, :] = part


def split_map(m):
    hi = m.astype(BF16)
    return hi, (m - hi.astype(F32)).astype(BF16)


def split_tile(tile, r, k, t_ref, d_ref, first=0):
    size = tile.shape[0]
    if size < LANES:
        tile = jnp.concatenate([tile, jnp.zeros((size, LANES - size), F32)], axis=1)
    hi, lo = split_map(tile)
    t_ref[r, 0:size, k * LANES : (k + 1) * LANES] = hi
    t_ref[r, LANES : LANES + size, k * LANES : (k + 1) * LANES] = lo
    if k == 0:
        row = lax.broadcasted_iota(jnp.int32, tile.shape, 0)
        col = lax.broadcasted_iota(jnp.int32, tile.shape, 1)
        diag = jnp.sum(jnp.where(row == col, tile, 0.0), axis=0, keepdims=True)
        lane = lax.broadcasted_iota(jnp.int32, diag.shape, 1)
        d_ref[first + r] = jnp.where(lane < size, diag, 1.0)


class Stream:
    def __init__(self, half, tiles, held, t_ref, far, sems, parts=4):
        self.count, self.slots = held.shape[0], held.shape[1]
        self.step = self.count // parts
        self.held, self.t_ref = held, t_ref
        spans = [pl.ds(i * self.step, self.step) for i in range(parts)]
        self.loads = [
            pltpu.make_async_copy(tiles.at[pl.ds(half * self.count + i * self.step, self.step)], held.at[a], sems.at[i])
            for i, a in enumerate(spans)
        ]
        self.stores = [
            pltpu.make_async_copy(t_ref.at[a], far.at[a], sems.at[parts + i]) for i, a in enumerate(spans)
        ]
        for load in self.loads:
            load.start()

    def run(self, d_ref, first):
        for i, load in enumerate(self.loads):
            load.wait()
            for r in range(i * self.step, (i + 1) * self.step):
                for k in range(self.slots):
                    split_tile(self.held[r, k], r, k, self.t_ref, d_ref, first)
            self.stores[i].start()

    def end(self):
        for store in self.stores:
            store.wait()


def second_half_kernel(tiles, d_first, t_ref, d_ref, far, held, sems):
    stream = Stream(1, tiles, held, t_ref, far, sems)
    count = d_first.shape[0]
    d_ref[0:count] = d_first[...]
    stream.run(d_ref, count)
    stream.end()


def setup_kernel(
    flags, columns1, live1, columns2, live2, tiles1, tiles2,
    idx1, idx2, t1, d1, t2, d2, far,
    in1, in2, in3, in4, held_tiles, held2, held1, held_two, turned, sems, stream_sems,
):
    ins = ((columns1, in1), (live1, in2), (columns2, in3), (live2, in4), (tiles2, held2))
    ins = [pltpu.make_async_copy(a, b, sems.at[i]) for i, (a, b) in enumerate(ins)]
    for copy in ins:
        copy.start()
    stream = Stream(0, tiles1, held_tiles, t1, far, stream_sems)
    for copy in ins:
        copy.wait()
    w_odd, n_odd = flags[W_ODD], flags[N_ODD]
    region = (0, 1 + w_odd, 2 - w_odd, 3 + n_odd, 4 - n_odd)
    there = (1, flags[HAS_WEST], flags[HAS_EAST], flags[HAS_SOUTH], flags[HAS_NORTH])
    for columns, live, held, dim in ((in1, in2, held1, 1), (in3, in4, held_two, 0)):
        code = columns[...]
        count = code.shape[dim]
        place = jnp.full(code.shape, 5 * count, jnp.int32)
        for s in range(5):
            at = code - s * count
            ok = (at >= 0) & (at < count) & (live[...] == 1) & (there[s] == 1)
            place = jnp.where(ok, at + region[s] * count, place)
        own = lax.broadcasted_iota(jnp.int32, held.shape, dim)
        held[...] = own
        if dim:
            held[1:, :] = place
        else:
            held[:, 1:] = place
    copies = [
        pltpu.make_async_copy(held1, idx1, sems.at[0]),
        pltpu.make_async_copy(held_two, turned, sems.at[1]),
    ]
    for copy in copies:
        copy.start()
    t2[...] = jnp.zeros_like(t2)
    for r in range(held2.shape[0]):
        for k in range(held2.shape[1]):
            split_tile(held2[r, k], r, k, t2, d2)
    stream.run(d1, 0)
    for copy in copies:
        copy.wait()
    slots, count = idx2.shape
    for k in range(slots):
        for r in range(count):
            idx2[k, r] = turned[r, k]
    stream.end()


def apply_tiles(t_ref, xs, idx):
    slots, count = idx.shape
    out = []
    for r in range(count):
        lhs = twice(jnp.concatenate([xs[idx[k, r]] for k in range(slots)], axis=1))
        t, at = t_ref[r // t_ref[0].shape[0]], r % t_ref[0].shape[0]
        both = dot_nt(lhs, t[at])[0:8]
        out.append(rows_sum(both[:, :LANES] + both[:, LANES:]))
    return out


def fill_blocks(xs, own, others, count):
    xs[5 * count] = jnp.zeros((8, LANES), F32)
    store_parts(xs, 0, own[0:count])
    for i, other in enumerate(others):
        store_parts(xs, (i + 1) * count, other[0:count])


def smooth_kernel(idx, t, d, b, own, o1, o2, o3, o4, out, xs):
    count = b.shape[0]
    fill_blocks(xs, own, (o1, o2, o3, o4), count)
    for r, ax in enumerate(apply_tiles(t, xs, idx)):
        out[r] = own[r] + JACOBI * (b[r] - ax) / d[r]


def residual_kernel(idx, t, d, b, own, o1, o2, o3, o4, left, scaled, xs):
    count = b.shape[0]
    fill_blocks(xs, own, (o1, o2, o3, o4), count)
    for r, ax in enumerate(apply_tiles(t, xs, idx)):
        rest = b[r] - ax
        left[r] = rest
        scaled[r] = rest / d[r]


def restrict_one_kernel(idx, t, left, groups, d2, own, o1, o2, o3, o4, b2, first, xs):
    count = left.shape[0]
    fill_blocks(xs, own, (o1, o2, o3, o4), count)
    total = None
    coarse_tiles, _, lanes = b2.shape
    size = coarse_tiles * lanes // 2
    for r, ax in enumerate(apply_tiles(t, xs, idx)):
        rows = twice(rows_of(left[r] - 0.5 * ax))
        hot = lax.broadcasted_iota(jnp.int32, (size, LANES), 0) == groups[r : r + 1, :]
        term = dot_nt(rows, hot.astype(F32).astype(BF16))
        total = term if total is None else total + term
    total = rows_sum(total[0:8])
    half = LANES // 2
    lane = lax.broadcasted_iota(jnp.int32, (4, LANES), 1)
    for tile in range(coarse_tiles):
        pair = total[:, (tile // 2) * LANES : (tile // 2 + 1) * LANES]
        if tile % 2:
            pair = pltpu.roll(pair, half, 1)
        value = jnp.where(lane < half, pair, 0.0)
        b2[tile] = value
        first[tile] = JACOBI * value / d2[tile]


def restrict_two_kernel(flags, idx, t, left, groups, gain, own, o1, o2, o3, o4, out, xs):
    count = left.shape[0]
    fill_blocks(xs, own, (o1, o2, o3, o4), count)
    offset = flags[N_AT] * flags[LEVEL3]
    first = groups.shape[1] - count
    total = None
    for r, ax in enumerate(apply_tiles(t, xs, idx)):
        rows = twice(rows_of(left[r] - 0.5 * ax))
        group = groups[0, first + r : first + r + 1, :] + offset
        hot = lax.broadcasted_iota(jnp.int32, (LANES, LANES), 0) == group
        term = dot_nt(rows, hot.astype(F32).astype(BF16))
        total = term if total is None else total + term
    total = map_product(jnp.concatenate(split_map(gain[0]), axis=0), rows_sum(total[0:8]))
    out[...] = jnp.broadcast_to(total[None], out.shape)


def chain_maps_kernel(order, flags, *refs):
    *pieces, out = refs
    position = -1
    for piece in pieces:
        rows = piece.shape[2]
        for k in range(piece.shape[0]):
            position += 1
            v, q = flags[W_AT], flags[N_AT]
            for bit, (axis, step) in enumerate(order):
                if position >> bit & 1:
                    v, q = (v ^ step, q) if axis == "wide" else (v, q ^ step)
            for i in range(piece.shape[1]):
                value = piece[k, i]
                hi = value.astype(BF16)
                at = pl.multiple_of(q * rows, rows)
                out[v, i, pl.ds(at, rows), :] = hi
                at = pl.multiple_of(LANES + q * rows, rows)
                out[v, i, pl.ds(at, rows), :] = (value - hi.astype(F32)).astype(BF16)


def map_product(m, x):
    both = dot_nt(twice(rows_of(x)), m)[0:8]
    return rows_sum(both[:, :LANES] + both[:, LANES:])


def take_lanes(table, lanes):
    return jnp.take_along_axis(table, jnp.broadcast_to(lanes, table.shape), axis=1)


def groups_kernel(own1, own, o1, o2, o3, o4, out):
    count1 = own1.shape[0]
    for p, ref in enumerate((own, o1, o2, o3, o4)):
        cols = ref.shape[1]
        for i in range(out.shape[1]):
            row = ref[count1 + i // cols, i % cols : i % cols + 1, :]
            out[p, i : i + 1] = row.astype(jnp.int32)


def chain_kernel(flags, maps, pieces, idx, t, d, x2, groups, out, xs, ys):
    blocks = maps.shape[0]
    narrow = pieces.shape[0] // blocks
    carry = None
    for v in range(blocks):
        now = pieces[v * narrow]
        for k in range(1, narrow):
            now = now + pieces[v * narrow + k]
        if carry is not None:
            now = now + map_product(maps[v, 0], carry)
        ys[v] = now
        carry = now
    for v in range(blocks - 2, -1, -1):
        carry = ys[v] + map_product(maps[v, 1], carry)
        ys[v] = carry
    count = x2.shape[0]
    xs[5 * count] = jnp.zeros((8, LANES), F32)
    size = flags[LEVEL3]
    w, n, w_odd, n_odd = flags[W_AT], flags[N_AT], flags[W_ODD], flags[N_ODD]
    n_first = n + 1 - 2 * n_odd
    n_second = jnp.clip(n - 1 + 2 * n_odd, 0, narrow - 1)
    w_first = w + 1 - 2 * w_odd
    w_second = jnp.clip(w - 1 + 2 * w_odd, 0, blocks - 1)
    where = ((w, n), (w_second, n), (w_first, n), (w, n_second), (w, n_first))
    lane = lax.broadcasted_iota(jnp.int32, (8, LANES), 1)
    first = groups.shape[1] - count
    for p, (pw, pn) in enumerate(where):
        table = rows_of(ys[pw])
        for tile in range(count):
            index = groups[p, first + tile : first + tile + 1, :]
            index = (index + pn * size) & (LANES - 1)
            got = take_lanes(table, index)
            xs[p * count + tile] = jnp.where(lane < LANES // 2, got, 0.0)
    for r, ax in enumerate(apply_tiles(t, xs, idx)):
        out[r] = x2[r] + (rows_sum(xs[r]) - 0.5 * ax / d[r])


def prolong_one_kernel(idx, t, d, x2, groups, own, o1, o2, o3, o4, out, xs):
    count = x2.shape[0]
    xs[5 * count] = jnp.zeros((8, LANES), F32)
    half = LANES // 2
    lane = lax.broadcasted_iota(jnp.int32, (4, LANES), 1)
    for p, u in enumerate((own, o1, o2, o3, o4)):
        tables = []
        for i in range(u.shape[0] // 2):
            wide = jnp.where(lane < half, u[2 * i], pltpu.roll(u[2 * i + 1], half, 1))
            tables.append(rows_of(wide))
        for tile in range(count):
            index = groups[p, tile : tile + 1, :]
            got = take_lanes(tables[0], index & (LANES - 1))
            for i in range(1, len(tables)):
                more = take_lanes(tables[i], index & (LANES - 1))
                got = jnp.where((index >> 7) == i, more, got)
            xs[p * count + tile] = got
    for r, ax in enumerate(apply_tiles(t, xs, idx)):
        out[r] = x2[r] + (rows_sum(xs[r]) - 0.5 * ax / d[r])


def live_weights(flags, east, north):
    row = lax.broadcasted_iota(jnp.int32, east.shape, 0)
    col = lax.broadcasted_iota(jnp.int32, east.shape, 1)
    east = jnp.where((flags[HAS_EAST] == 1) | (row < east.shape[0] - 1), east, 0.0)
    north = jnp.where((flags[HAS_NORTH] == 1) | (col < north.shape[1] - 1), north, 0.0)
    return east, north


def narrow_rims(flags, fields, first, second):
    odd = flags[N_ODD] == 1
    for i, field in enumerate(fields):
        turned = field.T
        low, high = turned[0:RIM], turned[-RIM:]
        first[i] = jnp.where(odd, low, high)
        second[i] = jnp.where(odd, high, low)


def narrow_sides(flags, first, second, i):
    odd = flags[N_ODD] == 1
    low = jnp.where(odd, first[i], second[i]) * flags[HAS_SOUTH].astype(F32)
    high = jnp.where(odd, second[i], first[i]) * flags[HAS_NORTH].astype(F32)
    return low, high


def with_sides(flags, field, first, second, i):
    low, high = narrow_sides(flags, first, second, i)
    side = jnp.concatenate([high, jnp.zeros((LANES - 2 * RIM, LANES), F32), low], axis=0)
    return jnp.concatenate([field, side.T], axis=1)


def wide_rims(flags, field, i, first, second):
    odd = flags[W_ODD] == 1
    low, high = field[0:RIM], field[-RIM:]
    first[i] = jnp.where(odd, low, high)
    second[i] = jnp.where(odd, high, low)


def with_rows(flags, field, first, second, i):
    odd = flags[W_ODD] == 1
    low = jnp.where(odd, first[i], second[i]) * flags[HAS_WEST].astype(F32)
    high = jnp.where(odd, second[i], first[i]) * flags[HAS_EAST].astype(F32)
    rim = jnp.concatenate([high, jnp.zeros((PAD - 2 * RIM, field.shape[1]), F32), low], axis=0)
    return jnp.concatenate([field, rim], axis=0)


def fine_first_kernel(
    sizes, block, east, north, forward, backward, flags, fields, first, second, piece, edges, sems
):
    wide, narrow = sizes
    w, n = lax.axis_index("wide"), lax.axis_index("narrow")
    values = (
        w & 1, n & 1, w > 0, w < wide - 1, n > 0, n < narrow - 1, w, n, forward.shape[1] // narrow,
    )
    for i, value in enumerate(values):
        flags[i] = jnp.int32(value)
    cols = block.shape[0]
    rows = piece.shape[2]
    at = pl.multiple_of(flags[N_AT] * rows, rows)
    copies = [
        (block, fields.at[0:cols]),
        (east, edges.at[0]),
        (north, edges.at[1]),
        *((m.at[0, pl.ds(at, rows)], piece.at[0, i]) for i, m in enumerate((forward, backward))),
    ]
    copies = [pltpu.make_async_copy(a, b, sems.at[i]) for i, (a, b) in enumerate(copies)]
    for copy in copies:
        copy.start()
    for copy in copies:
        copy.wait()
    fields[cols], fields[cols + 1] = live_weights(flags, edges[0], edges[1])
    narrow_rims(flags, [fields[c] for c in range(cols + 2)], first, second)


def fine_second_kernel(flags, fields, o2, o1, ext, first, second):
    for i in range(fields.shape[0]):
        wider = with_sides(flags, fields[i], o1, o2, i)
        ext[i] = wider
        wide_rims(flags, wider, i, first, second)


def beside(field, e, n):
    rows, lanes = field.shape
    return (
        e * pltpu.roll(field, rows - 1, 0)
        + pltpu.roll(e * field, 1, 0)
        + n * pltpu.roll(field, lanes - 1, 1)
        + pltpu.roll(n * field, 1, 1)
    )


def fine_down_kernel(flags, ext, o2, o1, groups, d1, near1, near2, far, b1, first, q_ref, keep, sem):
    cols = ext.shape[0] - 2
    rows = ext.shape[1]
    e = with_rows(flags, ext[cols], o1, o2, cols)
    n = with_rows(flags, ext[cols + 1], o1, o2, cols + 1)
    inv = 1.0 / (SHIFT + e + pltpu.roll(e, 1, 0) + n + pltpu.roll(n, 1, 1))
    diag = SHIFT + e + pltpu.roll(e, 1, 0) + n + pltpu.roll(n, 1, 1)
    keep[2 * cols] = e
    keep[2 * cols + 1] = n
    keep[2 * cols + 2] = inv
    for c in range(cols):
        b = with_rows(flags, ext[c], o1, o2, c)
        x1 = JACOBI * b * inv
        x2 = x1 + JACOBI * ((1.0 - JACOBI) * b + beside(x1, e, n)) * inv
        keep[c] = x2
        keep[cols + c] = b
        rest = b - diag * x2 + beside(x2, e, n)
        q = 0.5 * (rest + beside(rest * inv, e, n))
        for i, part in enumerate(parts_of(q[:rows, :LANES])):
            q_ref[i * cols + c] = part
    copy = pltpu.make_async_copy(keep, far, sem.at[0])
    copy.start()
    count = b1.shape[0]
    step = 32
    one, zero = jnp.ones((), BF16), jnp.zeros((), BF16)
    lanes = lax.broadcasted_iota(jnp.int32, (LANES, LANES), 0).astype(F32).astype(BF16)

    def over_rows(x):
        return jnp.broadcast_to(x, (16, LANES)).astype(BF16)

    def add_rows(j, total):
        left, right = [], []
        for k in range(step):
            row = pl.ds(j * step + k, 1)
            group = groups[row, :]
            mask = lanes[0:count] == over_rows((group >> 7).astype(F32))
            low = over_rows((group & (LANES - 1)).astype(F32))
            picked = [jnp.where(mask, over_rows(q_ref[i, row, :]), zero) for i in range(2 * cols)]
            left.append(jnp.concatenate(picked, axis=0))
            low = jnp.concatenate([low] * (LANES // 16), axis=0)
            right.append(jnp.where(lanes == low, one, zero))
        return total + dot_nt(jnp.concatenate(left, axis=1), jnp.concatenate(right, axis=1))

    total = lax.fori_loop(
        0, rows // step, add_rows, jnp.zeros((2 * cols * count, LANES), F32)
    )
    size = cols * count
    total = total[0:size] + total[size : 2 * size]
    for c in range(cols):
        value = total[c * count : (c + 1) * count]
        b1[:, c, :] = value
        first[0:count, c, :] = JACOBI * value / d1[:, 0, :]
    groups = [near1[i : i + 1, :] for i in range(count)]
    for i in range(near2.shape[0]):
        row = near2[i : i + 1, :]
        groups += [row, pltpu.roll(row, LANES // 2, 1)]
    for i, group in enumerate(groups):
        first[count + i // cols, i % cols : i % cols + 1, :] = group.astype(F32)
    copy.wait()


def fine_spread_kernel(flags, t, idx, d, b, groups, own, o1, o2, o3, o4, spread, first, second, xs, us):
    count, cols, _ = b.shape
    fill_blocks(xs, own, (o1, o2, o3, o4), count)
    for r, ax in enumerate(apply_tiles(t, xs, idx)):
        us[r] = own[r] + JACOBI * (b[r] - ax) / d[r]
    rows = groups.shape[0]
    for c in range(cols):
        for j in range(rows // 8):
            group = groups[8 * j : 8 * j + 8, :]
            high, low = group >> 7, group & (LANES - 1)
            value = jnp.zeros((8, LANES), F32)
            for h in range(count):
                table = jnp.broadcast_to(us[h, c : c + 1, :], (8, LANES))
                got = jnp.take_along_axis(table, low, axis=1)
                value = jnp.where(high == h, got, value)
            spread[c, 8 * j : 8 * j + 8, :] = value
    narrow_rims(flags, [spread[c] for c in range(cols)], first, second)


def fine_up_kernel(flags, keep, ext, o2, o1, far, out, sems):
    cols = out.shape[0]
    copies = []
    e, n, inv = keep[2 * cols], keep[2 * cols + 1], keep[2 * cols + 2]
    for c in range(cols):
        b = keep[cols + c]
        spread = with_rows(flags, ext[c], o1, o2, c)
        x = keep[c] + 0.5 * (spread + beside(spread, e, n) * inv)
        for _ in range(2):
            x = (1.0 - JACOBI) * x + JACOBI * (b + beside(x, e, n)) * inv
        out[c] = x[: out.shape[1], :LANES]
        copies.append(pltpu.make_async_copy(out.at[c], far.at[c], sems.at[c]))
        copies[-1].start()
    for copy in copies:
        copy.wait()


def pairs(start, count):
    out = []
    for i in range(start, count - 1, 2):
        out += [(i, i + 1), (i + 1, i)]
    return out


def routes(wide, narrow):
    narrow_first = pairs(0, narrow)
    narrow_second = pairs(1, narrow) + [(0, narrow - 1), (narrow - 1, 0)]
    wide_first = pairs(0, wide)
    both = [(a * narrow + k, b * narrow + k) for a, b in pairs(1, wide) for k in range(narrow)]
    for a in (0, wide - 1):
        both += [(a * narrow + k, a * narrow + (k ^ 1)) for k in range(narrow)]
    return narrow_first, narrow_second, wide_first, both


def exchange_narrow(first, second, route):
    second = lax.ppermute(second, "narrow", route[1])
    return second, lax.ppermute(first, "narrow", route[0])


def exchange_wide(first, second, route):
    second = lax.ppermute(second, ("wide", "narrow"), route[3])
    return second, lax.ppermute(first, "wide", route[2])


def exchange(x, route):
    return (*exchange_wide(x, x, route), *exchange_narrow(x, x, route))


def body(
    sizes,
    block,
    east,
    north,
    fine_groups,
    tiles_one,
    columns_one,
    live_one,
    coarse_groups,
    tiles_two,
    columns_two,
    live_two,
    coarser_groups,
    chain_forward,
    chain_gain,
    chain_backward,
):
    wide, narrow = sizes
    route = routes(wide, narrow)
    cols = block.shape[0]
    rows = block.shape[1]
    count1, slots = tiles_one.shape[:2]
    count2 = tiles_two.shape[0]

    order = [("wide", 1 << i) for i in reversed(range((wide - 1).bit_length()))]
    order += [("narrow", 1 << i) for i in reversed(range((narrow - 1).bit_length()))]
    share = chain_forward.shape[1] // narrow
    held = []
    done = []

    def swap(x, axis, step):
        return lax.ppermute(x, axis, [(i, i ^ step) for i in range(lax.axis_size(axis))])

    def gather_step(anchor):
        step = order[len(done)]
        merged = held if len(done) == len(order) - 1 or len(held) == 1 else [jnp.concatenate(held, axis=0)]
        merged, _ = lax.optimization_barrier((merged, anchor))
        held[:] = merged + [swap(m, *step) for m in merged]
        done.append(step)

    rim = sds((cols + 2, RIM, LANES))
    flags = sds((LEVEL3 + 1,), jnp.int32)
    flags, fields, first, second, piece = call(
        functools.partial(fine_first_kernel, sizes),
        [flags, sds((cols + 2, rows, LANES)), rim, rim, sds((1, 2, share, LANES))],
        (block, east, north, chain_forward, chain_backward),
        scratch=[pltpu.VMEM((2, rows, LANES), F32), pltpu.SemaphoreType.DMA((5,))],
        specs=[HBM] * 5,
        scalars=(0,),
    )
    held.append(piece)
    gather_step(first)
    o2, o1 = exchange_narrow(first, second, route)

    half = count1 // 2
    split = sds((half, 2 * LANES, slots * LANES), BF16)
    held_tiles = [pltpu.VMEM((half, *tiles_one.shape[1:]), F32)]
    stream_sems = [pltpu.SemaphoreType.DMA((8,))]
    idx1, idx2, tiles1, d1, tiles2, d2, tiles1_far = call(
        setup_kernel,
        [
            sds((slots, count1), jnp.int32),
            sds((slots, count2), jnp.int32),
            split,
            sds((half, 1, LANES)),
            sds((count2, *split.shape[1:]), BF16),
            sds((count2, 1, LANES)),
            split,
        ],
        (flags, columns_one.T, live_one.T, columns_two, live_two, tiles_one, tiles_two),
        scratch=[pltpu.VMEM((slots - 1, count1), jnp.int32)] * 2
        + [pltpu.VMEM((count2, slots - 1), jnp.int32)] * 2
        + held_tiles
        + [
            pltpu.VMEM(tiles_two.shape, F32),
            pltpu.VMEM((slots, count1), jnp.int32),
            pltpu.VMEM((count2, slots), jnp.int32),
            pltpu.SMEM((count2, slots), jnp.int32),
            pltpu.SemaphoreType.DMA((5,)),
        ]
        + stream_sems,
        specs=[SMEM] + [HBM] * 6,
        far=(6,),
        scalars=(0, 1),
    )
    groups1 = coarse_groups.reshape(count1, LANES)
    groups2 = coarser_groups.reshape(-1, LANES)
    o2, idx1, idx2, tiles1, tiles2, d1, d2 = lax.optimization_barrier((o2, idx1, idx2, tiles1, tiles2, d1, d2))

    rim = sds((cols + 2, RIM, 2 * LANES))
    ext, first, second = call(
        fine_second_kernel,
        [sds((cols + 2, rows, 2 * LANES)), rim, rim],
        (flags, fields, o2, o1),
        specs=[SMEM] + [VMEM] * 3,
    )
    gather_step(first)
    o2, o1 = exchange_wide(first, second, route)
    field1 = sds((count1, cols, LANES))
    field2 = sds((count2, cols, LANES))
    tiles1_second, d1, tiles1_second_far = call(
        second_half_kernel,
        [split, sds((count1, 1, LANES)), split],
        (tiles_one, d1),
        scratch=held_tiles + stream_sems,
        specs=[HBM, VMEM],
        far=(2,),
    )
    more = -(-(count1 + count2) // cols)
    hold = {"t1a": tiles1, "t1b": tiles1_second, "d1": d1}
    t1 = ("t1a", "t1b")
    kept = sds((2 * cols + 3, rows + PAD, 2 * LANES))
    keep, b1, x1 = call(
        fine_down_kernel,
        [kept, field1, sds((count1 + more, cols, LANES))],
        (flags, ext, o2, o1, fine_groups, "d1", groups1, groups2),
        scratch=[
            pltpu.VMEM((2 * cols, rows, LANES), F32),
            pltpu.VMEM(kept.shape, F32),
            pltpu.SemaphoreType.DMA((1,)),
        ],
        specs=[SMEM] + [VMEM] * 7,
        mib=16,
        us=7,
        hold=hold,
        far=(0,),
    )
    hold["b1"] = b1

    xs1 = [pltpu.VMEM((5 * count1 + 1, 8, LANES), F32)]
    xs2 = [pltpu.VMEM((5 * count2 + 1, 8, LANES), F32)]
    lead = [SMEM]

    def smooth(level, x):
        idx, like, xs = (idx1, field1, xs1) if level == 1 else (idx2, field2, xs2)
        near = exchange(x, route)
        ins = (idx, t1 if level == 1 else ("t2",), f"d{level}", f"b{level}", x, *near)
        return call(smooth_kernel, like, ins, xs, lead + [VMEM] * 8, hold=hold), near

    gather_step(x1)
    x2, near = smooth(1, x1)
    groups = call(
        groups_kernel,
        sds((5, count1 + count2, LANES), jnp.int32),
        (groups1, x1, *near),
        specs=[VMEM] * 6,
        us=1,
    )
    gather_step(x2)
    near = exchange(x2, route)
    hold |= {"x2": x2, "groups": groups, "d2": d2}
    left, scaled = call(
        residual_kernel,
        [field1, field1],
        (idx1, t1, "d1", "b1", "x2", *near),
        xs1,
        lead + [VMEM] * 8,
        hold=hold,
    )
    while len(done) < len(order):
        gather_step(scaled)
    b2, y1 = call(
        restrict_one_kernel,
        [field2, field2],
        (idx1, t1, left, groups1, "d2", scaled, *exchange(scaled, route)),
        xs1,
        lead + [VMEM] * 9,
        hold=hold,
    )

    del hold["t1a"], hold["t1b"]
    hold |= {"b2": b2, "t2": tiles2}
    y2, _ = smooth(2, y1)
    maps, y2 = lax.optimization_barrier((held, y2))
    near = exchange(y2, route)
    chain_shape = sds((wide, 2, 2 * LANES, LANES), BF16)
    big = wide > 16
    chain = call(
        functools.partial(chain_maps_kernel, order),
        chain_shape,
        (flags, *maps),
        specs=[SMEM] + [PLAIN if big else VMEM] * len(maps),
        mib=48 if big else 12,
        us=0.7,
        loose=(0,) if big else (),
    )
    if not big:
        hold["chain"] = chain
    hold["y2"] = y2
    left, scaled = call(
        residual_kernel,
        [field2, field2],
        (idx2, ("t2",), "d2", "b2", "y2", *near),
        xs2,
        lead + [VMEM] * 8,
        us=1,
        hold=hold,
    )
    out3 = call(
        restrict_two_kernel,
        sds((wide * narrow, cols, LANES)),
        (flags, idx2, ("t2",), left, "groups", chain_gain, scaled, *exchange(scaled, route)),
        xs2,
        [SMEM, SMEM] + [VMEM] * 9,
        hold=hold,
    )
    pieces = lax.all_to_all(out3, ("wide", "narrow"), 0, 0)
    y3 = call(
        chain_kernel,
        field2,
        (flags, chain if big else "chain", pieces, idx2, ("t2",), "d2", "y2", "groups"),
        xs2 + [pltpu.VMEM((wide, cols, LANES), F32)],
        [SMEM, PLAIN if big else VMEM, VMEM, SMEM] + [VMEM] * 4,
        mib=32 if big else 12,
        us=3,
        hold=hold,
    )
    hold.pop("chain", None)
    y4, _ = smooth(2, y3)
    y5, _ = smooth(2, y4)

    for name in ("t2", "d2", "b2", "y2"):
        del hold[name]
    hold |= {"t1a": tiles1_far, "t1b": tiles1_second_far}
    x3 = call(
        prolong_one_kernel,
        field1,
        (idx1, t1, "d1", "x2", "groups", y5, *exchange(y5, route)),
        xs1,
        lead + [VMEM] * 9,
        hold=hold,
    )
    del hold["x2"], hold["groups"]
    x4, _ = smooth(1, x3)
    rim = sds((cols, RIM, LANES))
    spread, first, second = call(
        fine_spread_kernel,
        [sds((cols, rows, LANES)), rim, rim],
        (flags, t1, idx1, "d1", "b1", fine_groups, x4, *exchange(x4, route)),
        xs1 + [pltpu.VMEM((count1, cols, LANES), F32)],
        [SMEM, VMEM, SMEM] + [VMEM] * 8,
        us=3,
        hold=hold,
    )
    o2, o1 = exchange_narrow(first, second, route)
    rim = sds((cols, RIM, 2 * LANES))
    for name in ("t1a", "t1b", "d1", "b1"):
        del hold[name]
    ext, first, second = call(
        fine_second_kernel,
        [sds((cols, rows, 2 * LANES)), rim, rim],
        (flags, spread, o2, o1),
        specs=[SMEM] + [VMEM] * 3,
        us=1,
        hold=hold,
    )
    o2, o1 = exchange_wide(first, second, route)
    whole = sds((cols, rows, LANES))
    return call(
        fine_up_kernel,
        whole,
        (flags, keep, ext, o2, o1),
        scratch=[pltpu.VMEM(whole.shape, F32), pltpu.SemaphoreType.DMA((cols,))],
        specs=[SMEM] + [VMEM] * 4,
        far=(0,),
    )


def solution(mesh):
    tile = P(("wide", "narrow"), None, None, None)
    pair = P(("wide", "narrow"), None)
    line = P(("wide", "narrow"))
    grid = P("wide", "narrow")
    chain = P("wide", None, None)
    field = P(None, "wide", "narrow")
    in_specs = (
        field, grid, grid, grid, tile, pair, pair, line, tile, pair, pair, line, chain, chain, chain,
    )
    sizes = (mesh.shape["wide"], mesh.shape["narrow"])
    return jax.shard_map(
        functools.partial(body, sizes), mesh=mesh, in_specs=in_specs, out_specs=field, check_vma=False
    )
```

```python
import functools

import jax
import jax.numpy as jnp
from jax import lax
from jax.experimental import pallas as pl
from jax.experimental.pallas import tpu as pltpu
from jax.sharding import PartitionSpec as P

F32 = jnp.float32
BF16 = jnp.bfloat16
SHIFT = 0.1
JACOBI = 0.6
LANES = 128
ORDER = -1
RIM = 4
PAD = 2 * RIM
VMEM = pl.BlockSpec(memory_space=pltpu.VMEM)
PLAIN = pl.BlockSpec(memory_space=pltpu.VMEM)
HBM = pl.BlockSpec(memory_space=pl.ANY)
SMEM = pl.BlockSpec(memory_space=pltpu.SMEM)
W_ODD, N_ODD, HAS_WEST, HAS_EAST, HAS_SOUTH, HAS_NORTH, W_AT, N_AT, LEVEL3 = range(9)


def sds(shape, dtype=F32):
    return jax.ShapeDtypeStruct(shape, dtype)


def constrain(x, spec):
    if spec is VMEM:
        return pltpu.with_memory_space_constraint(x, pltpu.VMEM)
    if spec is HBM:
        return pltpu.with_memory_space_constraint(x, pltpu.HBM)
    if spec is SMEM:
        return pltpu.with_memory_space_constraint(x, pltpu.SMEM)
    return x


def call(kernel, outs, ins, scratch=(), specs=None, mib=12, us=2, hold=None, far=(), loose=(), scalars=()):
    hold = {} if hold is None else hold
    outs, tree = jax.tree.flatten(outs)
    specs = jax.tree.leaves([[spec] * len(x) if isinstance(x, tuple) else spec for x, spec in zip(ins, specs)])
    ins, shape_in = jax.tree.flatten(list(ins))
    places = {x: i for i, x in enumerate(ins) if isinstance(x, str)}
    rest = [name for name in hold if name not in places]
    places |= {name: len(ins) + i for i, name in enumerate(rest)}
    inputs = [hold[x] if isinstance(x, str) else x for x in ins] + [hold[name] for name in rest]
    specs = list(specs) + [VMEM] * len(rest)
    inputs = [constrain(x, spec) for x, spec in zip(inputs, specs)]
    count_in, count_out = len(ins), len(outs)
    spaces = [pltpu.HBM if i in far else pltpu.SMEM if i in scalars else pltpu.VMEM for i in range(len(outs))]
    shapes = [o if i in loose else spaces[i](o.shape, o.dtype) for i, o in enumerate(outs)]
    shapes += [pltpu.VMEM(hold[name].shape, hold[name].dtype) for name in hold]

    def inner(*refs):
        first = len(inputs)
        kernel(
            *jax.tree.unflatten(shape_in, refs[:first][::ORDER][:count_in]),
            *refs[first : first + count_out],
            *refs[first + count_out + len(hold) :],
        )

    results = pl.pallas_call(
        inner,
        out_shape=shapes,
        in_specs=specs[::ORDER],
        out_specs=[{pltpu.HBM: HBM, pltpu.SMEM: SMEM, pltpu.VMEM: VMEM}[space] for space in spaces]
        + [VMEM] * len(hold),
        scratch_shapes=list(scratch),
        input_output_aliases={
            range(len(inputs))[::ORDER][places[name]]: count_out + i for i, name in enumerate(hold)
        },
        compiler_params=pltpu.CompilerParams(vmem_limit_bytes=mib * 1024 * 1024),
        cost_estimate=pl.CostEstimate(flops=0, bytes_accessed=int(us * 3.5e6), transcendentals=0),
    )(*inputs[::ORDER])
    for name, value in zip(list(hold), results[count_out:]):
        hold[name] = value
    return jax.tree.unflatten(tree, results[:count_out])


def parts_of(x):
    hi = x.astype(BF16).astype(F32)
    return hi, x - hi


def rows_of(x):
    return jnp.concatenate(parts_of(x), axis=0)


def twice(x):
    return jnp.concatenate([x, x], axis=0).astype(BF16)


def rows_sum(s):
    return s[0:4] + s[4:8]


def dot_nt(a, b):
    return lax.dot_general(a, b, (((1,), (1,)), ((), ())), preferred_element_type=F32)


def store_parts(xs, base, x):
    count, cols, _ = x.shape
    for i, part in enumerate(parts_of(x)):
        xs[pl.ds(base, count), i * cols : (i + 1) * cols, :] = part


def split_map(m):
    hi = m.astype(BF16)
    return hi, (m - hi.astype(F32)).astype(BF16)


def diagonal(tile):
    size = tile.shape[0]
    row = lax.broadcasted_iota(jnp.int32, tile.shape, 0)
    col = lax.broadcasted_iota(jnp.int32, tile.shape, 1)
    diag = jnp.sum(jnp.where(row == col, tile, 0.0), axis=0, keepdims=True)
    lane = lax.broadcasted_iota(jnp.int32, diag.shape, 1)
    return jnp.where(lane < size, diag, 1.0)


def split_tile(tile, r, k, t_ref):
    size = tile.shape[0]
    if size < LANES:
        tile = jnp.concatenate([tile, jnp.zeros((size, LANES - size), F32)], axis=1)
    hi, lo = split_map(tile)
    t_ref[r, 0:size, k * LANES : (k + 1) * LANES] = hi
    t_ref[r, LANES : LANES + size, k * LANES : (k + 1) * LANES] = lo
    return tile


class Stream:
    def __init__(self, half, tiles, held, t_ref, far, sems, parts=4):
        self.count, self.slots = held.shape[0], held.shape[1]
        self.step = self.count // parts
        self.held, self.t_ref = held, t_ref
        spans = [pl.ds(i * self.step, self.step) for i in range(parts)]
        self.loads = [
            pltpu.make_async_copy(tiles.at[pl.ds(half * self.count + i * self.step, self.step)], held.at[a], sems.at[i])
            for i, a in enumerate(spans)
        ]
        self.stores = [
            pltpu.make_async_copy(t_ref.at[a], far.at[a], sems.at[parts + i]) for i, a in enumerate(spans)
        ]
        for load in self.loads:
            load.start()

    def run(self):
        for i, load in enumerate(self.loads):
            load.wait()
            for r in range(i * self.step, (i + 1) * self.step):
                for k in range(self.slots):
                    split_tile(self.held[r, k], r, k, self.t_ref)
            self.stores[i].start()

    def end(self):
        for store in self.stores:
            store.wait()


def second_half_kernel(tiles, _, t_ref, far, held, sems):
    stream = Stream(1, tiles, held, t_ref, far, sems)
    stream.run()
    stream.end()


def setup_kernel(
    flags, columns1, live1, columns2, live2, tiles1, tiles2,
    idx1, idx2, t1, d1, t2, d2, far,
    in1, in2, in3, in4, held_tiles, held2, fronts, held1, held_two, turned, sems, stream_sems,
):
    ins = [(columns1, in1), (live1, in2), (columns2, in3), (live2, in4), (tiles2, held2)]
    half = fronts.shape[0]
    ins.append((tiles1.at[half:, 0], fronts))
    ins = [pltpu.make_async_copy(a, b, sems.at[i]) for i, (a, b) in enumerate(ins)]
    for copy in ins:
        copy.start()
    stream = Stream(0, tiles1, held_tiles, t1, far, stream_sems)
    for copy in ins:
        copy.wait()
    w_odd, n_odd = flags[W_ODD], flags[N_ODD]
    region = (0, 1 + w_odd, 2 - w_odd, 3 + n_odd, 4 - n_odd)
    there = (1, flags[HAS_WEST], flags[HAS_EAST], flags[HAS_SOUTH], flags[HAS_NORTH])
    for columns, live, held, dim in ((in1, in2, held1, 1), (in3, in4, held_two, 0)):
        code = columns[...]
        count = code.shape[dim]
        place = jnp.full(code.shape, 5 * count, jnp.int32)
        for s in range(5):
            at = code - s * count
            ok = (at >= 0) & (at < count) & (live[...] == 1) & (there[s] == 1)
            place = jnp.where(ok, at + region[s] * count, place)
        own = lax.broadcasted_iota(jnp.int32, held.shape, dim)
        held[...] = own
        if dim:
            held[1:, :] = place
        else:
            held[:, 1:] = place
    copies = [
        pltpu.make_async_copy(held1, idx1, sems.at[0]),
        pltpu.make_async_copy(held_two, turned, sems.at[1]),
    ]
    for copy in copies:
        copy.start()
    t2[...] = jnp.zeros_like(t2)
    for r in range(held2.shape[0]):
        for k in range(held2.shape[1]):
            tile = split_tile(held2[r, k], r, k, t2)
            if k == 0:
                row = lax.broadcasted_iota(jnp.int32, tile.shape, 0)
                col = lax.broadcasted_iota(jnp.int32, tile.shape, 1)
                diag = jnp.sum(jnp.where(row == col, tile, 0.0), axis=0, keepdims=True)
                lane = lax.broadcasted_iota(jnp.int32, diag.shape, 1)
                d2[r] = jnp.where(lane < tile.shape[0], diag, 1.0)
    for r in range(half):
        d1[half + r] = diagonal(fronts[r])
    stream.run()
    for r in range(half):
        d1[r] = diagonal(held_tiles[r, 0])
    for copy in copies:
        copy.wait()
    slots, count = idx2.shape
    for k in range(slots):
        for r in range(count):
            idx2[k, r] = turned[r, k]
    stream.end()


def apply_tiles(t_ref, xs, idx):
    slots, count = idx.shape
    out = []
    for r in range(count):
        lhs = twice(jnp.concatenate([xs[idx[k, r]] for k in range(slots)], axis=1))
        t, at = t_ref[r // t_ref[0].shape[0]], r % t_ref[0].shape[0]
        both = dot_nt(lhs, t[at])[0:8]
        out.append(rows_sum(both[:, :LANES] + both[:, LANES:]))
    return out


def fill_blocks(xs, own, others, count):
    xs[5 * count] = jnp.zeros((8, LANES), F32)
    store_parts(xs, 0, own[0:count])
    for i, other in enumerate(others):
        store_parts(xs, (i + 1) * count, other[0:count])


def ride(out, start, refs):
    for ref, first in refs:
        count = ref.shape[0] - first
        out[start : start + count] = ref[first:]
        start += count


def smooth_kernel(idx, t, d, b, own, o1, o2, o3, o4, out, xs):
    count = b.shape[0]
    fill_blocks(xs, own, (o1, o2, o3, o4), count)
    for r, ax in enumerate(apply_tiles(t, xs, idx)):
        out[r] = own[r] + JACOBI * (b[r] - ax) / d[r]


def smooth_ride_kernel(first, idx, t, d, b, own, o1, o2, o3, o4, sent_w, sent_n, out, out_w, out_n, xs):
    smooth_kernel(idx, t, d, b, own, o1, o2, o3, o4, out, xs)
    count = b.shape[0]
    out_w[0:count] = out[...]
    out_n[0:count] = out[...]
    ride(out_n, count, ((sent_w, first), (o2, first)))
    ride(out_w, count, ((sent_n, first), (o3, first)))


def residual_kernel(idx, t, d, b, own, o1, o2, o3, o4, left, scaled, xs):
    count = b.shape[0]
    fill_blocks(xs, own, (o1, o2, o3, o4), count)
    for r, ax in enumerate(apply_tiles(t, xs, idx)):
        rest = b[r] - ax
        left[r] = rest
        scaled[r] = rest / d[r]


def restrict_one_kernel(idx, t, left, groups, d2, own, o1, o2, o3, o4, b2, first, xs):
    count = left.shape[0]
    fill_blocks(xs, own, (o1, o2, o3, o4), count)
    total = None
    coarse_tiles, _, lanes = b2.shape
    size = coarse_tiles * lanes // 2
    for r, ax in enumerate(apply_tiles(t, xs, idx)):
        rows = twice(rows_of(left[r] - 0.5 * ax))
        hot = lax.broadcasted_iota(jnp.int32, (size, LANES), 0) == groups[r : r + 1, :]
        term = dot_nt(rows, hot.astype(F32).astype(BF16))
        total = term if total is None else total + term
    total = rows_sum(total[0:8])
    half = LANES // 2
    lane = lax.broadcasted_iota(jnp.int32, (4, LANES), 1)
    for tile in range(coarse_tiles):
        pair = total[:, (tile // 2) * LANES : (tile // 2 + 1) * LANES]
        if tile % 2:
            pair = pltpu.roll(pair, half, 1)
        value = jnp.where(lane < half, pair, 0.0)
        b2[tile] = value
        first[tile] = JACOBI * value / d2[tile]


def restrict_two_kernel(flags, idx, t, left, groups, gain, own, o1, o2, o3, o4, out, xs):
    count = left.shape[0]
    fill_blocks(xs, own, (o1, o2, o3, o4), count)
    offset = flags[N_AT] * flags[LEVEL3]
    first = groups.shape[1] - count
    total = None
    for r, ax in enumerate(apply_tiles(t, xs, idx)):
        rows = twice(rows_of(left[r] - 0.5 * ax))
        group = groups[0, first + r : first + r + 1, :] + offset
        hot = lax.broadcasted_iota(jnp.int32, (LANES, LANES), 0) == group
        term = dot_nt(rows, hot.astype(F32).astype(BF16))
        total = term if total is None else total + term
    total = map_product(jnp.concatenate(split_map(gain[0]), axis=0), rows_sum(total[0:8]))
    out[...] = jnp.broadcast_to(total[None], out.shape)


def bundle_kernel(first, _, *refs):
    *pieces, out = refs
    ride(out, 0, [(ref, first) for ref in pieces])


def chain_maps_kernel(orders, flags, bundle, other, out):
    half = bundle.shape[0] // 2
    for i, order in enumerate(orders):
        position = 0
        span = half * 2 >> len(order)
        rows = span * bundle.shape[1]
        for ref in (bundle, other):
            for start in range(i * half, (i + 1) * half, span):
                v, q = flags[W_AT], flags[N_AT]
                for bit, (axis, step) in enumerate(order):
                    if position >> bit & 1:
                        v, q = (v ^ step, q) if axis == "wide" else (v, q ^ step)
                hi, lo = split_map(ref[start : start + span].reshape(rows, LANES))
                out[v, i, pl.ds(pl.multiple_of(q * rows, rows), rows), :] = hi
                out[v, i, pl.ds(pl.multiple_of(LANES + q * rows, rows), rows), :] = lo
                position += 1


def map_product(m, x):
    both = dot_nt(twice(rows_of(x)), m)[0:8]
    return rows_sum(both[:, :LANES] + both[:, LANES:])


def take_lanes(table, lanes):
    return jnp.take_along_axis(table, jnp.broadcast_to(lanes, table.shape), axis=1)


def groups_kernel(own1, own, o1, o2, o3, o4, out):
    count1 = own1.shape[0]
    for p, ref in enumerate((own, o1, o2, o3, o4)):
        cols = ref.shape[1]
        for i in range(out.shape[1]):
            row = ref[count1 + i // cols, i % cols : i % cols + 1, :]
            out[p, i : i + 1] = row.astype(jnp.int32)


def chain_kernel(flags, maps, pieces, idx, t, d, x2, groups, out, xs, ys):
    blocks = maps.shape[0]
    narrow = pieces.shape[0] // blocks
    carry = None
    for v in range(blocks):
        now = pieces[v * narrow]
        for k in range(1, narrow):
            now = now + pieces[v * narrow + k]
        if carry is not None:
            now = now + map_product(maps[v, 0], carry)
        ys[v] = now
        carry = now
    for v in range(blocks - 2, -1, -1):
        carry = ys[v] + map_product(maps[v, 1], carry)
        ys[v] = carry
    count = x2.shape[0]
    xs[5 * count] = jnp.zeros((8, LANES), F32)
    size = flags[LEVEL3]
    w, n, w_odd, n_odd = flags[W_AT], flags[N_AT], flags[W_ODD], flags[N_ODD]
    n_first = n + 1 - 2 * n_odd
    n_second = jnp.clip(n - 1 + 2 * n_odd, 0, narrow - 1)
    w_first = w + 1 - 2 * w_odd
    w_second = jnp.clip(w - 1 + 2 * w_odd, 0, blocks - 1)
    where = ((w, n), (w_second, n), (w_first, n), (w, n_second), (w, n_first))
    lane = lax.broadcasted_iota(jnp.int32, (8, LANES), 1)
    first = groups.shape[1] - count
    for p, (pw, pn) in enumerate(where):
        table = rows_of(ys[pw])
        for tile in range(count):
            index = groups[p, first + tile : first + tile + 1, :]
            index = (index + pn * size) & (LANES - 1)
            got = take_lanes(table, index)
            xs[p * count + tile] = jnp.where(lane < LANES // 2, got, 0.0)
    for r, ax in enumerate(apply_tiles(t, xs, idx)):
        out[r] = x2[r] + (rows_sum(xs[r]) - 0.5 * ax / d[r])


def prolong_one_kernel(idx, t, d, x2, groups, own, o1, o2, o3, o4, out, xs):
    count = x2.shape[0]
    xs[5 * count] = jnp.zeros((8, LANES), F32)
    half = LANES // 2
    lane = lax.broadcasted_iota(jnp.int32, (4, LANES), 1)
    for p, u in enumerate((own, o1, o2, o3, o4)):
        tables = []
        for i in range(u.shape[0] // 2):
            wide = jnp.where(lane < half, u[2 * i], pltpu.roll(u[2 * i + 1], half, 1))
            tables.append(rows_of(wide))
        for tile in range(count):
            index = groups[p, tile : tile + 1, :]
            got = take_lanes(tables[0], index & (LANES - 1))
            for i in range(1, len(tables)):
                more = take_lanes(tables[i], index & (LANES - 1))
                got = jnp.where((index >> 7) == i, more, got)
            xs[p * count + tile] = got
    for r, ax in enumerate(apply_tiles(t, xs, idx)):
        out[r] = x2[r] + (rows_sum(xs[r]) - 0.5 * ax / d[r])


def live_weights(flags, east, north):
    row = lax.broadcasted_iota(jnp.int32, east.shape, 0)
    col = lax.broadcasted_iota(jnp.int32, east.shape, 1)
    east = jnp.where((flags[HAS_EAST] == 1) | (row < east.shape[0] - 1), east, 0.0)
    north = jnp.where((flags[HAS_NORTH] == 1) | (col < north.shape[1] - 1), north, 0.0)
    return east, north


def narrow_rims(flags, fields, first, second):
    odd = flags[N_ODD] == 1
    for i, field in enumerate(fields):
        turned = field.T
        low, high = turned[0:RIM], turned[-RIM:]
        first[i] = jnp.where(odd, low, high)
        second[i] = jnp.where(odd, high, low)


def narrow_sides(flags, first, second, i):
    odd = flags[N_ODD] == 1
    low = jnp.where(odd, first[i], second[i]) * flags[HAS_SOUTH].astype(F32)
    high = jnp.where(odd, second[i], first[i]) * flags[HAS_NORTH].astype(F32)
    return low, high


def with_sides(flags, field, first, second, i):
    low, high = narrow_sides(flags, first, second, i)
    side = jnp.concatenate([high, jnp.zeros((LANES - 2 * RIM, LANES), F32), low], axis=0)
    return jnp.concatenate([field, side.T], axis=1)


def wide_rims(flags, field, i, first, second):
    odd = flags[W_ODD] == 1
    low, high = field[0:RIM], field[-RIM:]
    first[i] = jnp.where(odd, low, high)
    second[i] = jnp.where(odd, high, low)


def with_rows(flags, field, first, second, i):
    odd = flags[W_ODD] == 1
    low = jnp.where(odd, first[i], second[i]) * flags[HAS_WEST].astype(F32)
    high = jnp.where(odd, second[i], first[i]) * flags[HAS_EAST].astype(F32)
    return jnp.concatenate([field, high, low], axis=0)


def fine_first_kernel(
    sizes, block, east, north, forward, backward, flags, fields, first, second, piece, edges, maps, sems
):
    wide, narrow = sizes
    w, n = lax.axis_index("wide"), lax.axis_index("narrow")
    values = (
        w & 1, n & 1, w > 0, w < wide - 1, n > 0, n < narrow - 1, w, n, forward.shape[1] // narrow,
    )
    for i, value in enumerate(values):
        flags[i] = jnp.int32(value)
    cols = block.shape[0]
    rows = maps.shape[1]
    at = pl.multiple_of(n * rows, rows)
    copies = [
        (block, fields.at[0:cols]),
        (east, edges.at[0]),
        (north, edges.at[1]),
        (forward.at[0, pl.ds(at, rows)], maps.at[0]),
        (backward.at[0, pl.ds(at, rows)], maps.at[1]),
    ]
    copies = [pltpu.make_async_copy(a, b, sems.at[i]) for i, (a, b) in enumerate(copies)]
    for copy in copies:
        copy.start()
    for copy in copies:
        copy.wait()
    fields[cols], fields[cols + 1] = live_weights(flags, edges[0], edges[1])
    narrow_rims(flags, [fields[c] for c in range(cols + 2)], first, second)
    piece[...] = maps[...].reshape(piece.shape)


def fine_second_kernel(flags, fields, o2, o1, ext, first, second):
    for i in range(fields.shape[0]):
        wider = with_sides(flags, fields[i], o1, o2, i)
        ext[i] = wider
        wide_rims(flags, wider, i, first, second)


def beside(field, e, n):
    rows, lanes = field.shape
    return (
        e * pltpu.roll(field, rows - 1, 0)
        + pltpu.roll(e * field, 1, 0)
        + n * pltpu.roll(field, lanes - 1, 1)
        + pltpu.roll(n * field, 1, 1)
    )


def fine_down_kernel(span, flags, ext, o2, o1, groups, d1, near1, near2, maps, far, b1, first, out_w, out_n, q_ref, keep, sem):
    cols = ext.shape[0] - 2
    rows = ext.shape[1]
    e = with_rows(flags, ext[cols], o1, o2, cols)
    n = with_rows(flags, ext[cols + 1], o1, o2, cols + 1)
    inv = 1.0 / (SHIFT + e + pltpu.roll(e, 1, 0) + n + pltpu.roll(n, 1, 1))
    diag = SHIFT + e + pltpu.roll(e, 1, 0) + n + pltpu.roll(n, 1, 1)
    keep[2 * cols] = e
    keep[2 * cols + 1] = n
    keep[2 * cols + 2] = inv
    for c in range(cols):
        b = with_rows(flags, ext[c], o1, o2, c)
        x1 = JACOBI * b * inv
        x2 = x1 + JACOBI * ((1.0 - JACOBI) * b + beside(x1, e, n)) * inv
        keep[c] = x2
        keep[cols + c] = b
        rest = b - diag * x2 + beside(x2, e, n)
        q = 0.5 * (rest + beside(rest * inv, e, n))
        for i, part in enumerate(parts_of(q[:rows, :LANES])):
            q_ref[i * cols + c] = part
    copy = pltpu.make_async_copy(keep, far, sem.at[0])
    copy.start()
    count = b1.shape[0]
    step = 32
    one, zero = jnp.ones((), BF16), jnp.zeros((), BF16)
    lanes = lax.broadcasted_iota(jnp.int32, (LANES, LANES), 0).astype(F32).astype(BF16)

    def over_rows(x):
        return jnp.broadcast_to(x, (16, LANES)).astype(BF16)

    def add_rows(j, total):
        left, right = [], []
        for k in range(step):
            row = pl.ds(j * step + k, 1)
            group = groups[row, :]
            mask = lanes[0:count] == over_rows((group >> 7).astype(F32))
            low = over_rows((group & (LANES - 1)).astype(F32))
            picked = [jnp.where(mask, over_rows(q_ref[i, row, :]), zero) for i in range(2 * cols)]
            left.append(jnp.concatenate(picked, axis=0))
            low = jnp.concatenate([low] * (LANES // 16), axis=0)
            right.append(jnp.where(lanes == low, one, zero))
        return total + dot_nt(jnp.concatenate(left, axis=1), jnp.concatenate(right, axis=1))

    total = lax.fori_loop(
        0, rows // step, add_rows, jnp.zeros((2 * cols * count, LANES), F32)
    )
    size = cols * count
    total = total[0:size] + total[size : 2 * size]
    for c in range(cols):
        value = total[c * count : (c + 1) * count]
        b1[:, c, :] = value
        first[0:count, c, :] = JACOBI * value / d1[:, 0, :]
    groups = [near1[i : i + 1, :] for i in range(count)]
    for i in range(near2.shape[0]):
        row = near2[i : i + 1, :]
        groups += [row, pltpu.roll(row, LANES // 2, 1)]
    for i, group in enumerate(groups):
        first[count + i // cols, i % cols : i % cols + 1, :] = group.astype(F32)
    out_w[0 : first.shape[0]] = first[...]
    out_n[0 : first.shape[0]] = first[...]
    at = first.shape[0]
    for ref in maps:
        for start in range(0, ref.shape[0], 2 * span):
            out_w[at : at + span] = ref[start : start + span]
            out_n[at : at + span] = ref[start + span : start + 2 * span]
            at += span
    copy.wait()


def fine_spread_kernel(flags, t, idx, d, b, groups, own, o1, o2, o3, o4, spread, first, second, xs, us):
    count, cols, _ = b.shape
    fill_blocks(xs, own, (o1, o2, o3, o4), count)
    for r, ax in enumerate(apply_tiles(t, xs, idx)):
        us[r] = own[r] + JACOBI * (b[r] - ax) / d[r]
    rows = groups.shape[0]
    for c in range(cols):
        for j in range(rows // 8):
            group = groups[8 * j : 8 * j + 8, :]
            high, low = group >> 7, group & (LANES - 1)
            value = jnp.zeros((8, LANES), F32)
            for h in range(count):
                table = jnp.broadcast_to(us[h, c : c + 1, :], (8, LANES))
                got = jnp.take_along_axis(table, low, axis=1)
                value = jnp.where(high == h, got, value)
            spread[c, 8 * j : 8 * j + 8, :] = value
    narrow_rims(flags, [spread[c] for c in range(cols)], first, second)


def fine_up_kernel(flags, keep, ext, o2, o1, far, out, sems):
    cols = out.shape[0]
    copies = []
    e, n, inv = keep[2 * cols], keep[2 * cols + 1], keep[2 * cols + 2]
    for c in range(cols):
        b = keep[cols + c]
        spread = with_rows(flags, ext[c], o1, o2, c)
        x = keep[c] + 0.5 * (spread + beside(spread, e, n) * inv)
        for _ in range(2):
            x = (1.0 - JACOBI) * x + JACOBI * (b + beside(x, e, n)) * inv
        out[c] = x[: out.shape[1], :LANES]
        copies.append(pltpu.make_async_copy(out.at[c], far.at[c], sems.at[c]))
        copies[-1].start()
    for copy in copies:
        copy.wait()


def pairs(start, count):
    out = []
    for i in range(start, count - 1, 2):
        out += [(i, i + 1), (i + 1, i)]
    return out


def routes(wide, narrow):
    narrow_first = pairs(0, narrow)
    narrow_second = pairs(1, narrow) + [(0, narrow - 1), (narrow - 1, 0)]
    wide_first = pairs(0, wide)
    both = [(a * narrow + k, b * narrow + k) for a, b in pairs(1, wide) for k in range(narrow)]
    for a in (0, wide - 1):
        both += [(a * narrow + k, a * narrow + (k ^ 1)) for k in range(narrow)]
    return narrow_first, narrow_second, wide_first, both


def exchange_narrow(first, second, route):
    second = lax.ppermute(second, "narrow", route[1])
    return second, lax.ppermute(first, "narrow", route[0])


def exchange_wide(first, second, route):
    second = lax.ppermute(second, ("wide", "narrow"), route[3])
    return second, lax.ppermute(first, "wide", route[2])


def exchange(x, route, wide=None, second=None, first=None):
    pick = lambda y: x if y is None else y
    return (*exchange_wide(pick(wide), x, route), *exchange_narrow(pick(first), pick(second), route))


def body(
    sizes,
    block,
    east,
    north,
    fine_groups,
    tiles_one,
    columns_one,
    live_one,
    coarse_groups,
    tiles_two,
    columns_two,
    live_two,
    coarser_groups,
    chain_forward,
    chain_gain,
    chain_backward,
):
    wide, narrow = sizes
    route = routes(wide, narrow)
    cols = block.shape[0]
    rows = block.shape[1]
    count1, slots = tiles_one.shape[:2]
    count2 = tiles_two.shape[0]

    if narrow != 4 or wide & (wide - 1):
        raise NotImplementedError("mesh shape")
    alone = [("wide", 1 << i) for i in reversed(range(1, (wide - 1).bit_length()))]
    near_wide, near_narrow = ("wide", 1), ("narrow", narrow - 1)
    orders = [
        alone + [near_wide, near_narrow, ("narrow", 1)],
        alone + [near_narrow, near_wide, ("narrow", 1)],
    ]
    share = chain_forward.shape[1] // narrow
    held = []
    done = []

    def swap(x, axis, step):
        return lax.ppermute(x, axis, [(i, i ^ step) for i in range(lax.axis_size(axis))])

    def gather_step(anchor):
        step = alone[len(done)]
        merged = held if len(held) == 1 else [jnp.concatenate(held, axis=0)]
        merged, _ = lax.optimization_barrier((merged, anchor))
        held[:] = merged + [swap(m, *step) for m in merged]
        done.append(step)

    rim = sds((cols + 2, RIM, LANES))
    flags = sds((LEVEL3 + 1,), jnp.int32)
    flags, fields, first, second, piece = call(
        functools.partial(fine_first_kernel, sizes),
        [flags, sds((cols + 2, rows, LANES)), rim, rim, sds((2 * share // cols, cols, LANES))],
        (block, east, north, chain_forward, chain_backward),
        scratch=[
            pltpu.VMEM((2, rows, LANES), F32),
            pltpu.VMEM((2, share, LANES), F32),
            pltpu.SemaphoreType.DMA((5,)),
        ],
        specs=[HBM] * 5,
        scalars=(0,),
    )
    held.append(piece)
    gather_step(first)
    o2, o1 = exchange_narrow(first, second, route)

    half = count1 // 2
    split = sds((half, 2 * LANES, slots * LANES), BF16)
    held_tiles = [pltpu.VMEM((half, *tiles_one.shape[1:]), F32)]
    stream_sems = [pltpu.SemaphoreType.DMA((8,))]
    idx1, idx2, tiles1, d1, tiles2, d2, tiles1_far = call(
        setup_kernel,
        [
            sds((slots, count1), jnp.int32),
            sds((slots, count2), jnp.int32),
            split,
            sds((count1, 1, LANES)),
            sds((count2, *split.shape[1:]), BF16),
            sds((count2, 1, LANES)),
            split,
        ],
        (flags, columns_one.T, live_one.T, columns_two, live_two, tiles_one, tiles_two),
        scratch=[pltpu.VMEM((slots - 1, count1), jnp.int32)] * 2
        + [pltpu.VMEM((count2, slots - 1), jnp.int32)] * 2
        + held_tiles
        + [
            pltpu.VMEM(tiles_two.shape, F32),
            pltpu.VMEM((half, *tiles_one.shape[2:]), F32),
            pltpu.VMEM((slots, count1), jnp.int32),
            pltpu.VMEM((count2, slots), jnp.int32),
            pltpu.SMEM((count2, slots), jnp.int32),
            pltpu.SemaphoreType.DMA((6,)),
        ]
        + stream_sems,
        specs=[SMEM] + [HBM] * 6,
        far=(6,),
        scalars=(0, 1),
    )
    groups1 = coarse_groups.reshape(count1, LANES)
    groups2 = coarser_groups.reshape(-1, LANES)
    o2, idx1, idx2, tiles1, tiles2, d1, d2 = lax.optimization_barrier((o2, idx1, idx2, tiles1, tiles2, d1, d2))

    rim = sds((cols + 2, RIM, 2 * LANES))
    ext, first, second = call(
        fine_second_kernel,
        [sds((cols + 2, rows, 2 * LANES)), rim, rim],
        (flags, fields, o2, o1),
        specs=[SMEM] + [VMEM] * 3,
    )
    while len(done) < len(alone):
        gather_step(first)
    o2, o1 = exchange_wide(first, second, route)
    field1 = sds((count1, cols, LANES))
    field2 = sds((count2, cols, LANES))
    more = -(-(count1 + count2) // cols)
    hold = {"t1a": tiles1, "d1": d1}
    t1 = ("t1a", "t1b")
    kept = sds((2 * cols + 3, rows + PAD, 2 * LANES))
    maps_rows = sum(x.shape[0] for x in held)
    x1_rows = count1 + more
    riding = sds((x1_rows + maps_rows // 2, cols, LANES))
    keep, b1, x1, x1_w, x1_n = call(
        functools.partial(fine_down_kernel, share // cols),
        [kept, field1, sds((x1_rows, cols, LANES)), riding, riding],
        (flags, ext, o2, o1, fine_groups, "d1", groups1, groups2, tuple(held)),
        scratch=[
            pltpu.VMEM((2 * cols, rows, LANES), F32),
            pltpu.VMEM(kept.shape, F32),
            pltpu.SemaphoreType.DMA((1,)),
        ],
        specs=[SMEM] + [VMEM] * 8,
        mib=16,
        us=7,
        hold=hold,
        far=(0,),
    )
    hold["b1"] = b1

    xs1 = [pltpu.VMEM((5 * count1 + 1, 8, LANES), F32)]
    xs2 = [pltpu.VMEM((5 * count2 + 1, 8, LANES), F32)]
    lead = [SMEM]

    def smooth(level, x):
        idx, like, xs = (idx1, field1, xs1) if level == 1 else (idx2, field2, xs2)
        near = exchange(x, route)
        ins = (idx, t1 if level == 1 else ("t2",), f"d{level}", f"b{level}", x, *near)
        return call(smooth_kernel, like, ins, xs, lead + [VMEM] * 8, hold=hold), near

    near = exchange(x1, route, wide=x1_w, second=x1_n)
    tiles1_second, tiles1_second_far = call(
        second_half_kernel,
        [split, split],
        (tiles_one, b1),
        scratch=held_tiles + stream_sems,
        specs=[HBM, VMEM],
        far=(1,),
    )
    hold["t1b"] = tiles1_second
    riding = sds((count1 + maps_rows, cols, LANES))
    x2, x2_w, x2_n = call(
        functools.partial(smooth_ride_kernel, x1_rows),
        [field1, riding, riding],
        (idx1, t1, "d1", "b1", x1, *near, x1_w, x1_n),
        xs1,
        lead + [VMEM] * 10,
        hold=hold,
    )
    groups = call(
        groups_kernel,
        sds((5, count1 + count2, LANES), jnp.int32),
        (groups1, x1, *near),
        specs=[VMEM] * 6,
        us=1,
    )
    near = exchange(x2, route, wide=x2_w, second=x2_n)
    maps = (x2_n, near[2], x2_w, near[1])
    hold |= {"x2": x2, "groups": groups, "d2": d2}
    left, scaled = call(
        residual_kernel,
        [field1, field1],
        (idx1, t1, "d1", "b1", "x2", *near),
        xs1,
        lead + [VMEM] * 8,
        hold=hold,
    )
    near = exchange(scaled, route)
    bundle = call(
        functools.partial(bundle_kernel, count1),
        sds((4 * maps_rows, cols, LANES)),
        (scaled, *maps),
        specs=[VMEM] * 5,
        us=0.5,
    )
    maps = (bundle, lax.ppermute(bundle, "narrow", route[0]))
    b2, y1 = call(
        restrict_one_kernel,
        [field2, field2],
        (idx1, t1, left, groups1, "d2", scaled, *near),
        xs1,
        lead + [VMEM] * 9,
        hold=hold,
    )

    del hold["t1a"], hold["t1b"]
    hold |= {"b2": b2, "t2": tiles2}
    y2, _ = smooth(2, y1)
    maps, y2 = lax.optimization_barrier((maps, y2))
    near = exchange(y2, route)
    chain_shape = sds((wide, 2, 2 * LANES, LANES), BF16)
    big = wide > 16
    chain = call(
        functools.partial(chain_maps_kernel, orders),
        chain_shape,
        (flags, *maps),
        specs=[SMEM] + [PLAIN if big else VMEM] * 2,
        mib=48 if big else 12,
        us=0.7,
        loose=(0,) if big else (),
    )
    if not big:
        hold["chain"] = chain
    hold["y2"] = y2
    left, scaled = call(
        residual_kernel,
        [field2, field2],
        (idx2, ("t2",), "d2", "b2", "y2", *near),
        xs2,
        lead + [VMEM] * 8,
        us=1,
        hold=hold,
    )
    out3 = call(
        restrict_two_kernel,
        sds((wide * narrow, cols, LANES)),
        (flags, idx2, ("t2",), left, "groups", chain_gain, scaled, *exchange(scaled, route)),
        xs2,
        [SMEM, SMEM] + [VMEM] * 9,
        hold=hold,
    )
    pieces = lax.all_to_all(out3, ("wide", "narrow"), 0, 0)
    y3 = call(
        chain_kernel,
        field2,
        (flags, chain if big else "chain", pieces, idx2, ("t2",), "d2", "y2", "groups"),
        xs2 + [pltpu.VMEM((wide, cols, LANES), F32)],
        [SMEM, PLAIN if big else VMEM, VMEM, SMEM] + [VMEM] * 4,
        mib=32 if big else 12,
        us=3,
        hold=hold,
    )
    hold.pop("chain", None)
    y4, _ = smooth(2, y3)
    y5, _ = smooth(2, y4)

    for name in ("t2", "d2", "b2", "y2"):
        del hold[name]
    hold |= {"t1a": tiles1_far, "t1b": tiles1_second_far}
    x3 = call(
        prolong_one_kernel,
        field1,
        (idx1, t1, "d1", "x2", "groups", y5, *exchange(y5, route)),
        xs1,
        lead + [VMEM] * 9,
        hold=hold,
    )
    del hold["x2"], hold["groups"]
    x4, _ = smooth(1, x3)
    rim = sds((cols, RIM, LANES))
    spread, first, second = call(
        fine_spread_kernel,
        [sds((cols, rows, LANES)), rim, rim],
        (flags, t1, idx1, "d1", "b1", fine_groups, x4, *exchange(x4, route)),
        xs1 + [pltpu.VMEM((count1, cols, LANES), F32)],
        [SMEM, VMEM, SMEM] + [VMEM] * 8,
        us=3,
        hold=hold,
    )
    o2, o1 = exchange_narrow(first, second, route)
    rim = sds((cols, RIM, 2 * LANES))
    for name in ("t1a", "t1b", "d1", "b1"):
        del hold[name]
    ext, first, second = call(
        fine_second_kernel,
        [sds((cols, rows, 2 * LANES)), rim, rim],
        (flags, spread, o2, o1),
        specs=[SMEM] + [VMEM] * 3,
        us=1,
        hold=hold,
    )
    o2, o1 = exchange_wide(first, second, route)
    whole = sds((cols, rows, LANES))
    return call(
        fine_up_kernel,
        whole,
        (flags, keep, ext, o2, o1),
        scratch=[pltpu.VMEM(whole.shape, F32), pltpu.SemaphoreType.DMA((cols,))],
        specs=[SMEM] + [VMEM] * 4,
        far=(0,),
    )


def solution(mesh):
    tile = P(("wide", "narrow"), None, None, None)
    pair = P(("wide", "narrow"), None)
    line = P(("wide", "narrow"))
    grid = P("wide", "narrow")
    chain = P("wide", None, None)
    field = P(None, "wide", "narrow")
    in_specs = (
        field, grid, grid, grid, tile, pair, pair, line, tile, pair, pair, line, chain, chain, chain,
    )
    sizes = (mesh.shape["wide"], mesh.shape["narrow"])
    return jax.shard_map(
        functools.partial(body, sizes), mesh=mesh, in_specs=in_specs, out_specs=field, check_vma=False
    )
```

```python
import functools

import jax
import jax.numpy as jnp
from jax import lax
from jax.experimental import pallas as pl
from jax.experimental.pallas import tpu as pltpu
from jax.sharding import PartitionSpec as P

F32 = jnp.float32
BF16 = jnp.bfloat16
SHIFT = 0.1
JACOBI = 0.6
LANES = 128
ORDER = 1
RIM = 4
PAD = 2 * RIM
VMEM = pl.BlockSpec(memory_space=pltpu.VMEM)
PLAIN = pl.BlockSpec(memory_space=pltpu.VMEM)
HBM = pl.BlockSpec(memory_space=pl.ANY)
SMEM = pl.BlockSpec(memory_space=pltpu.SMEM)
W_ODD, N_ODD, HAS_WEST, HAS_EAST, HAS_SOUTH, HAS_NORTH, W_AT, N_AT, LEVEL3 = range(9)


def sds(shape, dtype=F32):
    return jax.ShapeDtypeStruct(shape, dtype)


def constrain(x, spec):
    if spec is VMEM:
        return pltpu.with_memory_space_constraint(x, pltpu.VMEM)
    if spec is HBM:
        return pltpu.with_memory_space_constraint(x, pltpu.HBM)
    if spec is SMEM:
        return pltpu.with_memory_space_constraint(x, pltpu.SMEM)
    return x


def call(kernel, outs, ins, scratch=(), specs=None, mib=12, us=2, hold=None, far=(), loose=(), scalars=()):
    hold = {} if hold is None else hold
    outs, tree = jax.tree.flatten(outs)
    specs = jax.tree.leaves([[spec] * len(x) if isinstance(x, tuple) else spec for x, spec in zip(ins, specs)])
    ins, shape_in = jax.tree.flatten(list(ins))
    places = {x: i for i, x in enumerate(ins) if isinstance(x, str)}
    rest = [name for name in hold if name not in places]
    places |= {name: len(ins) + i for i, name in enumerate(rest)}
    inputs = [hold[x] if isinstance(x, str) else x for x in ins] + [hold[name] for name in rest]
    specs = list(specs) + [VMEM] * len(rest)
    inputs = [constrain(x, spec) for x, spec in zip(inputs, specs)]
    count_in, count_out = len(ins), len(outs)
    spaces = [pltpu.HBM if i in far else pltpu.SMEM if i in scalars else pltpu.VMEM for i in range(len(outs))]
    shapes = [o if i in loose else spaces[i](o.shape, o.dtype) for i, o in enumerate(outs)]
    shapes += [pltpu.VMEM(hold[name].shape, hold[name].dtype) for name in hold]

    def inner(*refs):
        first = len(inputs)
        kernel(
            *jax.tree.unflatten(shape_in, refs[:first][::ORDER][:count_in]),
            *refs[first : first + count_out],
            *refs[first + count_out + len(hold) :],
        )

    results = pl.pallas_call(
        inner,
        out_shape=shapes,
        in_specs=specs[::ORDER],
        out_specs=[{pltpu.HBM: HBM, pltpu.SMEM: SMEM, pltpu.VMEM: VMEM}[space] for space in spaces]
        + [VMEM] * len(hold),
        scratch_shapes=list(scratch),
        input_output_aliases={
            range(len(inputs))[::ORDER][places[name]]: count_out + i for i, name in enumerate(hold)
        },
        compiler_params=pltpu.CompilerParams(vmem_limit_bytes=mib * 1024 * 1024),
        cost_estimate=pl.CostEstimate(flops=0, bytes_accessed=int(us * 3.5e6), transcendentals=0),
    )(*inputs[::ORDER])
    for name, value in zip(list(hold), results[count_out:]):
        hold[name] = value
    return jax.tree.unflatten(tree, results[:count_out])


def parts_of(x):
    hi = x.astype(BF16).astype(F32)
    return hi, x - hi


def rows_of(x):
    return jnp.concatenate(parts_of(x), axis=0)


def twice(x):
    return jnp.concatenate([x, x], axis=0).astype(BF16)


def rows_sum(s):
    return s[0:4] + s[4:8]


def dot_nt(a, b):
    return lax.dot_general(a, b, (((1,), (1,)), ((), ())), preferred_element_type=F32)


def store_parts(xs, base, x):
    count, cols, _ = x.shape
    for i, part in enumerate(parts_of(x)):
        xs[pl.ds(base, count), i * cols : (i + 1) * cols, :] = part


def split_map(m):
    hi = m.astype(BF16)
    return hi, (m - hi.astype(F32)).astype(BF16)


def diagonal(tile):
    size = tile.shape[0]
    row = lax.broadcasted_iota(jnp.int32, tile.shape, 0)
    col = lax.broadcasted_iota(jnp.int32, tile.shape, 1)
    diag = jnp.sum(jnp.where(row == col, tile, 0.0), axis=0, keepdims=True)
    lane = lax.broadcasted_iota(jnp.int32, diag.shape, 1)
    return jnp.where(lane < size, diag, 1.0)


def split_tile(tile, r, k, t_ref):
    size = tile.shape[0]
    if size < LANES:
        tile = jnp.concatenate([tile, jnp.zeros((size, LANES - size), F32)], axis=1)
    hi, lo = split_map(tile)
    t_ref[r, 0:size, k * LANES : (k + 1) * LANES] = hi
    t_ref[r, LANES : LANES + size, k * LANES : (k + 1) * LANES] = lo
    return tile


class Stream:
    def __init__(self, half, tiles, held, t_ref, sems, parts=4):
        self.count, self.slots = held.shape[0], held.shape[1]
        self.step = self.count // parts
        self.held, self.t_ref = held, t_ref
        self.loads = [
            pltpu.make_async_copy(
                tiles.at[pl.ds(half * self.count + i * self.step, self.step)],
                held.at[pl.ds(i * self.step, self.step)],
                sems.at[i],
            )
            for i in range(parts)
        ]
        for load in self.loads:
            load.start()

    def run(self):
        for i, load in enumerate(self.loads):
            load.wait()
            for r in range(i * self.step, (i + 1) * self.step):
                for k in range(self.slots):
                    split_tile(self.held[r, k], r, k, self.t_ref)


def store_kernel(t_refs, _, *refs):
    *fars, sems = refs
    copies = [pltpu.make_async_copy(a, b, sems.at[i]) for i, (a, b) in enumerate(zip(t_refs, fars))]
    for copy in copies:
        copy.start()
    for copy in copies:
        copy.wait()


def half_kernel(half, tiles, _, t_ref, held, sems):
    Stream(half, tiles, held, t_ref, sems).run()


def setup_kernel(
    flags, columns1, live1, columns2, live2, tiles1, tiles2,
    idx1, idx2, d1, t2, d2,
    in1, in2, in3, in4, held2, fronts, held1, held_two, turned, sems,
):
    ins = [(columns1, in1), (live1, in2), (columns2, in3), (live2, in4), (tiles2, held2)]
    ins.append((tiles1.at[:, 0], fronts))
    ins = [pltpu.make_async_copy(a, b, sems.at[i]) for i, (a, b) in enumerate(ins)]
    for copy in ins:
        copy.start()
    for copy in ins:
        copy.wait()
    w_odd, n_odd = flags[W_ODD], flags[N_ODD]
    region = (0, 1 + w_odd, 2 - w_odd, 3 + n_odd, 4 - n_odd)
    there = (1, flags[HAS_WEST], flags[HAS_EAST], flags[HAS_SOUTH], flags[HAS_NORTH])
    for columns, live, held, dim in ((in1, in2, held1, 1), (in3, in4, held_two, 0)):
        code = columns[...]
        count = code.shape[dim]
        place = jnp.full(code.shape, 5 * count, jnp.int32)
        for s in range(5):
            at = code - s * count
            ok = (at >= 0) & (at < count) & (live[...] == 1) & (there[s] == 1)
            place = jnp.where(ok, at + region[s] * count, place)
        own = lax.broadcasted_iota(jnp.int32, held.shape, dim)
        held[...] = own
        if dim:
            held[1:, :] = place
        else:
            held[:, 1:] = place
    copies = [
        pltpu.make_async_copy(held1, idx1, sems.at[0]),
        pltpu.make_async_copy(held_two, turned, sems.at[1]),
    ]
    for copy in copies:
        copy.start()
    t2[...] = jnp.zeros_like(t2)
    for r in range(held2.shape[0]):
        for k in range(held2.shape[1]):
            tile = split_tile(held2[r, k], r, k, t2)
            if k == 0:
                row = lax.broadcasted_iota(jnp.int32, tile.shape, 0)
                col = lax.broadcasted_iota(jnp.int32, tile.shape, 1)
                diag = jnp.sum(jnp.where(row == col, tile, 0.0), axis=0, keepdims=True)
                lane = lax.broadcasted_iota(jnp.int32, diag.shape, 1)
                d2[r] = jnp.where(lane < tile.shape[0], diag, 1.0)
    for r in range(fronts.shape[0]):
        d1[r] = diagonal(fronts[r])
    for copy in copies:
        copy.wait()
    slots, count = idx2.shape
    for k in range(slots):
        for r in range(count):
            idx2[k, r] = turned[r, k]


def apply_tiles(t_ref, xs, idx, done=None):
    slots, count = idx.shape
    first = 0 if done is None else 1
    out = []
    for r in range(count):
        lhs = twice(jnp.concatenate([xs[idx[k, r]] for k in range(first, slots)], axis=1))
        t, at = t_ref[r // t_ref[0].shape[0]], r % t_ref[0].shape[0]
        both = dot_nt(lhs, t[at, :, first * LANES :])[0:8]
        value = rows_sum(both[:, :LANES] + both[:, LANES:])
        out.append(value if done is None else value + done[r])
    return out


def own_kernel(t_ref, x, out):
    for r in range(x.shape[0]):
        t, at = t_ref[r // t_ref[0].shape[0]], r % t_ref[0].shape[0]
        both = dot_nt(twice(rows_of(x[r])), t[at, :, :LANES])[0:8]
        out[r] = rows_sum(both[:, :LANES] + both[:, LANES:])


def fill_blocks(xs, own, others, count):
    xs[5 * count] = jnp.zeros((8, LANES), F32)
    store_parts(xs, 0, own[0:count])
    for i, other in enumerate(others):
        store_parts(xs, (i + 1) * count, other[0:count])


def ride(out, start, refs):
    for ref, first in refs:
        count = ref.shape[0] - first
        out[start : start + count] = ref[first:]
        start += count


def smooth_more_kernel(idx, t, d, b, own, o1, o2, o3, o4, done, out, xs):
    smooth_kernel(idx, t, d, b, own, o1, o2, o3, o4, out, xs, done)


def smooth_kernel(idx, t, d, b, own, o1, o2, o3, o4, out, xs, done=None):
    count = b.shape[0]
    fill_blocks(xs, own, (o1, o2, o3, o4), count)
    for r, ax in enumerate(apply_tiles(t, xs, idx, done)):
        out[r] = own[r] + JACOBI * (b[r] - ax) / d[r]


def smooth_ride_kernel(first, idx, t, d, b, own, o1, o2, o3, o4, sent_w, sent_n, out, out_w, out_n, xs):
    smooth_kernel(idx, t, d, b, own, o1, o2, o3, o4, out, xs)
    count = b.shape[0]
    out_w[0:count] = out[...]
    out_n[0:count] = out[...]
    ride(out_n, count, ((sent_w, first), (o2, first)))
    ride(out_w, count, ((sent_n, first), (o3, first)))


def residual_more_kernel(idx, t, d, b, own, o1, o2, o3, o4, done, left, scaled, xs):
    residual_kernel(idx, t, d, b, own, o1, o2, o3, o4, left, scaled, xs, done)


def residual_kernel(idx, t, d, b, own, o1, o2, o3, o4, left, scaled, xs, done=None):
    count = b.shape[0]
    fill_blocks(xs, own, (o1, o2, o3, o4), count)
    for r, ax in enumerate(apply_tiles(t, xs, idx, done)):
        rest = b[r] - ax
        left[r] = rest
        scaled[r] = rest / d[r]


def restrict_one_kernel(idx, t, left, groups, d2, own, o1, o2, o3, o4, done, b2, first, xs):
    count = left.shape[0]
    fill_blocks(xs, own, (o1, o2, o3, o4), count)
    total = None
    coarse_tiles, _, lanes = b2.shape
    size = coarse_tiles * lanes // 2
    for r, ax in enumerate(apply_tiles(t, xs, idx, done)):
        rows = twice(rows_of(left[r] - 0.5 * ax))
        hot = lax.broadcasted_iota(jnp.int32, (size, LANES), 0) == groups[r : r + 1, :]
        term = dot_nt(rows, hot.astype(F32).astype(BF16))
        total = term if total is None else total + term
    total = rows_sum(total[0:8])
    half = LANES // 2
    lane = lax.broadcasted_iota(jnp.int32, (4, LANES), 1)
    for tile in range(coarse_tiles):
        pair = total[:, (tile // 2) * LANES : (tile // 2 + 1) * LANES]
        if tile % 2:
            pair = pltpu.roll(pair, half, 1)
        value = jnp.where(lane < half, pair, 0.0)
        b2[tile] = value
        first[tile] = JACOBI * value / d2[tile]


def restrict_two_kernel(flags, idx, t, left, groups, gain, own, o1, o2, o3, o4, out, xs):
    count = left.shape[0]
    fill_blocks(xs, own, (o1, o2, o3, o4), count)
    offset = flags[N_AT] * flags[LEVEL3]
    first = groups.shape[1] - count
    total = None
    for r, ax in enumerate(apply_tiles(t, xs, idx)):
        rows = twice(rows_of(left[r] - 0.5 * ax))
        group = groups[0, first + r : first + r + 1, :] + offset
        hot = lax.broadcasted_iota(jnp.int32, (LANES, LANES), 0) == group
        term = dot_nt(rows, hot.astype(F32).astype(BF16))
        total = term if total is None else total + term
    total = map_product(jnp.concatenate(split_map(gain[0]), axis=0), rows_sum(total[0:8]))
    out[...] = jnp.broadcast_to(total[None], out.shape)


def bundle_kernel(first, _, *refs):
    *pieces, out = refs
    ride(out, 0, [(ref, first) for ref in pieces])


def chain_maps_kernel(orders, flags, bundle, other, out):
    half = bundle.shape[0] // 2
    for i, order in enumerate(orders):
        position = 0
        span = half * 2 >> len(order)
        rows = span * bundle.shape[1]
        for ref in (bundle, other):
            for start in range(i * half, (i + 1) * half, span):
                v, q = flags[W_AT], flags[N_AT]
                for bit, (axis, step) in enumerate(order):
                    if position >> bit & 1:
                        v, q = (v ^ step, q) if axis == "wide" else (v, q ^ step)
                hi, lo = split_map(ref[start : start + span].reshape(rows, LANES))
                out[v, i, pl.ds(pl.multiple_of(q * rows, rows), rows), :] = hi
                out[v, i, pl.ds(pl.multiple_of(LANES + q * rows, rows), rows), :] = lo
                position += 1


def map_product(m, x):
    both = dot_nt(twice(rows_of(x)), m)[0:8]
    return rows_sum(both[:, :LANES] + both[:, LANES:])


def take_lanes(table, lanes):
    return jnp.take_along_axis(table, jnp.broadcast_to(lanes, table.shape), axis=1)


def groups_kernel(own1, own, o1, o2, o3, o4, out):
    count1 = own1.shape[0]
    for p, ref in enumerate((own, o1, o2, o3, o4)):
        cols = ref.shape[1]
        for i in range(out.shape[1]):
            row = ref[count1 + i // cols, i % cols : i % cols + 1, :]
            out[p, i : i + 1] = row.astype(jnp.int32)


def chain_kernel(flags, maps, pieces, idx, t, d, x2, groups, out, xs, ys):
    blocks = maps.shape[0]
    narrow = pieces.shape[0] // blocks
    carry = None
    for v in range(blocks):
        now = pieces[v * narrow]
        for k in range(1, narrow):
            now = now + pieces[v * narrow + k]
        if carry is not None:
            now = now + map_product(maps[v, 0], carry)
        ys[v] = now
        carry = now
    for v in range(blocks - 2, -1, -1):
        carry = ys[v] + map_product(maps[v, 1], carry)
        ys[v] = carry
    count = x2.shape[0]
    xs[5 * count] = jnp.zeros((8, LANES), F32)
    size = flags[LEVEL3]
    w, n, w_odd, n_odd = flags[W_AT], flags[N_AT], flags[W_ODD], flags[N_ODD]
    n_first = n + 1 - 2 * n_odd
    n_second = jnp.clip(n - 1 + 2 * n_odd, 0, narrow - 1)
    w_first = w + 1 - 2 * w_odd
    w_second = jnp.clip(w - 1 + 2 * w_odd, 0, blocks - 1)
    where = ((w, n), (w_second, n), (w_first, n), (w, n_second), (w, n_first))
    lane = lax.broadcasted_iota(jnp.int32, (8, LANES), 1)
    first = groups.shape[1] - count
    for p, (pw, pn) in enumerate(where):
        table = rows_of(ys[pw])
        for tile in range(count):
            index = groups[p, first + tile : first + tile + 1, :]
            index = (index + pn * size) & (LANES - 1)
            got = take_lanes(table, index)
            xs[p * count + tile] = jnp.where(lane < LANES // 2, got, 0.0)
    for r, ax in enumerate(apply_tiles(t, xs, idx)):
        out[r] = x2[r] + (rows_sum(xs[r]) - 0.5 * ax / d[r])


def prolong_one_kernel(idx, t, d, x2, groups, own, o1, o2, o3, o4, out, xs):
    count = x2.shape[0]
    xs[5 * count] = jnp.zeros((8, LANES), F32)
    half = LANES // 2
    lane = lax.broadcasted_iota(jnp.int32, (4, LANES), 1)
    for p, u in enumerate((own, o1, o2, o3, o4)):
        tables = []
        for i in range(u.shape[0] // 2):
            wide = jnp.where(lane < half, u[2 * i], pltpu.roll(u[2 * i + 1], half, 1))
            tables.append(rows_of(wide))
        for tile in range(count):
            index = groups[p, tile : tile + 1, :]
            got = take_lanes(tables[0], index & (LANES - 1))
            for i in range(1, len(tables)):
                more = take_lanes(tables[i], index & (LANES - 1))
                got = jnp.where((index >> 7) == i, more, got)
            xs[p * count + tile] = got
    for r, ax in enumerate(apply_tiles(t, xs, idx)):
        out[r] = x2[r] + (rows_sum(xs[r]) - 0.5 * ax / d[r])


def live_weights(flags, east, north):
    row = lax.broadcasted_iota(jnp.int32, east.shape, 0)
    col = lax.broadcasted_iota(jnp.int32, east.shape, 1)
    east = jnp.where((flags[HAS_EAST] == 1) | (row < east.shape[0] - 1), east, 0.0)
    north = jnp.where((flags[HAS_NORTH] == 1) | (col < north.shape[1] - 1), north, 0.0)
    return east, north


def narrow_rims(flags, fields, first, second):
    odd = flags[N_ODD] == 1
    for i, field in enumerate(fields):
        turned = field.T
        low, high = turned[0:RIM], turned[-RIM:]
        first[i] = jnp.where(odd, low, high)
        second[i] = jnp.where(odd, high, low)


def narrow_sides(flags, first, second, i):
    odd = flags[N_ODD] == 1
    low = jnp.where(odd, first[i], second[i]) * flags[HAS_SOUTH].astype(F32)
    high = jnp.where(odd, second[i], first[i]) * flags[HAS_NORTH].astype(F32)
    return low, high


def with_sides(flags, field, first, second, i):
    low, high = narrow_sides(flags, first, second, i)
    side = jnp.concatenate([high, jnp.zeros((LANES - 2 * RIM, LANES), F32), low], axis=0)
    return jnp.concatenate([field, side.T], axis=1)


def wide_rims(flags, field, i, first, second):
    odd = flags[W_ODD] == 1
    low, high = field[0:RIM], field[-RIM:]
    first[i] = jnp.where(odd, low, high)
    second[i] = jnp.where(odd, high, low)


def with_rows(flags, field, first, second, i):
    odd = flags[W_ODD] == 1
    low = jnp.where(odd, first[i], second[i]) * flags[HAS_WEST].astype(F32)
    high = jnp.where(odd, second[i], first[i]) * flags[HAS_EAST].astype(F32)
    return jnp.concatenate([field, high, low], axis=0)


def fine_first_kernel(
    sizes, block, east, north, forward, backward, flags, fields, first, second, piece, edges, maps, sems
):
    wide, narrow = sizes
    w, n = lax.axis_index("wide"), lax.axis_index("narrow")
    values = (
        w & 1, n & 1, w > 0, w < wide - 1, n > 0, n < narrow - 1, w, n, forward.shape[1] // narrow,
    )
    for i, value in enumerate(values):
        flags[i] = jnp.int32(value)
    cols = block.shape[0]
    rows = maps.shape[1]
    at = pl.multiple_of(n * rows, rows)
    copies = [
        (block, fields.at[0:cols]),
        (east, edges.at[0]),
        (north, edges.at[1]),
        (forward.at[0, pl.ds(at, rows)], maps.at[0]),
        (backward.at[0, pl.ds(at, rows)], maps.at[1]),
    ]
    copies = [pltpu.make_async_copy(a, b, sems.at[i]) for i, (a, b) in enumerate(copies)]
    for copy in copies:
        copy.start()
    for copy in copies:
        copy.wait()
    fields[cols], fields[cols + 1] = live_weights(flags, edges[0], edges[1])
    narrow_rims(flags, [fields[c] for c in range(cols + 2)], first, second)
    piece[...] = maps[...].reshape(piece.shape)


def fine_second_kernel(flags, fields, o2, o1, ext, first, second):
    for i in range(fields.shape[0]):
        wider = with_sides(flags, fields[i], o1, o2, i)
        ext[i] = wider
        wide_rims(flags, wider, i, first, second)


def beside(field, e, n):
    rows, lanes = field.shape
    return (
        e * pltpu.roll(field, rows - 1, 0)
        + pltpu.roll(e * field, 1, 0)
        + n * pltpu.roll(field, lanes - 1, 1)
        + pltpu.roll(n * field, 1, 1)
    )


def fine_down_kernel(span, flags, ext, o2, o1, groups, d1, near1, near2, maps, far, b1, first, out_w, out_n, q_ref, keep, sem):
    cols = ext.shape[0] - 2
    rows = ext.shape[1]
    e = with_rows(flags, ext[cols], o1, o2, cols)
    n = with_rows(flags, ext[cols + 1], o1, o2, cols + 1)
    diag = SHIFT + e + pltpu.roll(e, 1, 0) + n + pltpu.roll(n, 1, 1)
    inv = 1.0 / diag
    step_inv = JACOBI * inv
    keep[2 * cols] = e
    keep[2 * cols + 1] = n
    keep[2 * cols + 2] = step_inv
    for c in range(cols):
        b = with_rows(flags, ext[c], o1, o2, c)
        x1 = b * step_inv
        x2 = (2.0 - JACOBI) * x1 + beside(x1, e, n) * step_inv
        keep[c] = x2
        keep[cols + c] = x1
        rest = b - diag * x2 + beside(x2, e, n)
        q = 0.5 * (rest + beside(rest * inv, e, n))
        for i, part in enumerate(parts_of(q[:rows, :LANES])):
            q_ref[i * cols + c] = part
    copy = pltpu.make_async_copy(keep, far, sem.at[0])
    copy.start()
    count = b1.shape[0]
    step = 64
    one, zero = jnp.ones((), BF16), jnp.zeros((), BF16)
    lanes = lax.broadcasted_iota(jnp.int32, (LANES, LANES), 0).astype(F32).astype(BF16)

    def over_rows(x):
        return jnp.broadcast_to(x, (16, LANES)).astype(BF16)

    def add_rows(j, total):
        left, right = [], []
        for k in range(step):
            row = pl.ds(j * step + k, 1)
            group = groups[row, :]
            mask = lanes[0:count] == over_rows((group >> 7).astype(F32))
            low = over_rows((group & (LANES - 1)).astype(F32))
            picked = [jnp.where(mask, over_rows(q_ref[i, row, :]), zero) for i in range(2 * cols)]
            left.append(jnp.concatenate(picked, axis=0))
            low = jnp.concatenate([low] * (LANES // 16), axis=0)
            right.append(jnp.where(lanes == low, one, zero))
        return total + dot_nt(jnp.concatenate(left, axis=1), jnp.concatenate(right, axis=1))

    total = lax.fori_loop(
        0, rows // step, add_rows, jnp.zeros((2 * cols * count, LANES), F32)
    )
    size = cols * count
    total = total[0:size] + total[size : 2 * size]
    for c in range(cols):
        value = total[c * count : (c + 1) * count]
        b1[:, c, :] = value
        first[0:count, c, :] = JACOBI * value / d1[:, 0, :]
    groups = [near1[i : i + 1, :] for i in range(count)]
    for i in range(near2.shape[0]):
        row = near2[i : i + 1, :]
        groups += [row, pltpu.roll(row, LANES // 2, 1)]
    for i, group in enumerate(groups):
        first[count + i // cols, i % cols : i % cols + 1, :] = group.astype(F32)
    out_w[0 : first.shape[0]] = first[...]
    out_n[0 : first.shape[0]] = first[...]
    at = first.shape[0]
    for ref in maps:
        for start in range(0, ref.shape[0], 2 * span):
            out_w[at : at + span] = ref[start : start + span]
            out_n[at : at + span] = ref[start + span : start + 2 * span]
            at += span
    copy.wait()


def fine_spread_kernel(flags, t, idx, d, b, groups, own, o1, o2, o3, o4, done, spread, first, second, xs, us):
    count, cols, _ = b.shape
    fill_blocks(xs, own, (o1, o2, o3, o4), count)
    for r, ax in enumerate(apply_tiles(t, xs, idx, done)):
        us[r] = own[r] + JACOBI * (b[r] - ax) / d[r]
    rows = groups.shape[0]
    tables = [[jnp.broadcast_to(us[h, c : c + 1, :], (8, LANES)) for h in range(count)] for c in range(cols)]
    for j in range(rows // 8):
        group = groups[8 * j : 8 * j + 8, :]
        high, low = group >> 7, group & (LANES - 1)
        masks = [high == h for h in range(1, count)]
        for c in range(cols):
            value = jnp.take_along_axis(tables[c][0], low, axis=1)
            for h in range(1, count):
                got = jnp.take_along_axis(tables[c][h], low, axis=1)
                value = jnp.where(masks[h - 1], got, value)
            spread[c, 8 * j : 8 * j + 8, :] = value
    narrow_rims(flags, [spread[c] for c in range(cols)], first, second)


def fine_up_kernel(flags, keep, ext, o2, o1, far, out, sems):
    cols = out.shape[0]
    copies = []
    e, n, step_inv = keep[2 * cols], keep[2 * cols + 1], keep[2 * cols + 2]
    half_inv = (0.5 / JACOBI) * step_inv
    for c in range(cols):
        x1 = keep[cols + c]
        spread = with_rows(flags, ext[c], o1, o2, c)
        x = keep[c] + 0.5 * spread + beside(spread, e, n) * half_inv
        for _ in range(2):
            x = (1.0 - JACOBI) * x + x1 + beside(x, e, n) * step_inv
        out[c] = x[: out.shape[1], :LANES]
        copies.append(pltpu.make_async_copy(out.at[c], far.at[c], sems.at[c]))
        copies[-1].start()
    for copy in copies:
        copy.wait()


def pairs(start, count):
    out = []
    for i in range(start, count - 1, 2):
        out += [(i, i + 1), (i + 1, i)]
    return out


def routes(wide, narrow):
    narrow_first = pairs(0, narrow)
    narrow_second = pairs(1, narrow) + [(0, narrow - 1), (narrow - 1, 0)]
    wide_first = pairs(0, wide)
    both = [(a * narrow + k, b * narrow + k) for a, b in pairs(1, wide) for k in range(narrow)]
    for a in (0, wide - 1):
        both += [(a * narrow + k, a * narrow + (k ^ 1)) for k in range(narrow)]
    return narrow_first, narrow_second, wide_first, both


def exchange_narrow(first, second, route):
    second = lax.ppermute(second, "narrow", route[1])
    return second, lax.ppermute(first, "narrow", route[0])


def exchange_wide(first, second, route):
    second = lax.ppermute(second, ("wide", "narrow"), route[3])
    return second, lax.ppermute(first, "wide", route[2])


def exchange(x, route, wide=None, second=None, first=None):
    pick = lambda y: x if y is None else y
    return (*exchange_wide(pick(wide), x, route), *exchange_narrow(pick(first), pick(second), route))


def body(
    sizes,
    block,
    east,
    north,
    fine_groups,
    tiles_one,
    columns_one,
    live_one,
    coarse_groups,
    tiles_two,
    columns_two,
    live_two,
    coarser_groups,
    chain_forward,
    chain_gain,
    chain_backward,
):
    wide, narrow = sizes
    route = routes(wide, narrow)
    cols = block.shape[0]
    rows = block.shape[1]
    count1, slots = tiles_one.shape[:2]
    count2 = tiles_two.shape[0]

    if narrow != 4 or wide & (wide - 1):
        raise NotImplementedError("mesh shape")
    alone = [("wide", 1 << i) for i in reversed(range(1, (wide - 1).bit_length()))]
    near_wide, near_narrow = ("wide", 1), ("narrow", narrow - 1)
    orders = [
        alone + [near_wide, near_narrow, ("narrow", 1)],
        alone + [near_narrow, near_wide, ("narrow", 1)],
    ]
    share = chain_forward.shape[1] // narrow
    held = []
    done = []

    def swap(x, axis, step):
        return lax.ppermute(x, axis, [(i, i ^ step) for i in range(lax.axis_size(axis))])

    def gather_step(anchor):
        step = alone[len(done)]
        merged = held if len(held) == 1 else [jnp.concatenate(held, axis=0)]
        merged, _ = lax.optimization_barrier((merged, anchor))
        held[:] = merged + [swap(m, *step) for m in merged]
        done.append(step)

    rim = sds((cols + 2, RIM, LANES))
    flags = sds((LEVEL3 + 1,), jnp.int32)
    flags, fields, first, second, piece = call(
        functools.partial(fine_first_kernel, sizes),
        [flags, sds((cols + 2, rows, LANES)), rim, rim, sds((2 * share // cols, cols, LANES))],
        (block, east, north, chain_forward, chain_backward),
        scratch=[
            pltpu.VMEM((2, rows, LANES), F32),
            pltpu.VMEM((2, share, LANES), F32),
            pltpu.SemaphoreType.DMA((5,)),
        ],
        specs=[HBM] * 5,
        scalars=(0,),
    )
    held.append(piece)
    gather_step(first)
    o2, o1 = exchange_narrow(first, second, route)

    half = count1 // 2
    split = sds((half, 2 * LANES, slots * LANES), BF16)
    held_tiles = [pltpu.VMEM((half, *tiles_one.shape[1:]), F32)]
    stream_sems = [pltpu.SemaphoreType.DMA((4,))]
    idx1, idx2, d1, tiles2, d2 = call(
        setup_kernel,
        [
            sds((slots, count1), jnp.int32),
            sds((slots, count2), jnp.int32),
            sds((count1, 1, LANES)),
            sds((count2, *split.shape[1:]), BF16),
            sds((count2, 1, LANES)),
        ],
        (flags, columns_one.T, live_one.T, columns_two, live_two, tiles_one, tiles_two),
        scratch=[pltpu.VMEM((slots - 1, count1), jnp.int32)] * 2
        + [pltpu.VMEM((count2, slots - 1), jnp.int32)] * 2
        + [
            pltpu.VMEM(tiles_two.shape, F32),
            pltpu.VMEM((count1, *tiles_one.shape[2:]), F32),
            pltpu.VMEM((slots, count1), jnp.int32),
            pltpu.VMEM((count2, slots), jnp.int32),
            pltpu.SMEM((count2, slots), jnp.int32),
            pltpu.SemaphoreType.DMA((6,)),
        ],
        specs=[SMEM] + [HBM] * 6,
        scalars=(0, 1),
    )
    groups1 = coarse_groups.reshape(count1, LANES)
    groups2 = coarser_groups.reshape(-1, LANES)
    o2, idx1, idx2, tiles2, d1, d2 = lax.optimization_barrier((o2, idx1, idx2, tiles2, d1, d2))

    rim = sds((cols + 2, RIM, 2 * LANES))
    ext, first, second = call(
        fine_second_kernel,
        [sds((cols + 2, rows, 2 * LANES)), rim, rim],
        (flags, fields, o2, o1),
        specs=[SMEM] + [VMEM] * 3,
    )
    while len(done) < len(alone):
        gather_step(first)
    o2, o1 = exchange_wide(first, second, route)

    def split_half(i, after):
        return call(
            functools.partial(half_kernel, i),
            split,
            (tiles_one, after),
            scratch=held_tiles + stream_sems,
            specs=[HBM, VMEM],
        )

    tiles1 = split_half(0, first)
    field1 = sds((count1, cols, LANES))
    field2 = sds((count2, cols, LANES))
    more = -(-(count1 + count2) // cols)
    hold = {"t1a": tiles1, "d1": d1}
    t1 = ("t1a", "t1b")
    kept = sds((2 * cols + 3, rows + PAD, 2 * LANES))
    maps_rows = sum(x.shape[0] for x in held)
    x1_rows = count1 + more
    riding = sds((x1_rows + maps_rows // 2, cols, LANES))
    keep, b1, x1, x1_w, x1_n = call(
        functools.partial(fine_down_kernel, share // cols),
        [kept, field1, sds((x1_rows, cols, LANES)), riding, riding],
        (flags, ext, o2, o1, fine_groups, "d1", groups1, groups2, tuple(held)),
        scratch=[
            pltpu.VMEM((2 * cols, rows, LANES), F32),
            pltpu.VMEM(kept.shape, F32),
            pltpu.SemaphoreType.DMA((1,)),
        ],
        specs=[SMEM] + [VMEM] * 8,
        mib=16,
        us=7,
        hold=hold,
        far=(0,),
    )
    hold["b1"] = b1

    xs1 = [pltpu.VMEM((5 * count1 + 1, 8, LANES), F32)]
    xs2 = [pltpu.VMEM((5 * count2 + 1, 8, LANES), F32)]
    lead = [SMEM]

    def own_part(x):
        return call(own_kernel, field1, (tuple(hold[name] for name in t1), x), specs=[VMEM, VMEM], us=0.5)

    def smooth(level, x):
        idx, like, xs = (idx1, field1, xs1) if level == 1 else (idx2, field2, xs2)
        near = exchange(x, route)
        ins = (idx, t1 if level == 1 else ("t2",), f"d{level}", f"b{level}", x, *near)
        if level == 1:
            ins = (*ins, own_part(x))
        kernel = smooth_more_kernel if level == 1 else smooth_kernel
        return call(kernel, like, ins, xs, lead + [VMEM] * (len(ins) - 1), hold=hold), near

    near = exchange(x1, route, wide=x1_w, second=x1_n)
    hold["t1b"] = split_half(1, b1)
    riding = sds((count1 + maps_rows, cols, LANES))
    x2, x2_w, x2_n = call(
        functools.partial(smooth_ride_kernel, x1_rows),
        [field1, riding, riding],
        (idx1, t1, "d1", "b1", x1, *near, x1_w, x1_n),
        xs1,
        lead + [VMEM] * 10,
        hold=hold,
    )
    groups = call(
        groups_kernel,
        sds((5, count1 + count2, LANES), jnp.int32),
        (groups1, x1, *near),
        specs=[VMEM] * 6,
        us=1,
    )
    near = exchange(x2, route, wide=x2_w, second=x2_n)
    maps = (x2_n, near[2], x2_w, near[1])
    hold |= {"x2": x2, "groups": groups, "d2": d2}
    left, scaled = call(
        residual_more_kernel,
        [field1, field1],
        (idx1, t1, "d1", "b1", "x2", *near, own_part(x2)),
        xs1,
        lead + [VMEM] * 9,
        hold=hold,
    )
    near = exchange(scaled, route)
    bundle = call(
        functools.partial(bundle_kernel, count1),
        sds((4 * maps_rows, cols, LANES)),
        (scaled, *maps),
        specs=[VMEM] * 5,
        us=0.5,
    )
    maps = (bundle, lax.ppermute(bundle, "narrow", route[0]))
    b2, y1 = call(
        restrict_one_kernel,
        [field2, field2],
        (idx1, t1, left, groups1, "d2", scaled, *near, own_part(scaled)),
        xs1,
        lead + [VMEM] * 10,
        hold=hold,
    )

    near = exchange(y1, route)
    tiles1 = call(
        store_kernel,
        [split, split],
        (t1, y1),
        scratch=[pltpu.SemaphoreType.DMA((2,))],
        specs=[VMEM, VMEM],
        far=(0, 1),
        hold=hold,
    )
    del hold["t1a"], hold["t1b"]
    hold |= {"b2": b2, "t2": tiles2}
    y2 = call(
        smooth_kernel, field2, (idx2, ("t2",), "d2", "b2", y1, *near), xs2, lead + [VMEM] * 8, hold=hold
    )
    maps, y2 = lax.optimization_barrier((maps, y2))
    near = exchange(y2, route)
    chain_shape = sds((wide, 2, 2 * LANES, LANES), BF16)
    big = wide > 16
    chain = call(
        functools.partial(chain_maps_kernel, orders),
        chain_shape,
        (flags, *maps),
        specs=[SMEM] + [PLAIN if big else VMEM] * 2,
        mib=48 if big else 12,
        us=0.7,
        loose=(0,) if big else (),
    )
    if not big:
        hold["chain"] = chain
    hold["y2"] = y2
    left, scaled = call(
        residual_kernel,
        [field2, field2],
        (idx2, ("t2",), "d2", "b2", "y2", *near),
        xs2,
        lead + [VMEM] * 8,
        us=1,
        hold=hold,
    )
    out3 = call(
        restrict_two_kernel,
        sds((wide * narrow, cols, LANES)),
        (flags, idx2, ("t2",), left, "groups", chain_gain, scaled, *exchange(scaled, route)),
        xs2,
        [SMEM, SMEM] + [VMEM] * 9,
        hold=hold,
    )
    pieces = lax.all_to_all(out3, ("wide", "narrow"), 0, 0)
    y3 = call(
        chain_kernel,
        field2,
        (flags, chain if big else "chain", pieces, idx2, ("t2",), "d2", "y2", "groups"),
        xs2 + [pltpu.VMEM((wide, cols, LANES), F32)],
        [SMEM, PLAIN if big else VMEM, VMEM, SMEM] + [VMEM] * 4,
        mib=32 if big else 12,
        us=3,
        hold=hold,
    )
    hold.pop("chain", None)
    y4, _ = smooth(2, y3)
    y5, _ = smooth(2, y4)

    for name in ("t2", "d2", "b2", "y2"):
        del hold[name]
    hold |= {"t1a": tiles1[0], "t1b": tiles1[1]}
    x3 = call(
        prolong_one_kernel,
        field1,
        (idx1, t1, "d1", "x2", "groups", y5, *exchange(y5, route)),
        xs1,
        lead + [VMEM] * 9,
        hold=hold,
    )
    del hold["x2"], hold["groups"]
    x4, _ = smooth(1, x3)
    rim = sds((cols, RIM, LANES))
    spread, first, second = call(
        fine_spread_kernel,
        [sds((cols, rows, LANES)), rim, rim],
        (flags, t1, idx1, "d1", "b1", fine_groups, x4, *exchange(x4, route), own_part(x4)),
        xs1 + [pltpu.VMEM((count1, cols, LANES), F32)],
        [SMEM, VMEM, SMEM] + [VMEM] * 9,
        us=3,
        hold=hold,
    )
    o2, o1 = exchange_narrow(first, second, route)
    rim = sds((cols, RIM, 2 * LANES))
    for name in ("t1a", "t1b", "d1", "b1"):
        del hold[name]
    ext, first, second = call(
        fine_second_kernel,
        [sds((cols, rows, 2 * LANES)), rim, rim],
        (flags, spread, o2, o1),
        specs=[SMEM] + [VMEM] * 3,
        us=1,
        hold=hold,
    )
    o2, o1 = exchange_wide(first, second, route)
    whole = sds((cols, rows, LANES))
    return call(
        fine_up_kernel,
        whole,
        (flags, keep, ext, o2, o1),
        scratch=[pltpu.VMEM(whole.shape, F32), pltpu.SemaphoreType.DMA((cols,))],
        specs=[SMEM] + [VMEM] * 4,
        far=(0,),
    )


def solution(mesh):
    tile = P(("wide", "narrow"), None, None, None)
    pair = P(("wide", "narrow"), None)
    line = P(("wide", "narrow"))
    grid = P("wide", "narrow")
    chain = P("wide", None, None)
    field = P(None, "wide", "narrow")
    in_specs = (
        field, grid, grid, grid, tile, pair, pair, line, tile, pair, pair, line, chain, chain, chain,
    )
    sizes = (mesh.shape["wide"], mesh.shape["narrow"])
    return jax.shard_map(
        functools.partial(body, sizes), mesh=mesh, in_specs=in_specs, out_specs=field, check_vma=False
    )
```

```python
import functools

import jax
import jax.numpy as jnp
from jax import lax
from jax.experimental import pallas as pl
from jax.experimental.pallas import tpu as pltpu
from jax.sharding import PartitionSpec as P

F32 = jnp.float32
BF16 = jnp.bfloat16
SHIFT = 0.1
JACOBI = 0.6
LANES = 128
ORDER = 1
RIM = 4
PAD = 2 * RIM
VMEM = pl.BlockSpec(memory_space=pltpu.VMEM)
PLAIN = pl.BlockSpec(memory_space=pltpu.VMEM)
HBM = pl.BlockSpec(memory_space=pl.ANY)
SMEM = pl.BlockSpec(memory_space=pltpu.SMEM)
W_ODD, N_ODD, HAS_WEST, HAS_EAST, HAS_SOUTH, HAS_NORTH, W_AT, N_AT, LEVEL3 = range(9)


def sds(shape, dtype=F32):
    return jax.ShapeDtypeStruct(shape, dtype)


def constrain(x, spec):
    if spec is VMEM:
        return pltpu.with_memory_space_constraint(x, pltpu.VMEM)
    if spec is HBM:
        return pltpu.with_memory_space_constraint(x, pltpu.HBM)
    if spec is SMEM:
        return pltpu.with_memory_space_constraint(x, pltpu.SMEM)
    return x


def call(kernel, outs, ins, scratch=(), specs=None, mib=12, us=2, hold=None, far=(), loose=(), scalars=()):
    hold = {} if hold is None else hold
    outs, tree = jax.tree.flatten(outs)
    specs = jax.tree.leaves([[spec] * len(x) if isinstance(x, tuple) else spec for x, spec in zip(ins, specs)])
    ins, shape_in = jax.tree.flatten(list(ins))
    places = {x: i for i, x in enumerate(ins) if isinstance(x, str)}
    rest = [name for name in hold if name not in places]
    places |= {name: len(ins) + i for i, name in enumerate(rest)}
    inputs = [hold[x] if isinstance(x, str) else x for x in ins] + [hold[name] for name in rest]
    specs = list(specs) + [VMEM] * len(rest)
    inputs = [constrain(x, spec) for x, spec in zip(inputs, specs)]
    count_in, count_out = len(ins), len(outs)
    spaces = [pltpu.HBM if i in far else pltpu.SMEM if i in scalars else pltpu.VMEM for i in range(len(outs))]
    shapes = [o if i in loose else spaces[i](o.shape, o.dtype) for i, o in enumerate(outs)]
    shapes += [pltpu.VMEM(hold[name].shape, hold[name].dtype) for name in hold]

    def inner(*refs):
        first = len(inputs)
        kernel(
            *jax.tree.unflatten(shape_in, refs[:first][::ORDER][:count_in]),
            *refs[first : first + count_out],
            *refs[first + count_out + len(hold) :],
        )

    results = pl.pallas_call(
        inner,
        out_shape=shapes,
        in_specs=specs[::ORDER],
        out_specs=[{pltpu.HBM: HBM, pltpu.SMEM: SMEM, pltpu.VMEM: VMEM}[space] for space in spaces]
        + [VMEM] * len(hold),
        scratch_shapes=list(scratch),
        input_output_aliases={
            range(len(inputs))[::ORDER][places[name]]: count_out + i for i, name in enumerate(hold)
        },
        compiler_params=pltpu.CompilerParams(vmem_limit_bytes=mib * 1024 * 1024),
        cost_estimate=pl.CostEstimate(flops=0, bytes_accessed=int(us * 3.5e6), transcendentals=0),
    )(*inputs[::ORDER])
    for name, value in zip(list(hold), results[count_out:]):
        hold[name] = value
    return jax.tree.unflatten(tree, results[:count_out])


def parts_of(x):
    hi = x.astype(BF16).astype(F32)
    return hi, x - hi


def rows_of(x):
    return jnp.concatenate(parts_of(x), axis=0)


def twice(x):
    return jnp.concatenate([x, x], axis=0).astype(BF16)


def rows_sum(s):
    return s[0:4] + s[4:8]


def dot_nt(a, b):
    return lax.dot_general(a, b, (((1,), (1,)), ((), ())), preferred_element_type=F32)


def store_parts(xs, base, x):
    count, cols, _ = x.shape
    for i, part in enumerate(parts_of(x)):
        xs[pl.ds(base, count), i * cols : (i + 1) * cols, :] = part


def split_map(m):
    hi = m.astype(BF16)
    return hi, (m - hi.astype(F32)).astype(BF16)


def diagonal(tile):
    size = tile.shape[0]
    row = lax.broadcasted_iota(jnp.int32, tile.shape, 0)
    col = lax.broadcasted_iota(jnp.int32, tile.shape, 1)
    diag = jnp.sum(jnp.where(row == col, tile, 0.0), axis=0, keepdims=True)
    lane = lax.broadcasted_iota(jnp.int32, diag.shape, 1)
    return jnp.where(lane < size, diag, 1.0)


def split_tile(tile, r, k, t_ref):
    size = tile.shape[0]
    if size < LANES:
        tile = jnp.concatenate([tile, jnp.zeros((size, LANES - size), F32)], axis=1)
    hi, lo = split_map(tile)
    t_ref[r, 0:size, k * LANES : (k + 1) * LANES] = hi
    t_ref[r, LANES : LANES + size, k * LANES : (k + 1) * LANES] = lo
    return tile


class Stream:
    def __init__(self, half, tiles, held, t_ref, sems, parts=4):
        self.count, self.slots = held.shape[0], held.shape[1]
        self.step = self.count // parts
        self.held, self.t_ref = held, t_ref
        self.loads = [
            pltpu.make_async_copy(
                tiles.at[pl.ds(half * self.count + i * self.step, self.step)],
                held.at[pl.ds(i * self.step, self.step)],
                sems.at[i],
            )
            for i in range(parts)
        ]
        for load in self.loads:
            load.start()

    def run(self):
        for i, load in enumerate(self.loads):
            load.wait()
            for r in range(i * self.step, (i + 1) * self.step):
                for k in range(self.slots):
                    split_tile(self.held[r, k], r, k, self.t_ref)


def store_kernel(t_refs, _, *refs):
    *fars, sems = refs
    copies = [pltpu.make_async_copy(a, b, sems.at[i]) for i, (a, b) in enumerate(zip(t_refs, fars))]
    for copy in copies:
        copy.start()
    for copy in copies:
        copy.wait()


def half_kernel(half, tiles, _, t_ref, held, sems):
    Stream(half, tiles, held, t_ref, sems).run()


def setup_kernel(
    flags, columns1, live1, columns2, live2, tiles1, tiles2,
    idx1, idx2, d1, t2, d2,
    in1, in2, in3, in4, held2, fronts, held1, held_two, turned, sems,
):
    ins = [(columns1, in1), (live1, in2), (columns2, in3), (live2, in4), (tiles2, held2)]
    ins.append((tiles1.at[:, 0], fronts))
    ins = [pltpu.make_async_copy(a, b, sems.at[i]) for i, (a, b) in enumerate(ins)]
    for copy in ins:
        copy.start()
    for copy in ins:
        copy.wait()
    w_odd, n_odd = flags[W_ODD], flags[N_ODD]
    region = (0, 1 + w_odd, 2 - w_odd, 3 + n_odd, 4 - n_odd)
    there = (1, flags[HAS_WEST], flags[HAS_EAST], flags[HAS_SOUTH], flags[HAS_NORTH])
    for columns, live, held, dim in ((in1, in2, held1, 1), (in3, in4, held_two, 0)):
        code = columns[...]
        count = code.shape[dim]
        place = jnp.full(code.shape, 5 * count, jnp.int32)
        for s in range(5):
            at = code - s * count
            ok = (at >= 0) & (at < count) & (live[...] == 1) & (there[s] == 1)
            place = jnp.where(ok, at + region[s] * count, place)
        own = lax.broadcasted_iota(jnp.int32, held.shape, dim)
        held[...] = own
        if dim:
            held[1:, :] = place
        else:
            held[:, 1:] = place
    copies = [
        pltpu.make_async_copy(held1, idx1, sems.at[0]),
        pltpu.make_async_copy(held_two, turned, sems.at[1]),
    ]
    for copy in copies:
        copy.start()
    t2[...] = jnp.zeros_like(t2)
    for r in range(held2.shape[0]):
        for k in range(held2.shape[1]):
            tile = split_tile(held2[r, k], r, k, t2)
            if k == 0:
                row = lax.broadcasted_iota(jnp.int32, tile.shape, 0)
                col = lax.broadcasted_iota(jnp.int32, tile.shape, 1)
                diag = jnp.sum(jnp.where(row == col, tile, 0.0), axis=0, keepdims=True)
                lane = lax.broadcasted_iota(jnp.int32, diag.shape, 1)
                d2[r] = jnp.where(lane < tile.shape[0], diag, 1.0)
    for r in range(fronts.shape[0]):
        d1[r] = diagonal(fronts[r])
    for copy in copies:
        copy.wait()
    slots, count = idx2.shape
    for k in range(slots):
        for r in range(count):
            idx2[k, r] = turned[r, k]


def apply_tiles(t_ref, xs, idx, done=None):
    slots, count = idx.shape
    first = 0 if done is None else 1
    out = []
    for r in range(count):
        lhs = twice(jnp.concatenate([xs[idx[k, r]] for k in range(first, slots)], axis=1))
        t, at = t_ref[r // t_ref[0].shape[0]], r % t_ref[0].shape[0]
        both = dot_nt(lhs, t[at, :, first * LANES :])[0:8]
        value = rows_sum(both[:, :LANES] + both[:, LANES:])
        out.append(value if done is None else value + done[r])
    return out


def own_kernel(t_ref, x, out):
    for r in range(x.shape[0]):
        t, at = t_ref[r // t_ref[0].shape[0]], r % t_ref[0].shape[0]
        both = dot_nt(twice(rows_of(x[r])), t[at, :, :LANES])[0:8]
        out[r] = rows_sum(both[:, :LANES] + both[:, LANES:])


def fill_blocks(xs, own, others, count):
    xs[5 * count] = jnp.zeros((8, LANES), F32)
    store_parts(xs, 0, own[0:count])
    for i, other in enumerate(others):
        store_parts(xs, (i + 1) * count, other[0:count])


def ride(out, start, refs):
    for ref, first in refs:
        count = ref.shape[0] - first
        out[start : start + count] = ref[first:]
        start += count


def smooth_more_kernel(idx, t, d, b, own, o1, o2, o3, o4, done, out, xs):
    smooth_kernel(idx, t, d, b, own, o1, o2, o3, o4, out, xs, done)


def smooth_kernel(idx, t, d, b, own, o1, o2, o3, o4, out, xs, done=None):
    count = b.shape[0]
    fill_blocks(xs, own, (o1, o2, o3, o4), count)
    for r, ax in enumerate(apply_tiles(t, xs, idx, done)):
        out[r] = own[r] + JACOBI * (b[r] - ax) / d[r]


def smooth_ride_kernel(span, idx, t, d, b, own, o1, o2, o3, o4, maps, out, out_w, out_n, xs):
    smooth_kernel(idx, t, d, b, own, o1, o2, o3, o4, out, xs)
    at = b.shape[0]
    out_w[0:at] = out[...]
    out_n[0:at] = out[...]
    for ref in maps:
        for start in range(0, ref.shape[0], 2 * span):
            out_w[at : at + span] = ref[start : start + span]
            out_n[at : at + span] = ref[start + span : start + 2 * span]
            at += span


def residual_ride_kernel(
    idx, t, d, b, own, o1, o2, o3, o4, done, sent_w, sent_n, left, scaled, out_w, out_n, xs
):
    residual_kernel(idx, t, d, b, own, o1, o2, o3, o4, left, scaled, xs, done)
    count = b.shape[0]
    out_w[0:count] = scaled[...]
    out_n[0:count] = scaled[...]
    ride(out_n, count, ((sent_w, count), (o2, count)))
    ride(out_w, count, ((sent_n, count), (o3, count)))


def residual_more_kernel(idx, t, d, b, own, o1, o2, o3, o4, done, left, scaled, xs):
    residual_kernel(idx, t, d, b, own, o1, o2, o3, o4, left, scaled, xs, done)


def residual_kernel(idx, t, d, b, own, o1, o2, o3, o4, left, scaled, xs, done=None):
    count = b.shape[0]
    fill_blocks(xs, own, (o1, o2, o3, o4), count)
    for r, ax in enumerate(apply_tiles(t, xs, idx, done)):
        rest = b[r] - ax
        left[r] = rest
        scaled[r] = rest / d[r]


def restrict_one_kernel(idx, t, left, groups, d2, own, o1, o2, o3, o4, done, b2, first, xs):
    count = left.shape[0]
    fill_blocks(xs, own, (o1, o2, o3, o4), count)
    total = None
    coarse_tiles, _, lanes = b2.shape
    size = coarse_tiles * lanes // 2
    for r, ax in enumerate(apply_tiles(t, xs, idx, done)):
        rows = twice(rows_of(left[r] - 0.5 * ax))
        hot = lax.broadcasted_iota(jnp.int32, (size, LANES), 0) == groups[r : r + 1, :]
        term = dot_nt(rows, hot.astype(F32).astype(BF16))
        total = term if total is None else total + term
    total = rows_sum(total[0:8])
    half = LANES // 2
    lane = lax.broadcasted_iota(jnp.int32, (4, LANES), 1)
    for tile in range(coarse_tiles):
        pair = total[:, (tile // 2) * LANES : (tile // 2 + 1) * LANES]
        if tile % 2:
            pair = pltpu.roll(pair, half, 1)
        value = jnp.where(lane < half, pair, 0.0)
        b2[tile] = value
        first[tile] = JACOBI * value / d2[tile]


def restrict_two_kernel(flags, idx, t, left, groups, gain, own, o1, o2, o3, o4, out, xs):
    count = left.shape[0]
    fill_blocks(xs, own, (o1, o2, o3, o4), count)
    offset = flags[N_AT] * flags[LEVEL3]
    first = groups.shape[1] - count
    total = None
    for r, ax in enumerate(apply_tiles(t, xs, idx)):
        rows = twice(rows_of(left[r] - 0.5 * ax))
        group = groups[0, first + r : first + r + 1, :] + offset
        hot = lax.broadcasted_iota(jnp.int32, (LANES, LANES), 0) == group
        term = dot_nt(rows, hot.astype(F32).astype(BF16))
        total = term if total is None else total + term
    total = map_product(jnp.concatenate(split_map(gain[0]), axis=0), rows_sum(total[0:8]))
    out[...] = jnp.broadcast_to(total[None], out.shape)


def bundle_kernel(first, _, *refs):
    *pieces, out = refs
    ride(out, 0, [(ref, first) for ref in pieces])


def chain_maps_kernel(orders, flags, bundle, other, out):
    half = bundle.shape[0] // 2
    for i, order in enumerate(orders):
        position = 0
        span = half * 2 >> len(order)
        rows = span * bundle.shape[1]
        for ref in (bundle, other):
            for start in range(i * half, (i + 1) * half, span):
                v, q = flags[W_AT], flags[N_AT]
                for bit, (axis, step) in enumerate(order):
                    if position >> bit & 1:
                        v, q = (v ^ step, q) if axis == "wide" else (v, q ^ step)
                hi, lo = split_map(ref[start : start + span].reshape(rows, LANES))
                out[v, i, pl.ds(pl.multiple_of(q * rows, rows), rows), :] = hi
                out[v, i, pl.ds(pl.multiple_of(LANES + q * rows, rows), rows), :] = lo
                position += 1


def map_product(m, x):
    both = dot_nt(twice(rows_of(x)), m)[0:8]
    return rows_sum(both[:, :LANES] + both[:, LANES:])


def take_lanes(table, lanes):
    return jnp.take_along_axis(table, jnp.broadcast_to(lanes, table.shape), axis=1)


def groups_kernel(own1, own, o1, o2, o3, o4, out):
    count1 = own1.shape[0]
    for p, ref in enumerate((own, o1, o2, o3, o4)):
        cols = ref.shape[1]
        for i in range(out.shape[1]):
            row = ref[count1 + i // cols, i % cols : i % cols + 1, :]
            out[p, i : i + 1] = row.astype(jnp.int32)


def chain_kernel(flags, maps, pieces, idx, t, d, x2, groups, out, xs, ys):
    blocks = maps.shape[0]
    narrow = pieces.shape[0] // blocks
    carry = None
    for v in range(blocks):
        now = pieces[v * narrow]
        for k in range(1, narrow):
            now = now + pieces[v * narrow + k]
        if carry is not None:
            now = now + map_product(maps[v, 0], carry)
        ys[v] = now
        carry = now
    for v in range(blocks - 2, -1, -1):
        carry = ys[v] + map_product(maps[v, 1], carry)
        ys[v] = carry
    count = x2.shape[0]
    xs[5 * count] = jnp.zeros((8, LANES), F32)
    size = flags[LEVEL3]
    w, n, w_odd, n_odd = flags[W_AT], flags[N_AT], flags[W_ODD], flags[N_ODD]
    n_first = n + 1 - 2 * n_odd
    n_second = jnp.clip(n - 1 + 2 * n_odd, 0, narrow - 1)
    w_first = w + 1 - 2 * w_odd
    w_second = jnp.clip(w - 1 + 2 * w_odd, 0, blocks - 1)
    where = ((w, n), (w_second, n), (w_first, n), (w, n_second), (w, n_first))
    lane = lax.broadcasted_iota(jnp.int32, (8, LANES), 1)
    first = groups.shape[1] - count
    for p, (pw, pn) in enumerate(where):
        table = rows_of(ys[pw])
        for tile in range(count):
            index = groups[p, first + tile : first + tile + 1, :]
            index = (index + pn * size) & (LANES - 1)
            got = take_lanes(table, index)
            xs[p * count + tile] = jnp.where(lane < LANES // 2, got, 0.0)
    for r, ax in enumerate(apply_tiles(t, xs, idx)):
        out[r] = x2[r] + (rows_sum(xs[r]) - 0.5 * ax / d[r])


def prolong_one_kernel(idx, t, d, x2, groups, own, o1, o2, o3, o4, out, xs):
    count = x2.shape[0]
    xs[5 * count] = jnp.zeros((8, LANES), F32)
    half = LANES // 2
    lane = lax.broadcasted_iota(jnp.int32, (4, LANES), 1)
    for p, u in enumerate((own, o1, o2, o3, o4)):
        tables = []
        for i in range(u.shape[0] // 2):
            wide = jnp.where(lane < half, u[2 * i], pltpu.roll(u[2 * i + 1], half, 1))
            tables.append(rows_of(wide))
        for tile in range(count):
            index = groups[p, tile : tile + 1, :]
            got = take_lanes(tables[0], index & (LANES - 1))
            for i in range(1, len(tables)):
                more = take_lanes(tables[i], index & (LANES - 1))
                got = jnp.where((index >> 7) == i, more, got)
            xs[p * count + tile] = got
    for r, ax in enumerate(apply_tiles(t, xs, idx)):
        out[r] = x2[r] + (rows_sum(xs[r]) - 0.5 * ax / d[r])


def live_weights(flags, east, north):
    row = lax.broadcasted_iota(jnp.int32, east.shape, 0)
    col = lax.broadcasted_iota(jnp.int32, east.shape, 1)
    east = jnp.where((flags[HAS_EAST] == 1) | (row < east.shape[0] - 1), east, 0.0)
    north = jnp.where((flags[HAS_NORTH] == 1) | (col < north.shape[1] - 1), north, 0.0)
    return east, north


def narrow_rims(flags, fields, first, second):
    odd = flags[N_ODD] == 1
    for i, field in enumerate(fields):
        turned = field.T
        low, high = turned[0:RIM], turned[-RIM:]
        first[i] = jnp.where(odd, low, high)
        second[i] = jnp.where(odd, high, low)


def narrow_sides(flags, first, second, i):
    odd = flags[N_ODD] == 1
    low = jnp.where(odd, first[i], second[i]) * flags[HAS_SOUTH].astype(F32)
    high = jnp.where(odd, second[i], first[i]) * flags[HAS_NORTH].astype(F32)
    return low, high


def with_sides(flags, field, first, second, i):
    low, high = narrow_sides(flags, first, second, i)
    side = jnp.concatenate([high, jnp.zeros((LANES - 2 * RIM, LANES), F32), low], axis=0)
    return jnp.concatenate([field, side.T], axis=1)


def wide_rims(flags, field, i, first, second):
    odd = flags[W_ODD] == 1
    low, high = field[0:RIM], field[-RIM:]
    first[i] = jnp.where(odd, low, high)
    second[i] = jnp.where(odd, high, low)


def with_rows(flags, field, first, second, i):
    odd = flags[W_ODD] == 1
    low = jnp.where(odd, first[i], second[i]) * flags[HAS_WEST].astype(F32)
    high = jnp.where(odd, second[i], first[i]) * flags[HAS_EAST].astype(F32)
    return jnp.concatenate([field, high, low], axis=0)


def fine_first_kernel(
    sizes, block, east, north, forward, backward, flags, fields, first, second, piece, edges, maps, sems
):
    wide, narrow = sizes
    w, n = lax.axis_index("wide"), lax.axis_index("narrow")
    values = (
        w & 1, n & 1, w > 0, w < wide - 1, n > 0, n < narrow - 1, w, n, forward.shape[1] // narrow,
    )
    for i, value in enumerate(values):
        flags[i] = jnp.int32(value)
    cols = block.shape[0]
    rows = maps.shape[1]
    at = pl.multiple_of(n * rows, rows)
    copies = [
        (block, fields.at[0:cols]),
        (east, edges.at[0]),
        (north, edges.at[1]),
        (forward.at[0, pl.ds(at, rows)], maps.at[0]),
        (backward.at[0, pl.ds(at, rows)], maps.at[1]),
    ]
    copies = [pltpu.make_async_copy(a, b, sems.at[i]) for i, (a, b) in enumerate(copies)]
    for copy in copies:
        copy.start()
    for copy in copies:
        copy.wait()
    fields[cols], fields[cols + 1] = live_weights(flags, edges[0], edges[1])
    narrow_rims(flags, [fields[c] for c in range(cols + 2)], first, second)
    piece[...] = maps[...].reshape(piece.shape)


def fine_second_kernel(flags, fields, o2, o1, ext, first, second):
    for i in range(fields.shape[0]):
        wider = with_sides(flags, fields[i], o1, o2, i)
        ext[i] = wider
        wide_rims(flags, wider, i, first, second)


def beside(field, e, n):
    rows, lanes = field.shape
    return (
        e * pltpu.roll(field, rows - 1, 0)
        + pltpu.roll(e * field, 1, 0)
        + n * pltpu.roll(field, lanes - 1, 1)
        + pltpu.roll(n * field, 1, 1)
    )


def fine_down_kernel(flags, ext, o2, o1, groups, d1, near1, near2, far, b1, first, q_ref, keep, sem):
    cols = ext.shape[0] - 2
    rows = ext.shape[1]
    e = with_rows(flags, ext[cols], o1, o2, cols)
    n = with_rows(flags, ext[cols + 1], o1, o2, cols + 1)
    diag = SHIFT + e + pltpu.roll(e, 1, 0) + n + pltpu.roll(n, 1, 1)
    inv = 1.0 / diag
    step_inv = JACOBI * inv
    keep[2 * cols] = e
    keep[2 * cols + 1] = n
    keep[2 * cols + 2] = step_inv
    for c in range(cols):
        b = with_rows(flags, ext[c], o1, o2, c)
        x1 = b * step_inv
        x2 = (2.0 - JACOBI) * x1 + beside(x1, e, n) * step_inv
        keep[c] = x2
        keep[cols + c] = x1
        rest = b - diag * x2 + beside(x2, e, n)
        q = 0.5 * (rest + beside(rest * inv, e, n))
        for i, part in enumerate(parts_of(q[:rows, :LANES])):
            q_ref[i * cols + c] = part
    copy = pltpu.make_async_copy(keep, far, sem.at[0])
    copy.start()
    count = b1.shape[0]
    step = 64
    one, zero = jnp.ones((), BF16), jnp.zeros((), BF16)
    lanes = lax.broadcasted_iota(jnp.int32, (LANES, LANES), 0).astype(F32).astype(BF16)

    def over_rows(x):
        return jnp.broadcast_to(x, (16, LANES)).astype(BF16)

    def add_rows(j, total):
        left, right = [], []
        for k in range(step):
            row = pl.ds(j * step + k, 1)
            group = groups[row, :]
            mask = lanes[0:count] == over_rows((group >> 7).astype(F32))
            low = over_rows((group & (LANES - 1)).astype(F32))
            picked = [jnp.where(mask, over_rows(q_ref[i, row, :]), zero) for i in range(2 * cols)]
            left.append(jnp.concatenate(picked, axis=0))
            low = jnp.concatenate([low] * (LANES // 16), axis=0)
            right.append(jnp.where(lanes == low, one, zero))
        return total + dot_nt(jnp.concatenate(left, axis=1), jnp.concatenate(right, axis=1))

    total = lax.fori_loop(
        0, rows // step, add_rows, jnp.zeros((2 * cols * count, LANES), F32)
    )
    size = cols * count
    total = total[0:size] + total[size : 2 * size]
    for c in range(cols):
        value = total[c * count : (c + 1) * count]
        b1[:, c, :] = value
        first[0:count, c, :] = JACOBI * value / d1[:, 0, :]
    groups = [near1[i : i + 1, :] for i in range(count)]
    for i in range(near2.shape[0]):
        row = near2[i : i + 1, :]
        groups += [row, pltpu.roll(row, LANES // 2, 1)]
    for i, group in enumerate(groups):
        first[count + i // cols, i % cols : i % cols + 1, :] = group.astype(F32)
    copy.wait()


def fine_spread_kernel(flags, t, idx, d, b, groups, own, o1, o2, o3, o4, done, spread, first, second, xs, us):
    count, cols, _ = b.shape
    fill_blocks(xs, own, (o1, o2, o3, o4), count)
    for r, ax in enumerate(apply_tiles(t, xs, idx, done)):
        us[r] = own[r] + JACOBI * (b[r] - ax) / d[r]
    rows = groups.shape[0]
    tables = [[jnp.broadcast_to(us[h, c : c + 1, :], (8, LANES)) for h in range(count)] for c in range(cols)]
    for j in range(rows // 8):
        group = groups[8 * j : 8 * j + 8, :]
        high, low = group >> 7, group & (LANES - 1)
        masks = [high == h for h in range(1, count)]
        for c in range(cols):
            value = jnp.take_along_axis(tables[c][0], low, axis=1)
            for h in range(1, count):
                got = jnp.take_along_axis(tables[c][h], low, axis=1)
                value = jnp.where(masks[h - 1], got, value)
            spread[c, 8 * j : 8 * j + 8, :] = value
    narrow_rims(flags, [spread[c] for c in range(cols)], first, second)


def fine_up_kernel(flags, keep, ext, o2, o1, far, out, sems):
    cols = out.shape[0]
    copies = []
    e, n, step_inv = keep[2 * cols], keep[2 * cols + 1], keep[2 * cols + 2]
    half_inv = (0.5 / JACOBI) * step_inv
    for c in range(cols):
        x1 = keep[cols + c]
        spread = with_rows(flags, ext[c], o1, o2, c)
        x = keep[c] + 0.5 * spread + beside(spread, e, n) * half_inv
        for _ in range(2):
            x = (1.0 - JACOBI) * x + x1 + beside(x, e, n) * step_inv
        out[c] = x[: out.shape[1], :LANES]
        copies.append(pltpu.make_async_copy(out.at[c], far.at[c], sems.at[c]))
        copies[-1].start()
    for copy in copies:
        copy.wait()


def pairs(start, count):
    out = []
    for i in range(start, count - 1, 2):
        out += [(i, i + 1), (i + 1, i)]
    return out


def routes(wide, narrow):
    narrow_first = pairs(0, narrow)
    narrow_second = pairs(1, narrow) + [(0, narrow - 1), (narrow - 1, 0)]
    wide_first = pairs(0, wide)
    both = [(a * narrow + k, b * narrow + k) for a, b in pairs(1, wide) for k in range(narrow)]
    for a in (0, wide - 1):
        both += [(a * narrow + k, a * narrow + (k ^ 1)) for k in range(narrow)]
    return narrow_first, narrow_second, wide_first, both


def exchange_narrow(first, second, route):
    second = lax.ppermute(second, "narrow", route[1])
    return second, lax.ppermute(first, "narrow", route[0])


def exchange_wide(first, second, route):
    second = lax.ppermute(second, ("wide", "narrow"), route[3])
    return second, lax.ppermute(first, "wide", route[2])


def exchange(x, route, wide=None, second=None, first=None):
    pick = lambda y: x if y is None else y
    return (*exchange_wide(pick(wide), x, route), *exchange_narrow(pick(first), pick(second), route))


def body(
    sizes,
    block,
    east,
    north,
    fine_groups,
    tiles_one,
    columns_one,
    live_one,
    coarse_groups,
    tiles_two,
    columns_two,
    live_two,
    coarser_groups,
    chain_forward,
    chain_gain,
    chain_backward,
):
    wide, narrow = sizes
    route = routes(wide, narrow)
    cols = block.shape[0]
    rows = block.shape[1]
    count1, slots = tiles_one.shape[:2]
    count2 = tiles_two.shape[0]

    if narrow != 4 or wide & (wide - 1):
        raise NotImplementedError("mesh shape")
    alone = [("wide", 1 << i) for i in reversed(range(1, (wide - 1).bit_length()))]
    near_wide, near_narrow = ("wide", 1), ("narrow", narrow - 1)
    orders = [
        alone + [near_wide, near_narrow, ("narrow", 1)],
        alone + [near_narrow, near_wide, ("narrow", 1)],
    ]
    share = chain_forward.shape[1] // narrow
    held = []
    done = []

    def swap(x, axis, step):
        return lax.ppermute(x, axis, [(i, i ^ step) for i in range(lax.axis_size(axis))])

    def gather_step(anchor):
        step = alone[len(done)]
        merged = held if len(held) == 1 else [jnp.concatenate(held, axis=0)]
        merged, _ = lax.optimization_barrier((merged, anchor))
        held[:] = merged + [swap(m, *step) for m in merged]
        done.append(step)

    rim = sds((cols + 2, RIM, LANES))
    flags = sds((LEVEL3 + 1,), jnp.int32)
    flags, fields, first, second, piece = call(
        functools.partial(fine_first_kernel, sizes),
        [flags, sds((cols + 2, rows, LANES)), rim, rim, sds((2 * share // cols, cols, LANES))],
        (block, east, north, chain_forward, chain_backward),
        scratch=[
            pltpu.VMEM((2, rows, LANES), F32),
            pltpu.VMEM((2, share, LANES), F32),
            pltpu.SemaphoreType.DMA((5,)),
        ],
        specs=[HBM] * 5,
        scalars=(0,),
    )
    held.append(piece)
    gather_step(first)
    o2, o1 = exchange_narrow(first, second, route)

    half = count1 // 2
    split = sds((half, 2 * LANES, slots * LANES), BF16)
    held_tiles = [pltpu.VMEM((half, *tiles_one.shape[1:]), F32)]
    stream_sems = [pltpu.SemaphoreType.DMA((4,))]
    idx1, idx2, d1, tiles2, d2 = call(
        setup_kernel,
        [
            sds((slots, count1), jnp.int32),
            sds((slots, count2), jnp.int32),
            sds((count1, 1, LANES)),
            sds((count2, *split.shape[1:]), BF16),
            sds((count2, 1, LANES)),
        ],
        (flags, columns_one.T, live_one.T, columns_two, live_two, tiles_one, tiles_two),
        scratch=[pltpu.VMEM((slots - 1, count1), jnp.int32)] * 2
        + [pltpu.VMEM((count2, slots - 1), jnp.int32)] * 2
        + [
            pltpu.VMEM(tiles_two.shape, F32),
            pltpu.VMEM((count1, *tiles_one.shape[2:]), F32),
            pltpu.VMEM((slots, count1), jnp.int32),
            pltpu.VMEM((count2, slots), jnp.int32),
            pltpu.SMEM((count2, slots), jnp.int32),
            pltpu.SemaphoreType.DMA((6,)),
        ],
        specs=[SMEM] + [HBM] * 6,
        scalars=(0, 1),
    )
    groups1 = coarse_groups.reshape(count1, LANES)
    groups2 = coarser_groups.reshape(-1, LANES)
    o2, idx1, idx2, tiles2, d1, d2 = lax.optimization_barrier((o2, idx1, idx2, tiles2, d1, d2))

    rim = sds((cols + 2, RIM, 2 * LANES))
    ext, first, second = call(
        fine_second_kernel,
        [sds((cols + 2, rows, 2 * LANES)), rim, rim],
        (flags, fields, o2, o1),
        specs=[SMEM] + [VMEM] * 3,
    )
    if alone:
        gather_step(first)
    o2, o1 = exchange_wide(first, second, route)

    def split_half(i, after):
        return call(
            functools.partial(half_kernel, i),
            split,
            (tiles_one, after),
            scratch=held_tiles + stream_sems,
            specs=[HBM, VMEM],
        )

    tiles1 = split_half(0, first)
    field1 = sds((count1, cols, LANES))
    field2 = sds((count2, cols, LANES))
    more = -(-(count1 + count2) // cols)
    hold = {"t1a": tiles1, "d1": d1}
    t1 = ("t1a", "t1b")
    kept = sds((2 * cols + 3, rows + PAD, 2 * LANES))
    x1_rows = count1 + more
    keep, b1, x1 = call(
        fine_down_kernel,
        [kept, field1, sds((x1_rows, cols, LANES))],
        (flags, ext, o2, o1, fine_groups, "d1", groups1, groups2),
        scratch=[
            pltpu.VMEM((2 * cols, rows, LANES), F32),
            pltpu.VMEM(kept.shape, F32),
            pltpu.SemaphoreType.DMA((1,)),
        ],
        specs=[SMEM] + [VMEM] * 7,
        mib=16,
        us=7,
        hold=hold,
        far=(0,),
    )
    hold["b1"] = b1

    xs1 = [pltpu.VMEM((5 * count1 + 1, 8, LANES), F32)]
    xs2 = [pltpu.VMEM((5 * count2 + 1, 8, LANES), F32)]
    lead = [SMEM]

    def own_part(x):
        return call(own_kernel, field1, (tuple(hold[name] for name in t1), x), specs=[VMEM, VMEM], us=0.5)

    def smooth(level, x):
        idx, like, xs = (idx1, field1, xs1) if level == 1 else (idx2, field2, xs2)
        near = exchange(x, route)
        ins = (idx, t1 if level == 1 else ("t2",), f"d{level}", f"b{level}", x, *near)
        if level == 1:
            ins = (*ins, own_part(x))
        kernel = smooth_more_kernel if level == 1 else smooth_kernel
        return call(kernel, like, ins, xs, lead + [VMEM] * (len(ins) - 1), hold=hold), near

    while len(done) < len(alone):
        gather_step(x1)
    near = exchange(x1, route)
    hold["t1b"] = split_half(1, b1)
    maps_rows = sum(x.shape[0] for x in held)
    riding = sds((count1 + maps_rows // 2, cols, LANES))
    x2, x2_w, x2_n = call(
        functools.partial(smooth_ride_kernel, share // cols),
        [field1, riding, riding],
        (idx1, t1, "d1", "b1", x1, *near, tuple(held)),
        xs1,
        lead + [VMEM] * 9,
        hold=hold,
    )
    groups = call(
        groups_kernel,
        sds((5, count1 + count2, LANES), jnp.int32),
        (groups1, x1, *near),
        specs=[VMEM] * 6,
        us=1,
    )
    near = exchange(x2, route, wide=x2_w, second=x2_n)
    hold |= {"x2": x2, "groups": groups, "d2": d2}
    riding = sds((count1 + maps_rows, cols, LANES))
    left, scaled, scaled_w, scaled_n = call(
        residual_ride_kernel,
        [field1, field1, riding, riding],
        (idx1, t1, "d1", "b1", "x2", *near, own_part(x2), x2_w, x2_n),
        xs1,
        lead + [VMEM] * 11,
        hold=hold,
    )
    near = exchange(scaled, route, wide=scaled_w, second=scaled_n)
    maps = (scaled_n, near[2], scaled_w, near[1])
    b2, y1 = call(
        restrict_one_kernel,
        [field2, field2],
        (idx1, t1, left, groups1, "d2", scaled, *near, own_part(scaled)),
        xs1,
        lead + [VMEM] * 10,
        hold=hold,
    )

    near = exchange(y1, route)
    bundle = call(
        functools.partial(bundle_kernel, count1),
        sds((4 * maps_rows, cols, LANES)),
        (y1, *maps),
        specs=[VMEM] * 5,
        us=0.5,
    )
    maps = (bundle, lax.ppermute(bundle, "narrow", route[0]))
    tiles1 = call(
        store_kernel,
        [split, split],
        (t1, y1),
        scratch=[pltpu.SemaphoreType.DMA((2,))],
        specs=[VMEM, VMEM],
        far=(0, 1),
        hold=hold,
    )
    del hold["t1a"], hold["t1b"]
    hold |= {"b2": b2, "t2": tiles2}
    y2 = call(
        smooth_kernel, field2, (idx2, ("t2",), "d2", "b2", y1, *near), xs2, lead + [VMEM] * 8, hold=hold
    )
    near = exchange(y2, route)
    hold["y2"] = y2
    left, scaled = call(
        residual_kernel,
        [field2, field2],
        (idx2, ("t2",), "d2", "b2", "y2", *near),
        xs2,
        lead + [VMEM] * 8,
        us=1,
        hold=hold,
    )
    maps, scaled = lax.optimization_barrier((maps, scaled))
    near = exchange(scaled, route)
    chain_shape = sds((wide, 2, 2 * LANES, LANES), BF16)
    big = wide > 16
    chain = call(
        functools.partial(chain_maps_kernel, orders),
        chain_shape,
        (flags, *maps),
        specs=[SMEM] + [PLAIN if big else VMEM] * 2,
        mib=48 if big else 12,
        us=0.7,
        loose=(0,) if big else (),
    )
    if not big:
        hold["chain"] = chain
    out3 = call(
        restrict_two_kernel,
        sds((wide * narrow, cols, LANES)),
        (flags, idx2, ("t2",), left, "groups", chain_gain, scaled, *near),
        xs2,
        [SMEM, SMEM] + [VMEM] * 9,
        hold=hold,
    )
    pieces = lax.all_to_all(out3, ("wide", "narrow"), 0, 0)
    y3 = call(
        chain_kernel,
        field2,
        (flags, chain if big else "chain", pieces, idx2, ("t2",), "d2", "y2", "groups"),
        xs2 + [pltpu.VMEM((wide, cols, LANES), F32)],
        [SMEM, PLAIN if big else VMEM, VMEM, SMEM] + [VMEM] * 4,
        mib=32 if big else 12,
        us=3,
        hold=hold,
    )
    hold.pop("chain", None)
    y4, _ = smooth(2, y3)
    y5, _ = smooth(2, y4)

    for name in ("t2", "d2", "b2", "y2"):
        del hold[name]
    hold |= {"t1a": tiles1[0], "t1b": tiles1[1]}
    x3 = call(
        prolong_one_kernel,
        field1,
        (idx1, t1, "d1", "x2", "groups", y5, *exchange(y5, route)),
        xs1,
        lead + [VMEM] * 9,
        hold=hold,
    )
    del hold["x2"], hold["groups"]
    x4, _ = smooth(1, x3)
    rim = sds((cols, RIM, LANES))
    spread, first, second = call(
        fine_spread_kernel,
        [sds((cols, rows, LANES)), rim, rim],
        (flags, t1, idx1, "d1", "b1", fine_groups, x4, *exchange(x4, route), own_part(x4)),
        xs1 + [pltpu.VMEM((count1, cols, LANES), F32)],
        [SMEM, VMEM, SMEM] + [VMEM] * 9,
        us=3,
        hold=hold,
    )
    o2, o1 = exchange_narrow(first, second, route)
    rim = sds((cols, RIM, 2 * LANES))
    for name in ("t1a", "t1b", "d1", "b1"):
        del hold[name]
    ext, first, second = call(
        fine_second_kernel,
        [sds((cols, rows, 2 * LANES)), rim, rim],
        (flags, spread, o2, o1),
        specs=[SMEM] + [VMEM] * 3,
        us=1,
        hold=hold,
    )
    o2, o1 = exchange_wide(first, second, route)
    whole = sds((cols, rows, LANES))
    return call(
        fine_up_kernel,
        whole,
        (flags, keep, ext, o2, o1),
        scratch=[pltpu.VMEM(whole.shape, F32), pltpu.SemaphoreType.DMA((cols,))],
        specs=[SMEM] + [VMEM] * 4,
        far=(0,),
    )


def solution(mesh):
    tile = P(("wide", "narrow"), None, None, None)
    pair = P(("wide", "narrow"), None)
    line = P(("wide", "narrow"))
    grid = P("wide", "narrow")
    chain = P("wide", None, None)
    field = P(None, "wide", "narrow")
    in_specs = (
        field, grid, grid, grid, tile, pair, pair, line, tile, pair, pair, line, chain, chain, chain,
    )
    sizes = (mesh.shape["wide"], mesh.shape["narrow"])
    return jax.shard_map(
        functools.partial(body, sizes), mesh=mesh, in_specs=in_specs, out_specs=field, check_vma=False
    )
```

```python
import functools

import jax
import jax.numpy as jnp
from jax import lax
from jax.experimental import pallas as pl
from jax.experimental.pallas import tpu as pltpu
from jax.sharding import PartitionSpec as P

F32 = jnp.float32
BF16 = jnp.bfloat16
SHIFT = 0.1
JACOBI = 0.6
LANES = 128
ORDER = 1
RIM = 4
PAD = 2 * RIM
VMEM = pl.BlockSpec(memory_space=pltpu.VMEM)
PLAIN = pl.BlockSpec(memory_space=pltpu.VMEM)
HBM = pl.BlockSpec(memory_space=pl.ANY)
SMEM = pl.BlockSpec(memory_space=pltpu.SMEM)
W_ODD, N_ODD, HAS_WEST, HAS_EAST, HAS_SOUTH, HAS_NORTH, W_AT, N_AT, LEVEL3 = range(9)


def sds(shape, dtype=F32):
    return jax.ShapeDtypeStruct(shape, dtype)


def constrain(x, spec):
    if spec is VMEM:
        return pltpu.with_memory_space_constraint(x, pltpu.VMEM)
    if spec is HBM:
        return pltpu.with_memory_space_constraint(x, pltpu.HBM)
    if spec is SMEM:
        return pltpu.with_memory_space_constraint(x, pltpu.SMEM)
    return x


def call(kernel, outs, ins, scratch=(), specs=None, mib=12, us=2, hold=None, far=(), loose=(), scalars=()):
    hold = {} if hold is None else hold
    outs, tree = jax.tree.flatten(outs)
    specs = jax.tree.leaves([[spec] * len(x) if isinstance(x, tuple) else spec for x, spec in zip(ins, specs)])
    ins, shape_in = jax.tree.flatten(list(ins))
    places = {x: i for i, x in enumerate(ins) if isinstance(x, str)}
    rest = [name for name in hold if name not in places]
    places |= {name: len(ins) + i for i, name in enumerate(rest)}
    inputs = [hold[x] if isinstance(x, str) else x for x in ins] + [hold[name] for name in rest]
    specs = list(specs) + [VMEM] * len(rest)
    inputs = [constrain(x, spec) for x, spec in zip(inputs, specs)]
    count_in, count_out = len(ins), len(outs)
    spaces = [pltpu.HBM if i in far else pltpu.SMEM if i in scalars else pltpu.VMEM for i in range(len(outs))]
    shapes = [o if i in loose else spaces[i](o.shape, o.dtype) for i, o in enumerate(outs)]
    shapes += [pltpu.VMEM(hold[name].shape, hold[name].dtype) for name in hold]

    def inner(*refs):
        first = len(inputs)
        kernel(
            *jax.tree.unflatten(shape_in, refs[:first][::ORDER][:count_in]),
            *refs[first : first + count_out],
            *refs[first + count_out + len(hold) :],
        )

    results = pl.pallas_call(
        inner,
        out_shape=shapes,
        in_specs=specs[::ORDER],
        out_specs=[{pltpu.HBM: HBM, pltpu.SMEM: SMEM, pltpu.VMEM: VMEM}[space] for space in spaces]
        + [VMEM] * len(hold),
        scratch_shapes=list(scratch),
        input_output_aliases={
            range(len(inputs))[::ORDER][places[name]]: count_out + i for i, name in enumerate(hold)
        },
        compiler_params=pltpu.CompilerParams(vmem_limit_bytes=mib * 1024 * 1024),
        cost_estimate=pl.CostEstimate(flops=0, bytes_accessed=int(us * 3.5e6), transcendentals=0),
    )(*inputs[::ORDER])
    for name, value in zip(list(hold), results[count_out:]):
        hold[name] = value
    return jax.tree.unflatten(tree, results[:count_out])


def parts_of(x):
    hi = x.astype(BF16).astype(F32)
    return hi, x - hi


def rows_of(x):
    return jnp.concatenate(parts_of(x), axis=0)


def twice(x):
    return jnp.concatenate([x, x], axis=0).astype(BF16)


def rows_sum(s):
    return s[0:4] + s[4:8]


def dot_nt(a, b):
    return lax.dot_general(a, b, (((1,), (1,)), ((), ())), preferred_element_type=F32)


def store_parts(xs, base, x):
    count, cols, _ = x.shape
    for i, part in enumerate(parts_of(x)):
        xs[pl.ds(base, count), i * cols : (i + 1) * cols, :] = part


def split_map(m):
    hi = m.astype(BF16)
    return hi, (m - hi.astype(F32)).astype(BF16)


def diagonal(tile):
    size = tile.shape[0]
    row = lax.broadcasted_iota(jnp.int32, tile.shape, 0)
    col = lax.broadcasted_iota(jnp.int32, tile.shape, 1)
    diag = jnp.sum(jnp.where(row == col, tile, 0.0), axis=0, keepdims=True)
    lane = lax.broadcasted_iota(jnp.int32, diag.shape, 1)
    return jnp.where(lane < size, diag, 1.0)


def split_tile(tile, r, k, t_ref):
    size = tile.shape[0]
    if size < LANES:
        tile = jnp.concatenate([tile, jnp.zeros((size, LANES - size), F32)], axis=1)
    hi, lo = split_map(tile)
    t_ref[r, 0:size, k * LANES : (k + 1) * LANES] = hi
    t_ref[r, LANES : LANES + size, k * LANES : (k + 1) * LANES] = lo
    return tile


class Stream:
    def __init__(self, half, tiles, held, t_ref, sems, parts=4):
        self.count, self.slots = held.shape[0], held.shape[1]
        self.step = self.count // parts
        self.held, self.t_ref = held, t_ref
        self.loads = [
            pltpu.make_async_copy(
                tiles.at[pl.ds(half * self.count + i * self.step, self.step)],
                held.at[pl.ds(i * self.step, self.step)],
                sems.at[i],
            )
            for i in range(parts)
        ]
        for load in self.loads:
            load.start()

    def run(self):
        for i, load in enumerate(self.loads):
            load.wait()
            for r in range(i * self.step, (i + 1) * self.step):
                for k in range(self.slots):
                    split_tile(self.held[r, k], r, k, self.t_ref)


def store_kernel(t_refs, _, *refs):
    *fars, sems = refs
    copies = [pltpu.make_async_copy(a, b, sems.at[i]) for i, (a, b) in enumerate(zip(t_refs, fars))]
    for copy in copies:
        copy.start()
    for copy in copies:
        copy.wait()


def half_kernel(half, tiles, _, t_ref, held, sems):
    Stream(half, tiles, held, t_ref, sems).run()


def setup_kernel(
    flags, columns1, live1, columns2, live2, tiles1, tiles2,
    idx1, idx2, d1, t2, d2,
    in1, in2, in3, in4, held2, fronts, held1, held_two, turned, sems,
):
    ins = [(columns1, in1), (live1, in2), (columns2, in3), (live2, in4), (tiles2, held2)]
    ins.append((tiles1.at[:, 0], fronts))
    ins = [pltpu.make_async_copy(a, b, sems.at[i]) for i, (a, b) in enumerate(ins)]
    for copy in ins:
        copy.start()
    for copy in ins:
        copy.wait()
    w_odd, n_odd = flags[W_ODD], flags[N_ODD]
    region = (0, 1 + w_odd, 2 - w_odd, 3 + n_odd, 4 - n_odd)
    there = (1, flags[HAS_WEST], flags[HAS_EAST], flags[HAS_SOUTH], flags[HAS_NORTH])
    for columns, live, held, dim in ((in1, in2, held1, 1), (in3, in4, held_two, 0)):
        code = columns[...]
        count = code.shape[dim]
        place = jnp.full(code.shape, 5 * count, jnp.int32)
        for s in range(5):
            at = code - s * count
            ok = (at >= 0) & (at < count) & (live[...] == 1) & (there[s] == 1)
            place = jnp.where(ok, at + region[s] * count, place)
        own = lax.broadcasted_iota(jnp.int32, held.shape, dim)
        held[...] = own
        if dim:
            held[1:, :] = place
        else:
            held[:, 1:] = place
    copies = [
        pltpu.make_async_copy(held1, idx1, sems.at[0]),
        pltpu.make_async_copy(held_two, turned, sems.at[1]),
    ]
    for copy in copies:
        copy.start()
    t2[...] = jnp.zeros_like(t2)
    for r in range(held2.shape[0]):
        for k in range(held2.shape[1]):
            tile = split_tile(held2[r, k], r, k, t2)
            if k == 0:
                row = lax.broadcasted_iota(jnp.int32, tile.shape, 0)
                col = lax.broadcasted_iota(jnp.int32, tile.shape, 1)
                diag = jnp.sum(jnp.where(row == col, tile, 0.0), axis=0, keepdims=True)
                lane = lax.broadcasted_iota(jnp.int32, diag.shape, 1)
                d2[r] = jnp.where(lane < tile.shape[0], diag, 1.0)
    for r in range(fronts.shape[0]):
        d1[r] = diagonal(fronts[r])
    for copy in copies:
        copy.wait()
    slots, count = idx2.shape
    for k in range(slots):
        for r in range(count):
            idx2[k, r] = turned[r, k]


def apply_tiles(t_ref, xs, idx, done=None):
    slots, count = idx.shape
    first = 0 if done is None else 1
    out = []
    for r in range(count):
        lhs = twice(jnp.concatenate([xs[idx[k, r]] for k in range(first, slots)], axis=1))
        t, at = t_ref[r // t_ref[0].shape[0]], r % t_ref[0].shape[0]
        both = dot_nt(lhs, t[at, :, first * LANES :])[0:8]
        value = rows_sum(both[:, :LANES] + both[:, LANES:])
        out.append(value if done is None else value + done[r])
    return out


def own_kernel(t_ref, x, out):
    for r in range(x.shape[0]):
        t, at = t_ref[r // t_ref[0].shape[0]], r % t_ref[0].shape[0]
        both = dot_nt(twice(rows_of(x[r])), t[at, :, :LANES])[0:8]
        out[r] = rows_sum(both[:, :LANES] + both[:, LANES:])


def fill_blocks(xs, own, others, count):
    xs[5 * count] = jnp.zeros((8, LANES), F32)
    store_parts(xs, 0, own[0:count])
    for i, other in enumerate(others):
        store_parts(xs, (i + 1) * count, other[0:count])


def ride(out, start, refs):
    for ref, first in refs:
        count = ref.shape[0] - first
        out[start : start + count] = ref[first:]
        start += count


def smooth_more_kernel(idx, t, d, b, own, o1, o2, o3, o4, done, out, xs):
    smooth_kernel(idx, t, d, b, own, o1, o2, o3, o4, out, xs, done)


def smooth_kernel(idx, t, d, b, own, o1, o2, o3, o4, out, xs, done=None):
    count = b.shape[0]
    fill_blocks(xs, own, (o1, o2, o3, o4), count)
    for r, ax in enumerate(apply_tiles(t, xs, idx, done)):
        out[r] = own[r] + JACOBI * (b[r] - ax) / d[r]


def smooth_ride_kernel(span, idx, t, d, b, own, o1, o2, o3, o4, maps, out, out_w, out_n, xs):
    smooth_kernel(idx, t, d, b, own, o1, o2, o3, o4, out, xs)
    at = b.shape[0]
    out_w[0:at] = out[...]
    out_n[0:at] = out[...]
    for ref in maps:
        for start in range(0, ref.shape[0], 2 * span):
            out_w[at : at + span] = ref[start : start + span]
            out_n[at : at + span] = ref[start + span : start + 2 * span]
            at += span


def residual_ride_kernel(
    idx, t, d, b, own, o1, o2, o3, o4, done, sent_w, sent_n, left, scaled, out_w, out_n, xs
):
    residual_kernel(idx, t, d, b, own, o1, o2, o3, o4, left, scaled, xs, done)
    count = b.shape[0]
    out_w[0:count] = scaled[...]
    out_n[0:count] = scaled[...]
    ride(out_n, count, ((sent_w, count), (o2, count)))
    ride(out_w, count, ((sent_n, count), (o3, count)))


def residual_more_kernel(idx, t, d, b, own, o1, o2, o3, o4, done, left, scaled, xs):
    residual_kernel(idx, t, d, b, own, o1, o2, o3, o4, left, scaled, xs, done)


def residual_kernel(idx, t, d, b, own, o1, o2, o3, o4, left, scaled, xs, done=None):
    count = b.shape[0]
    fill_blocks(xs, own, (o1, o2, o3, o4), count)
    for r, ax in enumerate(apply_tiles(t, xs, idx, done)):
        rest = b[r] - ax
        left[r] = rest
        scaled[r] = rest / d[r]


def restrict_one_kernel(idx, t, left, groups, d2, own, o1, o2, o3, o4, done, b2, first, xs):
    count = left.shape[0]
    fill_blocks(xs, own, (o1, o2, o3, o4), count)
    total = None
    coarse_tiles, _, lanes = b2.shape
    size = coarse_tiles * lanes // 2
    for r, ax in enumerate(apply_tiles(t, xs, idx, done)):
        rows = twice(rows_of(left[r] - 0.5 * ax))
        hot = lax.broadcasted_iota(jnp.int32, (size, LANES), 0) == groups[r : r + 1, :]
        term = dot_nt(rows, hot.astype(F32).astype(BF16))
        total = term if total is None else total + term
    total = rows_sum(total[0:8])
    half = LANES // 2
    lane = lax.broadcasted_iota(jnp.int32, (4, LANES), 1)
    for tile in range(coarse_tiles):
        pair = total[:, (tile // 2) * LANES : (tile // 2 + 1) * LANES]
        if tile % 2:
            pair = pltpu.roll(pair, half, 1)
        value = jnp.where(lane < half, pair, 0.0)
        b2[tile] = value
        first[tile] = JACOBI * value / d2[tile]


def restrict_two_kernel(flags, idx, t, left, groups, gain, own, o1, o2, o3, o4, out, xs):
    count = left.shape[0]
    fill_blocks(xs, own, (o1, o2, o3, o4), count)
    offset = flags[N_AT] * flags[LEVEL3]
    first = groups.shape[1] - count
    total = None
    for r, ax in enumerate(apply_tiles(t, xs, idx)):
        rows = twice(rows_of(left[r] - 0.5 * ax))
        group = groups[0, first + r : first + r + 1, :] + offset
        hot = lax.broadcasted_iota(jnp.int32, (LANES, LANES), 0) == group
        term = dot_nt(rows, hot.astype(F32).astype(BF16))
        total = term if total is None else total + term
    total = map_product(jnp.concatenate(split_map(gain[0]), axis=0), rows_sum(total[0:8]))
    out[...] = jnp.broadcast_to(total[None], out.shape)


def bundle_kernel(first, _, *refs):
    *pieces, out = refs
    ride(out, 0, [(ref, first) for ref in pieces])


def chain_maps_kernel(orders, flags, bundle, other, out):
    half = bundle.shape[0] // 2
    for i, order in enumerate(orders):
        position = 0
        span = half * 2 >> len(order)
        rows = span * bundle.shape[1]
        for ref in (bundle, other):
            for start in range(i * half, (i + 1) * half, span):
                v, q = flags[W_AT], flags[N_AT]
                for bit, (axis, step) in enumerate(order):
                    if position >> bit & 1:
                        v, q = (v ^ step, q) if axis == "wide" else (v, q ^ step)
                hi, lo = split_map(ref[start : start + span].reshape(rows, LANES))
                out[v, i, pl.ds(pl.multiple_of(q * rows, rows), rows), :] = hi
                out[v, i, pl.ds(pl.multiple_of(LANES + q * rows, rows), rows), :] = lo
                position += 1


def map_product(m, x):
    both = dot_nt(twice(rows_of(x)), m)[0:8]
    return rows_sum(both[:, :LANES] + both[:, LANES:])


def take_lanes(table, lanes):
    return jnp.take_along_axis(table, jnp.broadcast_to(lanes, table.shape), axis=1)


def groups_kernel(own1, own, o1, o2, o3, o4, out):
    count1 = own1.shape[0]
    for p, ref in enumerate((own, o1, o2, o3, o4)):
        cols = ref.shape[1]
        for i in range(out.shape[1]):
            row = ref[count1 + i // cols, i % cols : i % cols + 1, :]
            out[p, i : i + 1] = row.astype(jnp.int32)


def chain_kernel(flags, maps, pieces, idx, t, d, x2, groups, out, xs, ys):
    blocks = maps.shape[0]
    narrow = pieces.shape[0] // blocks
    carry = None
    for v in range(blocks):
        now = pieces[v * narrow]
        for k in range(1, narrow):
            now = now + pieces[v * narrow + k]
        if carry is not None:
            now = now + map_product(maps[v, 0], carry)
        ys[v] = now
        carry = now
    for v in range(blocks - 2, -1, -1):
        carry = ys[v] + map_product(maps[v, 1], carry)
        ys[v] = carry
    count = x2.shape[0]
    xs[5 * count] = jnp.zeros((8, LANES), F32)
    size = flags[LEVEL3]
    w, n, w_odd, n_odd = flags[W_AT], flags[N_AT], flags[W_ODD], flags[N_ODD]
    n_first = n + 1 - 2 * n_odd
    n_second = jnp.clip(n - 1 + 2 * n_odd, 0, narrow - 1)
    w_first = w + 1 - 2 * w_odd
    w_second = jnp.clip(w - 1 + 2 * w_odd, 0, blocks - 1)
    where = ((w, n), (w_second, n), (w_first, n), (w, n_second), (w, n_first))
    lane = lax.broadcasted_iota(jnp.int32, (8, LANES), 1)
    first = groups.shape[1] - count
    for p, (pw, pn) in enumerate(where):
        table = rows_of(ys[pw])
        for tile in range(count):
            index = groups[p, first + tile : first + tile + 1, :]
            index = (index + pn * size) & (LANES - 1)
            got = take_lanes(table, index)
            xs[p * count + tile] = jnp.where(lane < LANES // 2, got, 0.0)
    for r, ax in enumerate(apply_tiles(t, xs, idx)):
        out[r] = x2[r] + (rows_sum(xs[r]) - 0.5 * ax / d[r])


def prolong_one_kernel(idx, t, d, x2, groups, own, o1, o2, o3, o4, out, xs):
    count = x2.shape[0]
    xs[5 * count] = jnp.zeros((8, LANES), F32)
    half = LANES // 2
    lane = lax.broadcasted_iota(jnp.int32, (4, LANES), 1)
    for p, u in enumerate((own, o1, o2, o3, o4)):
        tables = []
        for i in range(u.shape[0] // 2):
            wide = jnp.where(lane < half, u[2 * i], pltpu.roll(u[2 * i + 1], half, 1))
            tables.append(rows_of(wide))
        for tile in range(count):
            index = groups[p, tile : tile + 1, :]
            got = take_lanes(tables[0], index & (LANES - 1))
            for i in range(1, len(tables)):
                more = take_lanes(tables[i], index & (LANES - 1))
                got = jnp.where((index >> 7) == i, more, got)
            xs[p * count + tile] = got
    for r, ax in enumerate(apply_tiles(t, xs, idx)):
        out[r] = x2[r] + (rows_sum(xs[r]) - 0.5 * ax / d[r])


def live_weights(flags, east, north):
    row = lax.broadcasted_iota(jnp.int32, east.shape, 0)
    col = lax.broadcasted_iota(jnp.int32, east.shape, 1)
    east = jnp.where((flags[HAS_EAST] == 1) | (row < east.shape[0] - 1), east, 0.0)
    north = jnp.where((flags[HAS_NORTH] == 1) | (col < north.shape[1] - 1), north, 0.0)
    return east, north


def narrow_rims(flags, fields, first, second):
    odd = flags[N_ODD] == 1
    for i, field in enumerate(fields):
        turned = field.T
        low, high = turned[0:RIM], turned[-RIM:]
        first[i] = jnp.where(odd, low, high)
        second[i] = jnp.where(odd, high, low)


def narrow_sides(flags, first, second, i):
    odd = flags[N_ODD] == 1
    low = jnp.where(odd, first[i], second[i]) * flags[HAS_SOUTH].astype(F32)
    high = jnp.where(odd, second[i], first[i]) * flags[HAS_NORTH].astype(F32)
    return low, high


def with_sides(flags, field, first, second, i):
    low, high = narrow_sides(flags, first, second, i)
    side = jnp.concatenate([high, jnp.zeros((LANES - 2 * RIM, LANES), F32), low], axis=0)
    return jnp.concatenate([field, side.T], axis=1)


def wide_rims(flags, field, i, first, second):
    odd = flags[W_ODD] == 1
    low, high = field[0:RIM], field[-RIM:]
    first[i] = jnp.where(odd, low, high)
    second[i] = jnp.where(odd, high, low)


def with_rows(flags, field, first, second, i):
    odd = flags[W_ODD] == 1
    low = jnp.where(odd, first[i], second[i]) * flags[HAS_WEST].astype(F32)
    high = jnp.where(odd, second[i], first[i]) * flags[HAS_EAST].astype(F32)
    return jnp.concatenate([field, high, low], axis=0)


def fine_first_kernel(
    sizes, block, east, north, forward, backward, flags, fields, first, second, piece, edges, maps, sems
):
    wide, narrow = sizes
    w, n = lax.axis_index("wide"), lax.axis_index("narrow")
    values = (
        w & 1, n & 1, w > 0, w < wide - 1, n > 0, n < narrow - 1, w, n, forward.shape[1] // narrow,
    )
    for i, value in enumerate(values):
        flags[i] = jnp.int32(value)
    cols = block.shape[0]
    rows = maps.shape[1]
    at = pl.multiple_of(n * rows, rows)
    copies = [
        (block, fields.at[0:cols]),
        (east, edges.at[0]),
        (north, edges.at[1]),
        (forward.at[0, pl.ds(at, rows)], maps.at[0]),
        (backward.at[0, pl.ds(at, rows)], maps.at[1]),
    ]
    copies = [pltpu.make_async_copy(a, b, sems.at[i]) for i, (a, b) in enumerate(copies)]
    for copy in copies:
        copy.start()
    for copy in copies:
        copy.wait()
    fields[cols], fields[cols + 1] = live_weights(flags, edges[0], edges[1])
    narrow_rims(flags, [fields[c] for c in range(cols + 2)], first, second)
    piece[...] = maps[...].reshape(piece.shape)


def fine_second_kernel(flags, fields, o2, o1, ext, first, second):
    for i in range(fields.shape[0]):
        wider = with_sides(flags, fields[i], o1, o2, i)
        ext[i] = wider
        wide_rims(flags, wider, i, first, second)


def beside(field, e, n):
    rows, lanes = field.shape
    return (
        e * pltpu.roll(field, rows - 1, 0)
        + pltpu.roll(e * field, 1, 0)
        + n * pltpu.roll(field, lanes - 1, 1)
        + pltpu.roll(n * field, 1, 1)
    )


def fine_down_kernel(flags, ext, o2, o1, groups, d1, near1, near2, far, b1, first, q_ref, keep, sem):
    cols = ext.shape[0] - 2
    rows = ext.shape[1]
    e = with_rows(flags, ext[cols], o1, o2, cols)
    n = with_rows(flags, ext[cols + 1], o1, o2, cols + 1)
    diag = SHIFT + e + pltpu.roll(e, 1, 0) + n + pltpu.roll(n, 1, 1)
    inv = 1.0 / diag
    step_inv = JACOBI * inv
    keep[2 * cols] = e
    keep[2 * cols + 1] = n
    keep[2 * cols + 2] = step_inv
    for c in range(cols):
        b = with_rows(flags, ext[c], o1, o2, c)
        x1 = b * step_inv
        x2 = (2.0 - JACOBI) * x1 + beside(x1, e, n) * step_inv
        keep[c] = x2
        keep[cols + c] = x1
        rest = b - diag * x2 + beside(x2, e, n)
        q = 0.5 * (rest + beside(rest * inv, e, n))
        for i, part in enumerate(parts_of(q[:rows, :LANES])):
            q_ref[i * cols + c] = part
    copy = pltpu.make_async_copy(keep, far, sem.at[0])
    copy.start()
    count = b1.shape[0]
    one, zero = jnp.ones((), BF16), jnp.zeros((), BF16)
    lanes = lax.broadcasted_iota(jnp.int32, (LANES, LANES), 0).astype(F32).astype(BF16)

    def over_rows(x):
        return jnp.broadcast_to(x, (16, LANES)).astype(BF16)

    left, right = [], []
    for row in range(rows):
        row = slice(row, row + 1)
        group = groups[row, :]
        mask = lanes[0:count] == over_rows((group >> 7).astype(F32))
        low = over_rows((group & (LANES - 1)).astype(F32))
        picked = [jnp.where(mask, over_rows(q_ref[i, row, :]), zero) for i in range(2 * cols)]
        left.append(jnp.concatenate(picked, axis=0))
        low = jnp.concatenate([low] * (LANES // 16), axis=0)
        right.append(jnp.where(lanes == low, one, zero))
    total = dot_nt(jnp.concatenate(left, axis=1), jnp.concatenate(right, axis=1))
    size = cols * count
    total = total[0:size] + total[size : 2 * size]
    for c in range(cols):
        value = total[c * count : (c + 1) * count]
        b1[:, c, :] = value
        first[0:count, c, :] = JACOBI * value / d1[:, 0, :]
    groups = [near1[i : i + 1, :] for i in range(count)]
    for i in range(near2.shape[0]):
        row = near2[i : i + 1, :]
        groups += [row, pltpu.roll(row, LANES // 2, 1)]
    for i, group in enumerate(groups):
        first[count + i // cols, i % cols : i % cols + 1, :] = group.astype(F32)
    copy.wait()


def fine_spread_kernel(flags, t, idx, d, b, groups, own, o1, o2, o3, o4, done, spread, first, second, xs, us):
    count, cols, _ = b.shape
    fill_blocks(xs, own, (o1, o2, o3, o4), count)
    for r, ax in enumerate(apply_tiles(t, xs, idx, done)):
        us[r] = own[r] + JACOBI * (b[r] - ax) / d[r]
    rows = groups.shape[0]
    tables = [[jnp.broadcast_to(us[h, c : c + 1, :], (8, LANES)) for h in range(count)] for c in range(cols)]
    for j in range(rows // 8):
        group = groups[8 * j : 8 * j + 8, :]
        high, low = group >> 7, group & (LANES - 1)
        masks = [high == h for h in range(1, count)]
        for c in range(cols):
            value = jnp.take_along_axis(tables[c][0], low, axis=1)
            for h in range(1, count):
                got = jnp.take_along_axis(tables[c][h], low, axis=1)
                value = jnp.where(masks[h - 1], got, value)
            spread[c, 8 * j : 8 * j + 8, :] = value
    narrow_rims(flags, [spread[c] for c in range(cols)], first, second)


def fine_up_kernel(flags, keep, ext, o2, o1, far, out, sems):
    cols = out.shape[0]
    copies = []
    e, n, step_inv = keep[2 * cols], keep[2 * cols + 1], keep[2 * cols + 2]
    half_inv = (0.5 / JACOBI) * step_inv
    for c in range(cols):
        x1 = keep[cols + c]
        spread = with_rows(flags, ext[c], o1, o2, c)
        x = keep[c] + 0.5 * spread + beside(spread, e, n) * half_inv
        for _ in range(2):
            x = (1.0 - JACOBI) * x + x1 + beside(x, e, n) * step_inv
        out[c] = x[: out.shape[1], :LANES]
        copies.append(pltpu.make_async_copy(out.at[c], far.at[c], sems.at[c]))
        copies[-1].start()
    for copy in copies:
        copy.wait()


def pairs(start, count):
    out = []
    for i in range(start, count - 1, 2):
        out += [(i, i + 1), (i + 1, i)]
    return out


def routes(wide, narrow):
    narrow_first = pairs(0, narrow)
    narrow_second = pairs(1, narrow) + [(0, narrow - 1), (narrow - 1, 0)]
    wide_first = pairs(0, wide)
    both = [(a * narrow + k, b * narrow + k) for a, b in pairs(1, wide) for k in range(narrow)]
    for a in (0, wide - 1):
        both += [(a * narrow + k, a * narrow + (k ^ 1)) for k in range(narrow)]
    return narrow_first, narrow_second, wide_first, both


def exchange_narrow(first, second, route):
    second = lax.ppermute(second, "narrow", route[1])
    return second, lax.ppermute(first, "narrow", route[0])


def exchange_wide(first, second, route):
    second = lax.ppermute(second, ("wide", "narrow"), route[3])
    return second, lax.ppermute(first, "wide", route[2])


def exchange(x, route, wide=None, second=None, first=None):
    pick = lambda y: x if y is None else y
    return (*exchange_wide(pick(wide), x, route), *exchange_narrow(pick(first), pick(second), route))


def body(
    sizes,
    block,
    east,
    north,
    fine_groups,
    tiles_one,
    columns_one,
    live_one,
    coarse_groups,
    tiles_two,
    columns_two,
    live_two,
    coarser_groups,
    chain_forward,
    chain_gain,
    chain_backward,
):
    wide, narrow = sizes
    route = routes(wide, narrow)
    cols = block.shape[0]
    rows = block.shape[1]
    count1, slots = tiles_one.shape[:2]
    count2 = tiles_two.shape[0]

    if narrow != 4 or wide & (wide - 1):
        raise NotImplementedError("mesh shape")
    alone = [("wide", 1 << i) for i in reversed(range(1, (wide - 1).bit_length()))]
    near_wide, near_narrow = ("wide", 1), ("narrow", narrow - 1)
    orders = [
        alone + [near_wide, near_narrow, ("narrow", 1)],
        alone + [near_narrow, near_wide, ("narrow", 1)],
    ]
    share = chain_forward.shape[1] // narrow
    held = []
    done = []

    def swap(x, axis, step):
        return lax.ppermute(x, axis, [(i, i ^ step) for i in range(lax.axis_size(axis))])

    def gather_step(anchor):
        step = alone[len(done)]
        merged = held if len(held) == 1 else [jnp.concatenate(held, axis=0)]
        merged, _ = lax.optimization_barrier((merged, anchor))
        held[:] = merged + [swap(m, *step) for m in merged]
        done.append(step)

    rim = sds((cols + 2, RIM, LANES))
    flags = sds((LEVEL3 + 1,), jnp.int32)
    flags, fields, first, second, piece = call(
        functools.partial(fine_first_kernel, sizes),
        [flags, sds((cols + 2, rows, LANES)), rim, rim, sds((2 * share // cols, cols, LANES))],
        (block, east, north, chain_forward, chain_backward),
        scratch=[
            pltpu.VMEM((2, rows, LANES), F32),
            pltpu.VMEM((2, share, LANES), F32),
            pltpu.SemaphoreType.DMA((5,)),
        ],
        specs=[HBM] * 5,
        scalars=(0,),
    )
    held.append(piece)
    gather_step(first)
    o2, o1 = exchange_narrow(first, second, route)

    half = count1 // 2
    split = sds((half, 2 * LANES, slots * LANES), BF16)
    held_tiles = [pltpu.VMEM((half, *tiles_one.shape[1:]), F32)]
    stream_sems = [pltpu.SemaphoreType.DMA((4,))]
    idx1, idx2, d1, tiles2, d2 = call(
        setup_kernel,
        [
            sds((slots, count1), jnp.int32),
            sds((slots, count2), jnp.int32),
            sds((count1, 1, LANES)),
            sds((count2, *split.shape[1:]), BF16),
            sds((count2, 1, LANES)),
        ],
        (flags, columns_one.T, live_one.T, columns_two, live_two, tiles_one, tiles_two),
        scratch=[pltpu.VMEM((slots - 1, count1), jnp.int32)] * 2
        + [pltpu.VMEM((count2, slots - 1), jnp.int32)] * 2
        + [
            pltpu.VMEM(tiles_two.shape, F32),
            pltpu.VMEM((count1, *tiles_one.shape[2:]), F32),
            pltpu.VMEM((slots, count1), jnp.int32),
            pltpu.VMEM((count2, slots), jnp.int32),
            pltpu.SMEM((count2, slots), jnp.int32),
            pltpu.SemaphoreType.DMA((6,)),
        ],
        specs=[SMEM] + [HBM] * 6,
        scalars=(0, 1),
    )
    groups1 = coarse_groups.reshape(count1, LANES)
    groups2 = coarser_groups.reshape(-1, LANES)
    o2, idx1, idx2, tiles2, d1, d2 = lax.optimization_barrier((o2, idx1, idx2, tiles2, d1, d2))

    rim = sds((cols + 2, RIM, 2 * LANES))
    ext, first, second = call(
        fine_second_kernel,
        [sds((cols + 2, rows, 2 * LANES)), rim, rim],
        (flags, fields, o2, o1),
        specs=[SMEM] + [VMEM] * 3,
    )
    if alone:
        gather_step(first)
    o2, o1 = exchange_wide(first, second, route)

    def split_half(i, after):
        return call(
            functools.partial(half_kernel, i),
            split,
            (tiles_one, after),
            scratch=held_tiles + stream_sems,
            specs=[HBM, VMEM],
        )

    tiles1 = split_half(0, first)
    field1 = sds((count1, cols, LANES))
    field2 = sds((count2, cols, LANES))
    more = -(-(count1 + count2) // cols)
    hold = {"t1a": tiles1, "d1": d1}
    t1 = ("t1a", "t1b")
    kept = sds((2 * cols + 3, rows + PAD, 2 * LANES))
    x1_rows = count1 + more
    keep, b1, x1 = call(
        fine_down_kernel,
        [kept, field1, sds((x1_rows, cols, LANES))],
        (flags, ext, o2, o1, fine_groups, "d1", groups1, groups2),
        scratch=[
            pltpu.VMEM((2 * cols, rows, LANES), F32),
            pltpu.VMEM(kept.shape, F32),
            pltpu.SemaphoreType.DMA((1,)),
        ],
        specs=[SMEM] + [VMEM] * 7,
        mib=16,
        us=7,
        hold=hold,
        far=(0,),
    )
    hold["b1"] = b1

    xs1 = [pltpu.VMEM((5 * count1 + 1, 8, LANES), F32)]
    xs2 = [pltpu.VMEM((5 * count2 + 1, 8, LANES), F32)]
    lead = [SMEM]

    def own_part(x):
        return call(own_kernel, field1, (tuple(hold[name] for name in t1), x), specs=[VMEM, VMEM], us=0.5)

    def smooth(level, x):
        idx, like, xs = (idx1, field1, xs1) if level == 1 else (idx2, field2, xs2)
        near = exchange(x, route)
        ins = (idx, t1 if level == 1 else ("t2",), f"d{level}", f"b{level}", x, *near)
        if level == 1:
            ins = (*ins, own_part(x))
        kernel = smooth_more_kernel if level == 1 else smooth_kernel
        return call(kernel, like, ins, xs, lead + [VMEM] * (len(ins) - 1), hold=hold), near

    while len(done) < len(alone):
        gather_step(x1)
    near = exchange(x1, route)
    hold["t1b"] = split_half(1, b1)
    maps_rows = sum(x.shape[0] for x in held)
    riding = sds((count1 + maps_rows // 2, cols, LANES))
    x2, x2_w, x2_n = call(
        functools.partial(smooth_ride_kernel, share // cols),
        [field1, riding, riding],
        (idx1, t1, "d1", "b1", x1, *near, tuple(held)),
        xs1,
        lead + [VMEM] * 9,
        hold=hold,
    )
    groups = call(
        groups_kernel,
        sds((5, count1 + count2, LANES), jnp.int32),
        (groups1, x1, *near),
        specs=[VMEM] * 6,
        us=1,
    )
    near = exchange(x2, route, wide=x2_w, second=x2_n)
    hold |= {"x2": x2, "groups": groups, "d2": d2}
    riding = sds((count1 + maps_rows, cols, LANES))
    left, scaled, scaled_w, scaled_n = call(
        residual_ride_kernel,
        [field1, field1, riding, riding],
        (idx1, t1, "d1", "b1", "x2", *near, own_part(x2), x2_w, x2_n),
        xs1,
        lead + [VMEM] * 11,
        hold=hold,
    )
    near = exchange(scaled, route, wide=scaled_w, second=scaled_n)
    maps = (scaled_n, near[2], scaled_w, near[1])
    b2, y1 = call(
        restrict_one_kernel,
        [field2, field2],
        (idx1, t1, left, groups1, "d2", scaled, *near, own_part(scaled)),
        xs1,
        lead + [VMEM] * 10,
        hold=hold,
    )

    near = exchange(y1, route)
    bundle = call(
        functools.partial(bundle_kernel, count1),
        sds((4 * maps_rows, cols, LANES)),
        (y1, *maps),
        specs=[VMEM] * 5,
        us=0.5,
    )
    maps = (bundle, lax.ppermute(bundle, "narrow", route[0]))
    tiles1 = call(
        store_kernel,
        [split, split],
        (t1, y1),
        scratch=[pltpu.SemaphoreType.DMA((2,))],
        specs=[VMEM, VMEM],
        far=(0, 1),
        hold=hold,
    )
    del hold["t1a"], hold["t1b"]
    hold |= {"b2": b2, "t2": tiles2}
    y2 = call(
        smooth_kernel, field2, (idx2, ("t2",), "d2", "b2", y1, *near), xs2, lead + [VMEM] * 8, hold=hold
    )
    near = exchange(y2, route)
    hold["y2"] = y2
    left, scaled = call(
        residual_kernel,
        [field2, field2],
        (idx2, ("t2",), "d2", "b2", "y2", *near),
        xs2,
        lead + [VMEM] * 8,
        us=1,
        hold=hold,
    )
    maps, scaled = lax.optimization_barrier((maps, scaled))
    near = exchange(scaled, route)
    chain_shape = sds((wide, 2, 2 * LANES, LANES), BF16)
    big = wide > 16
    chain = call(
        functools.partial(chain_maps_kernel, orders),
        chain_shape,
        (flags, *maps),
        specs=[SMEM] + [PLAIN if big else VMEM] * 2,
        mib=48 if big else 12,
        us=0.7,
        loose=(0,) if big else (),
    )
    if not big:
        hold["chain"] = chain
    out3 = call(
        restrict_two_kernel,
        sds((wide * narrow, cols, LANES)),
        (flags, idx2, ("t2",), left, "groups", chain_gain, scaled, *near),
        xs2,
        [SMEM, SMEM] + [VMEM] * 9,
        hold=hold,
    )
    pieces = lax.all_to_all(out3, ("wide", "narrow"), 0, 0)
    y3 = call(
        chain_kernel,
        field2,
        (flags, chain if big else "chain", pieces, idx2, ("t2",), "d2", "y2", "groups"),
        xs2 + [pltpu.VMEM((wide, cols, LANES), F32)],
        [SMEM, PLAIN if big else VMEM, VMEM, SMEM] + [VMEM] * 4,
        mib=32 if big else 12,
        us=3,
        hold=hold,
    )
    hold.pop("chain", None)
    y4, _ = smooth(2, y3)
    y5, _ = smooth(2, y4)

    for name in ("t2", "d2", "b2", "y2"):
        del hold[name]
    hold |= {"t1a": tiles1[0], "t1b": tiles1[1]}
    x3 = call(
        prolong_one_kernel,
        field1,
        (idx1, t1, "d1", "x2", "groups", y5, *exchange(y5, route)),
        xs1,
        lead + [VMEM] * 9,
        hold=hold,
    )
    del hold["x2"], hold["groups"]
    x4, _ = smooth(1, x3)
    rim = sds((cols, RIM, LANES))
    spread, first, second = call(
        fine_spread_kernel,
        [sds((cols, rows, LANES)), rim, rim],
        (flags, t1, idx1, "d1", "b1", fine_groups, x4, *exchange(x4, route), own_part(x4)),
        xs1 + [pltpu.VMEM((count1, cols, LANES), F32)],
        [SMEM, VMEM, SMEM] + [VMEM] * 9,
        us=3,
        hold=hold,
    )
    o2, o1 = exchange_narrow(first, second, route)
    rim = sds((cols, RIM, 2 * LANES))
    for name in ("t1a", "t1b", "d1", "b1"):
        del hold[name]
    ext, first, second = call(
        fine_second_kernel,
        [sds((cols, rows, 2 * LANES)), rim, rim],
        (flags, spread, o2, o1),
        specs=[SMEM] + [VMEM] * 3,
        us=1,
        hold=hold,
    )
    o2, o1 = exchange_wide(first, second, route)
    whole = sds((cols, rows, LANES))
    return call(
        fine_up_kernel,
        whole,
        (flags, keep, ext, o2, o1),
        scratch=[pltpu.VMEM(whole.shape, F32), pltpu.SemaphoreType.DMA((cols,))],
        specs=[SMEM] + [VMEM] * 4,
        far=(0,),
    )


def solution(mesh):
    tile = P(("wide", "narrow"), None, None, None)
    pair = P(("wide", "narrow"), None)
    line = P(("wide", "narrow"))
    grid = P("wide", "narrow")
    chain = P("wide", None, None)
    field = P(None, "wide", "narrow")
    in_specs = (
        field, grid, grid, grid, tile, pair, pair, line, tile, pair, pair, line, chain, chain, chain,
    )
    sizes = (mesh.shape["wide"], mesh.shape["narrow"])
    return jax.shard_map(
        functools.partial(body, sizes), mesh=mesh, in_specs=in_specs, out_specs=field, check_vma=False
    )
```

```python
import functools

import jax
import jax.numpy as jnp
from jax import lax
from jax.experimental import pallas as pl
from jax.experimental.pallas import tpu as pltpu
from jax.sharding import PartitionSpec as P

F32 = jnp.float32
BF16 = jnp.bfloat16
SHIFT = 0.1
JACOBI = 0.6
LANES = 128
ORDER = 1
RIM = 4
PAD = 2 * RIM
VMEM = pl.BlockSpec(memory_space=pltpu.VMEM)
PLAIN = pl.BlockSpec(memory_space=pltpu.VMEM)
HBM = pl.BlockSpec(memory_space=pl.ANY)
SMEM = pl.BlockSpec(memory_space=pltpu.SMEM)
W_ODD, N_ODD, HAS_WEST, HAS_EAST, HAS_SOUTH, HAS_NORTH, W_AT, N_AT, LEVEL3 = range(9)


def sds(shape, dtype=F32):
    return jax.ShapeDtypeStruct(shape, dtype)


def constrain(x, spec):
    if spec is VMEM:
        return pltpu.with_memory_space_constraint(x, pltpu.VMEM)
    if spec is HBM:
        return pltpu.with_memory_space_constraint(x, pltpu.HBM)
    if spec is SMEM:
        return pltpu.with_memory_space_constraint(x, pltpu.SMEM)
    return x


def call(kernel, outs, ins, scratch=(), specs=None, mib=12, us=2, hold=None, far=(), loose=(), scalars=()):
    hold = {} if hold is None else hold
    outs, tree = jax.tree.flatten(outs)
    specs = jax.tree.leaves([[spec] * len(x) if isinstance(x, tuple) else spec for x, spec in zip(ins, specs)])
    ins, shape_in = jax.tree.flatten(list(ins))
    places = {x: i for i, x in enumerate(ins) if isinstance(x, str)}
    rest = [name for name in hold if name not in places]
    places |= {name: len(ins) + i for i, name in enumerate(rest)}
    inputs = [hold[x] if isinstance(x, str) else x for x in ins] + [hold[name] for name in rest]
    specs = list(specs) + [VMEM] * len(rest)
    inputs = [constrain(x, spec) for x, spec in zip(inputs, specs)]
    count_in, count_out = len(ins), len(outs)
    spaces = [pltpu.HBM if i in far else pltpu.SMEM if i in scalars else pltpu.VMEM for i in range(len(outs))]
    shapes = [o if i in loose else spaces[i](o.shape, o.dtype) for i, o in enumerate(outs)]
    shapes += [pltpu.VMEM(hold[name].shape, hold[name].dtype) for name in hold]

    def inner(*refs):
        first = len(inputs)
        kernel(
            *jax.tree.unflatten(shape_in, refs[:first][::ORDER][:count_in]),
            *refs[first : first + count_out],
            *refs[first + count_out + len(hold) :],
        )

    results = pl.pallas_call(
        inner,
        out_shape=shapes,
        in_specs=specs[::ORDER],
        out_specs=[{pltpu.HBM: HBM, pltpu.SMEM: SMEM, pltpu.VMEM: VMEM}[space] for space in spaces]
        + [VMEM] * len(hold),
        scratch_shapes=list(scratch),
        input_output_aliases={
            range(len(inputs))[::ORDER][places[name]]: count_out + i for i, name in enumerate(hold)
        },
        compiler_params=pltpu.CompilerParams(vmem_limit_bytes=mib * 1024 * 1024),
        cost_estimate=pl.CostEstimate(flops=0, bytes_accessed=int(us * 3.5e6), transcendentals=0),
    )(*inputs[::ORDER])
    for name, value in zip(list(hold), results[count_out:]):
        hold[name] = value
    return jax.tree.unflatten(tree, results[:count_out])


def parts_of(x):
    hi = x.astype(BF16).astype(F32)
    return hi, x - hi


def rows_of(x):
    return jnp.concatenate(parts_of(x), axis=0)


def twice(x):
    return jnp.concatenate([x, x], axis=0).astype(BF16)


def rows_sum(s):
    return s[0:4] + s[4:8]


def dot_nt(a, b):
    return lax.dot_general(a, b, (((1,), (1,)), ((), ())), preferred_element_type=F32)


def store_parts(xs, base, x):
    count, cols, _ = x.shape
    for i, part in enumerate(parts_of(x)):
        xs[pl.ds(base, count), i * cols : (i + 1) * cols, :] = part


def split_map(m):
    hi = m.astype(BF16)
    return hi, (m - hi.astype(F32)).astype(BF16)


def diagonal(tile):
    size = tile.shape[0]
    row = lax.broadcasted_iota(jnp.int32, tile.shape, 0)
    col = lax.broadcasted_iota(jnp.int32, tile.shape, 1)
    diag = jnp.sum(jnp.where(row == col, tile, 0.0), axis=0, keepdims=True)
    lane = lax.broadcasted_iota(jnp.int32, diag.shape, 1)
    return jnp.where(lane < size, diag, 1.0)


def split_tile(tile, r, k, t_ref):
    size = tile.shape[0]
    if size < LANES:
        tile = jnp.concatenate([tile, jnp.zeros((size, LANES - size), F32)], axis=1)
    hi, lo = split_map(tile)
    t_ref[r, 0:size, k * LANES : (k + 1) * LANES] = hi
    t_ref[r, LANES : LANES + size, k * LANES : (k + 1) * LANES] = lo
    return tile


class Stream:
    def __init__(self, half, tiles, held, t_ref, sems, parts=4):
        self.count, self.slots = held.shape[0], held.shape[1]
        self.step = self.count // parts
        self.held, self.t_ref = held, t_ref
        self.loads = [
            pltpu.make_async_copy(
                tiles.at[pl.ds(half * self.count + i * self.step, self.step)],
                held.at[pl.ds(i * self.step, self.step)],
                sems.at[i],
            )
            for i in range(parts)
        ]
        for load in self.loads:
            load.start()

    def run(self):
        for i, load in enumerate(self.loads):
            load.wait()
            for r in range(i * self.step, (i + 1) * self.step):
                for k in range(self.slots):
                    split_tile(self.held[r, k], r, k, self.t_ref)


def store_kernel(t_refs, _, *refs):
    *fars, sems = refs
    copies = [pltpu.make_async_copy(a, b, sems.at[i]) for i, (a, b) in enumerate(zip(t_refs, fars))]
    for copy in copies:
        copy.start()
    for copy in copies:
        copy.wait()


def half_kernel(half, tiles, _, t_ref, held, sems):
    Stream(half, tiles, held, t_ref, sems).run()


def setup_kernel(
    flags, columns1, live1, columns2, live2, tiles1, tiles2,
    idx1, idx2, d1, t2, d2,
    in1, in2, in3, in4, held2, fronts, held1, held_two, turned, sems,
):
    ins = [(columns1, in1), (live1, in2), (columns2, in3), (live2, in4), (tiles2, held2)]
    ins.append((tiles1.at[:, 0], fronts))
    ins = [pltpu.make_async_copy(a, b, sems.at[i]) for i, (a, b) in enumerate(ins)]
    for copy in ins:
        copy.start()
    for copy in ins:
        copy.wait()
    w_odd, n_odd = flags[W_ODD], flags[N_ODD]
    region = (0, 1 + w_odd, 2 - w_odd, 3 + n_odd, 4 - n_odd)
    there = (1, flags[HAS_WEST], flags[HAS_EAST], flags[HAS_SOUTH], flags[HAS_NORTH])
    for columns, live, held, dim in ((in1, in2, held1, 1), (in3, in4, held_two, 0)):
        code = columns[...]
        count = code.shape[dim]
        place = jnp.full(code.shape, 5 * count, jnp.int32)
        for s in range(5):
            at = code - s * count
            ok = (at >= 0) & (at < count) & (live[...] == 1) & (there[s] == 1)
            place = jnp.where(ok, at + region[s] * count, place)
        own = lax.broadcasted_iota(jnp.int32, held.shape, dim)
        held[...] = own
        if dim:
            held[1:, :] = place
        else:
            held[:, 1:] = place
    copies = [
        pltpu.make_async_copy(held1, idx1, sems.at[0]),
        pltpu.make_async_copy(held_two, turned, sems.at[1]),
    ]
    for copy in copies:
        copy.start()
    t2[...] = jnp.zeros_like(t2)
    for r in range(held2.shape[0]):
        for k in range(held2.shape[1]):
            tile = split_tile(held2[r, k], r, k, t2)
            if k == 0:
                row = lax.broadcasted_iota(jnp.int32, tile.shape, 0)
                col = lax.broadcasted_iota(jnp.int32, tile.shape, 1)
                diag = jnp.sum(jnp.where(row == col, tile, 0.0), axis=0, keepdims=True)
                lane = lax.broadcasted_iota(jnp.int32, diag.shape, 1)
                d2[r] = jnp.where(lane < tile.shape[0], diag, 1.0)
    for r in range(fronts.shape[0]):
        d1[r] = diagonal(fronts[r])
    for copy in copies:
        copy.wait()
    slots, count = idx2.shape
    for k in range(slots):
        for r in range(count):
            idx2[k, r] = turned[r, k]


def apply_tiles(t_ref, xs, idx, done=None):
    slots, count = idx.shape
    first = 0 if done is None else 1
    out = []
    for r in range(count):
        lhs = twice(jnp.concatenate([xs[idx[k, r]] for k in range(first, slots)], axis=1))
        t, at = t_ref[r // t_ref[0].shape[0]], r % t_ref[0].shape[0]
        both = dot_nt(lhs, t[at, :, first * LANES :])[0:8]
        value = rows_sum(both[:, :LANES] + both[:, LANES:])
        out.append(value if done is None else value + done[r])
    return out


def own_kernel(t_ref, x, out):
    for r in range(x.shape[0]):
        t, at = t_ref[r // t_ref[0].shape[0]], r % t_ref[0].shape[0]
        both = dot_nt(twice(rows_of(x[r])), t[at, :, :LANES])[0:8]
        out[r] = rows_sum(both[:, :LANES] + both[:, LANES:])


def fill_blocks(xs, own, others, count):
    xs[5 * count] = jnp.zeros((8, LANES), F32)
    store_parts(xs, 0, own[0:count])
    for i, other in enumerate(others):
        store_parts(xs, (i + 1) * count, other[0:count])


def ride(out, start, refs):
    for ref, first in refs:
        count = ref.shape[0] - first
        out[start : start + count] = ref[first:]
        start += count


def smooth_more_kernel(idx, t, d, b, own, o1, o2, o3, o4, done, out, xs):
    smooth_kernel(idx, t, d, b, own, o1, o2, o3, o4, out, xs, done)


def smooth_kernel(idx, t, d, b, own, o1, o2, o3, o4, out, xs, done=None):
    count = b.shape[0]
    fill_blocks(xs, own, (o1, o2, o3, o4), count)
    for r, ax in enumerate(apply_tiles(t, xs, idx, done)):
        out[r] = own[r] + JACOBI * (b[r] - ax) / d[r]


def smooth_ride_kernel(span, idx, t, d, b, own, o1, o2, o3, o4, maps, out, out_w, out_n, xs):
    smooth_kernel(idx, t, d, b, own, o1, o2, o3, o4, out, xs)
    at = b.shape[0]
    out_w[0:at] = out[...]
    out_n[0:at] = out[...]
    for ref in maps:
        for start in range(0, ref.shape[0], 2 * span):
            out_w[at : at + span] = ref[start : start + span]
            out_n[at : at + span] = ref[start + span : start + 2 * span]
            at += span


def residual_ride_kernel(
    idx, t, d, b, own, o1, o2, o3, o4, done, sent_w, sent_n, left, scaled, out_w, out_n, xs
):
    residual_kernel(idx, t, d, b, own, o1, o2, o3, o4, left, scaled, xs, done)
    count = b.shape[0]
    out_w[0:count] = scaled[...]
    out_n[0:count] = scaled[...]
    ride(out_n, count, ((sent_w, count), (o2, count)))
    ride(out_w, count, ((sent_n, count), (o3, count)))


def residual_more_kernel(idx, t, d, b, own, o1, o2, o3, o4, done, left, scaled, xs):
    residual_kernel(idx, t, d, b, own, o1, o2, o3, o4, left, scaled, xs, done)


def residual_kernel(idx, t, d, b, own, o1, o2, o3, o4, left, scaled, xs, done=None):
    count = b.shape[0]
    fill_blocks(xs, own, (o1, o2, o3, o4), count)
    for r, ax in enumerate(apply_tiles(t, xs, idx, done)):
        rest = b[r] - ax
        left[r] = rest
        scaled[r] = rest / d[r]


def restrict_one_kernel(idx, t, left, groups, d2, own, o1, o2, o3, o4, done, b2, first, xs):
    count = left.shape[0]
    fill_blocks(xs, own, (o1, o2, o3, o4), count)
    total = None
    coarse_tiles, _, lanes = b2.shape
    size = coarse_tiles * lanes // 2
    for r, ax in enumerate(apply_tiles(t, xs, idx, done)):
        rows = twice(rows_of(left[r] - 0.5 * ax))
        hot = lax.broadcasted_iota(jnp.int32, (size, LANES), 0) == groups[r : r + 1, :]
        term = dot_nt(rows, hot.astype(F32).astype(BF16))
        total = term if total is None else total + term
    total = rows_sum(total[0:8])
    half = LANES // 2
    lane = lax.broadcasted_iota(jnp.int32, (4, LANES), 1)
    for tile in range(coarse_tiles):
        pair = total[:, (tile // 2) * LANES : (tile // 2 + 1) * LANES]
        if tile % 2:
            pair = pltpu.roll(pair, half, 1)
        value = jnp.where(lane < half, pair, 0.0)
        b2[tile] = value
        first[tile] = JACOBI * value / d2[tile]


def restrict_two_kernel(flags, idx, t, left, groups, gain, own, o1, o2, o3, o4, out, xs):
    count = left.shape[0]
    fill_blocks(xs, own, (o1, o2, o3, o4), count)
    offset = flags[N_AT] * flags[LEVEL3]
    first = groups.shape[1] - count
    total = None
    for r, ax in enumerate(apply_tiles(t, xs, idx)):
        rows = twice(rows_of(left[r] - 0.5 * ax))
        group = groups[0, first + r : first + r + 1, :] + offset
        hot = lax.broadcasted_iota(jnp.int32, (LANES, LANES), 0) == group
        term = dot_nt(rows, hot.astype(F32).astype(BF16))
        total = term if total is None else total + term
    total = map_product(jnp.concatenate(split_map(gain[0]), axis=0), rows_sum(total[0:8]))
    out[...] = jnp.broadcast_to(total[None], out.shape)


def bundle_kernel(first, _, *refs):
    *pieces, out = refs
    ride(out, 0, [(ref, first) for ref in pieces])


def chain_maps_kernel(orders, flags, bundle, other, out):
    half = bundle.shape[0] // 2
    for i, order in enumerate(orders):
        position = 0
        span = half * 2 >> len(order)
        rows = span * bundle.shape[1]
        for ref in (bundle, other):
            for start in range(i * half, (i + 1) * half, span):
                v, q = flags[W_AT], flags[N_AT]
                for bit, (axis, step) in enumerate(order):
                    if position >> bit & 1:
                        v, q = (v ^ step, q) if axis == "wide" else (v, q ^ step)
                hi, lo = split_map(ref[start : start + span].reshape(rows, LANES))
                out[v, i, pl.ds(pl.multiple_of(q * rows, rows), rows), :] = hi
                out[v, i, pl.ds(pl.multiple_of(LANES + q * rows, rows), rows), :] = lo
                position += 1


def map_product(m, x):
    both = dot_nt(twice(rows_of(x)), m)[0:8]
    return rows_sum(both[:, :LANES] + both[:, LANES:])


def take_lanes(table, lanes):
    return jnp.take_along_axis(table, jnp.broadcast_to(lanes, table.shape), axis=1)


def groups_kernel(own1, own, o1, o2, o3, o4, out):
    count1 = own1.shape[0]
    for p, ref in enumerate((own, o1, o2, o3, o4)):
        cols = ref.shape[1]
        for i in range(out.shape[1]):
            row = ref[count1 + i // cols, i % cols : i % cols + 1, :]
            out[p, i : i + 1] = row.astype(jnp.int32)


def chain_kernel(flags, maps, pieces, idx, t, d, x2, groups, out, xs, ys):
    blocks = maps.shape[0]
    narrow = pieces.shape[0] // blocks
    carry = None
    for v in range(blocks):
        now = pieces[v * narrow]
        for k in range(1, narrow):
            now = now + pieces[v * narrow + k]
        if carry is not None:
            now = now + map_product(maps[v, 0], carry)
        ys[v] = now
        carry = now
    for v in range(blocks - 2, -1, -1):
        carry = ys[v] + map_product(maps[v, 1], carry)
        ys[v] = carry
    count = x2.shape[0]
    xs[5 * count] = jnp.zeros((8, LANES), F32)
    size = flags[LEVEL3]
    w, n, w_odd, n_odd = flags[W_AT], flags[N_AT], flags[W_ODD], flags[N_ODD]
    n_first = n + 1 - 2 * n_odd
    n_second = jnp.clip(n - 1 + 2 * n_odd, 0, narrow - 1)
    w_first = w + 1 - 2 * w_odd
    w_second = jnp.clip(w - 1 + 2 * w_odd, 0, blocks - 1)
    where = ((w, n), (w_second, n), (w_first, n), (w, n_second), (w, n_first))
    lane = lax.broadcasted_iota(jnp.int32, (8, LANES), 1)
    first = groups.shape[1] - count
    for p, (pw, pn) in enumerate(where):
        table = rows_of(ys[pw])
        for tile in range(count):
            index = groups[p, first + tile : first + tile + 1, :]
            index = (index + pn * size) & (LANES - 1)
            got = take_lanes(table, index)
            xs[p * count + tile] = jnp.where(lane < LANES // 2, got, 0.0)
    for r, ax in enumerate(apply_tiles(t, xs, idx)):
        out[r] = x2[r] + (rows_sum(xs[r]) - 0.5 * ax / d[r])


def prolong_one_kernel(idx, t, d, x2, groups, own, o1, o2, o3, o4, out, xs):
    count = x2.shape[0]
    xs[5 * count] = jnp.zeros((8, LANES), F32)
    half = LANES // 2
    lane = lax.broadcasted_iota(jnp.int32, (4, LANES), 1)
    for p, u in enumerate((own, o1, o2, o3, o4)):
        tables = []
        for i in range(u.shape[0] // 2):
            wide = jnp.where(lane < half, u[2 * i], pltpu.roll(u[2 * i + 1], half, 1))
            tables.append(rows_of(wide))
        for tile in range(count):
            index = groups[p, tile : tile + 1, :]
            got = take_lanes(tables[0], index & (LANES - 1))
            for i in range(1, len(tables)):
                more = take_lanes(tables[i], index & (LANES - 1))
                got = jnp.where((index >> 7) == i, more, got)
            xs[p * count + tile] = got
    for r, ax in enumerate(apply_tiles(t, xs, idx)):
        out[r] = x2[r] + (rows_sum(xs[r]) - 0.5 * ax / d[r])


def live_weights(flags, east, north):
    row = lax.broadcasted_iota(jnp.int32, east.shape, 0)
    col = lax.broadcasted_iota(jnp.int32, east.shape, 1)
    east = jnp.where((flags[HAS_EAST] == 1) | (row < east.shape[0] - 1), east, 0.0)
    north = jnp.where((flags[HAS_NORTH] == 1) | (col < north.shape[1] - 1), north, 0.0)
    return east, north


def narrow_rims(flags, fields, first, second):
    odd = flags[N_ODD] == 1
    for i, field in enumerate(fields):
        turned = field.T
        low, high = turned[0:RIM], turned[-RIM:]
        first[i] = jnp.where(odd, low, high)
        second[i] = jnp.where(odd, high, low)


def narrow_sides(flags, first, second, i):
    odd = flags[N_ODD] == 1
    low = jnp.where(odd, first[i], second[i]) * flags[HAS_SOUTH].astype(F32)
    high = jnp.where(odd, second[i], first[i]) * flags[HAS_NORTH].astype(F32)
    return low, high


def with_sides(flags, field, first, second, i):
    low, high = narrow_sides(flags, first, second, i)
    side = jnp.concatenate([high, jnp.zeros((LANES - 2 * RIM, LANES), F32), low], axis=0)
    return jnp.concatenate([field, side.T], axis=1)


def wide_rims(flags, field, i, first, second):
    odd = flags[W_ODD] == 1
    low, high = field[0:RIM], field[-RIM:]
    first[i] = jnp.where(odd, low, high)
    second[i] = jnp.where(odd, high, low)


def with_rows(flags, field, first, second, i):
    odd = flags[W_ODD] == 1
    low = jnp.where(odd, first[i], second[i]) * flags[HAS_WEST].astype(F32)
    high = jnp.where(odd, second[i], first[i]) * flags[HAS_EAST].astype(F32)
    return jnp.concatenate([field, high, low], axis=0)


def fine_first_kernel(
    sizes, block, east, north, forward, backward, flags, fields, first, second, piece, edges, maps, sems
):
    wide, narrow = sizes
    w, n = lax.axis_index("wide"), lax.axis_index("narrow")
    values = (
        w & 1, n & 1, w > 0, w < wide - 1, n > 0, n < narrow - 1, w, n, forward.shape[1] // narrow,
    )
    for i, value in enumerate(values):
        flags[i] = jnp.int32(value)
    cols = block.shape[0]
    rows = maps.shape[1]
    at = pl.multiple_of(n * rows, rows)
    copies = [
        (block, fields.at[0:cols]),
        (east, edges.at[0]),
        (north, edges.at[1]),
        (forward.at[0, pl.ds(at, rows)], maps.at[0]),
        (backward.at[0, pl.ds(at, rows)], maps.at[1]),
    ]
    copies = [pltpu.make_async_copy(a, b, sems.at[i]) for i, (a, b) in enumerate(copies)]
    for copy in copies:
        copy.start()
    for copy in copies:
        copy.wait()
    fields[cols], fields[cols + 1] = live_weights(flags, edges[0], edges[1])
    narrow_rims(flags, [fields[c] for c in range(cols + 2)], first, second)
    piece[...] = maps[...].reshape(piece.shape)


def fine_second_kernel(flags, fields, o2, o1, ext, first, second):
    for i in range(fields.shape[0]):
        wider = with_sides(flags, fields[i], o1, o2, i)
        ext[i] = wider
        wide_rims(flags, wider, i, first, second)


def beside(field, e, n):
    rows, lanes = field.shape
    return (
        e * pltpu.roll(field, rows - 1, 0)
        + pltpu.roll(e * field, 1, 0)
        + n * pltpu.roll(field, lanes - 1, 1)
        + pltpu.roll(n * field, 1, 1)
    )


def fine_down_kernel(flags, ext, o2, o1, groups, d1, near1, near2, far, b1, first, q_ref, keep, sem):
    cols = ext.shape[0] - 2
    rows = ext.shape[1]
    e = with_rows(flags, ext[cols], o1, o2, cols)
    n = with_rows(flags, ext[cols + 1], o1, o2, cols + 1)
    diag = SHIFT + e + pltpu.roll(e, 1, 0) + n + pltpu.roll(n, 1, 1)
    inv = 1.0 / diag
    step_inv = JACOBI * inv
    keep[2 * cols] = e
    keep[2 * cols + 1] = n
    keep[2 * cols + 2] = step_inv
    for c in range(cols):
        b = with_rows(flags, ext[c], o1, o2, c)
        x1 = b * step_inv
        x2 = (2.0 - JACOBI) * x1 + beside(x1, e, n) * step_inv
        keep[c] = x2
        keep[cols + c] = x1
        rest = b - diag * x2 + beside(x2, e, n)
        q = 0.5 * (rest + beside(rest * inv, e, n))
        for i, part in enumerate(parts_of(q[:rows, :LANES])):
            q_ref[i * cols + c] = part
    copy = pltpu.make_async_copy(keep, far, sem.at[0])
    copy.start()
    count = b1.shape[0]
    one, zero = jnp.ones((), BF16), jnp.zeros((), BF16)
    lanes = lax.broadcasted_iota(jnp.int32, (LANES, LANES), 0).astype(F32).astype(BF16)

    def over_rows(x):
        return jnp.broadcast_to(x, (16, LANES)).astype(BF16)

    left, right = [], []
    for row in range(rows):
        row = slice(row, row + 1)
        group = groups[row, :]
        mask = lanes[0:count] == over_rows((group >> 7).astype(F32))
        low = over_rows((group & (LANES - 1)).astype(F32))
        picked = [jnp.where(mask, over_rows(q_ref[i, row, :]), zero) for i in range(2 * cols)]
        left.append(jnp.concatenate(picked, axis=0))
        low = jnp.concatenate([low] * (LANES // 16), axis=0)
        right.append(jnp.where(lanes == low, one, zero))
    total = dot_nt(jnp.concatenate(left, axis=1), jnp.concatenate(right, axis=1))
    size = cols * count
    total = total[0:size] + total[size : 2 * size]
    for c in range(cols):
        value = total[c * count : (c + 1) * count]
        b1[:, c, :] = value
        first[0:count, c, :] = JACOBI * value / d1[:, 0, :]
    groups = [near1[i : i + 1, :] for i in range(count)]
    for i in range(near2.shape[0]):
        row = near2[i : i + 1, :]
        groups += [row, pltpu.roll(row, LANES // 2, 1)]
    for i, group in enumerate(groups):
        first[count + i // cols, i % cols : i % cols + 1, :] = group.astype(F32)
    copy.wait()


def fine_spread_kernel(flags, t, idx, d, b, groups, own, o1, o2, o3, o4, done, spread, first, second, xs, us):
    count, cols, _ = b.shape
    fill_blocks(xs, own, (o1, o2, o3, o4), count)
    for r, ax in enumerate(apply_tiles(t, xs, idx, done)):
        us[r] = own[r] + JACOBI * (b[r] - ax) / d[r]
    rows = groups.shape[0]
    tables = [[jnp.broadcast_to(us[h, c : c + 1, :], (8, LANES)) for h in range(count)] for c in range(cols)]
    for j in range(rows // 8):
        group = groups[8 * j : 8 * j + 8, :]
        high, low = group >> 7, group & (LANES - 1)
        masks = [high == h for h in range(1, count)]
        for c in range(cols):
            value = jnp.take_along_axis(tables[c][0], low, axis=1)
            for h in range(1, count):
                got = jnp.take_along_axis(tables[c][h], low, axis=1)
                value = jnp.where(masks[h - 1], got, value)
            spread[c, 8 * j : 8 * j + 8, :] = value
    narrow_rims(flags, [spread[c] for c in range(cols)], first, second)


def fine_up_kernel(flags, keep, ext, o2, o1, far, out, sems):
    cols = out.shape[0]
    copies = []
    e, n, step_inv = keep[2 * cols], keep[2 * cols + 1], keep[2 * cols + 2]
    half_inv = (0.5 / JACOBI) * step_inv
    for c in range(cols):
        x1 = keep[cols + c]
        spread = with_rows(flags, ext[c], o1, o2, c)
        x = keep[c] + 0.5 * spread + beside(spread, e, n) * half_inv
        for _ in range(2):
            x = (1.0 - JACOBI) * x + x1 + beside(x, e, n) * step_inv
        out[c] = x[: out.shape[1], :LANES]
        copies.append(pltpu.make_async_copy(out.at[c], far.at[c], sems.at[c]))
        copies[-1].start()
    for copy in copies:
        copy.wait()


def pairs(start, count):
    out = []
    for i in range(start, count - 1, 2):
        out += [(i, i + 1), (i + 1, i)]
    return out


def routes(wide, narrow):
    narrow_first = pairs(0, narrow)
    narrow_second = pairs(1, narrow) + [(0, narrow - 1), (narrow - 1, 0)]
    wide_first = pairs(0, wide)
    both = [(a * narrow + k, b * narrow + k) for a, b in pairs(1, wide) for k in range(narrow)]
    for a in (0, wide - 1):
        both += [(a * narrow + k, a * narrow + (k ^ 1)) for k in range(narrow)]
    return narrow_first, narrow_second, wide_first, both


def exchange_narrow(first, second, route):
    second = lax.ppermute(second, "narrow", route[1])
    return second, lax.ppermute(first, "narrow", route[0])


def exchange_wide(first, second, route):
    second = lax.ppermute(second, ("wide", "narrow"), route[3])
    return second, lax.ppermute(first, "wide", route[2])


def exchange(x, route, wide=None, second=None, first=None):
    pick = lambda y: x if y is None else y
    return (*exchange_wide(pick(wide), x, route), *exchange_narrow(pick(first), pick(second), route))


def body(
    sizes,
    block,
    east,
    north,
    fine_groups,
    tiles_one,
    columns_one,
    live_one,
    coarse_groups,
    tiles_two,
    columns_two,
    live_two,
    coarser_groups,
    chain_forward,
    chain_gain,
    chain_backward,
):
    wide, narrow = sizes
    route = routes(wide, narrow)
    cols = block.shape[0]
    rows = block.shape[1]
    count1, slots = tiles_one.shape[:2]
    count2 = tiles_two.shape[0]

    if narrow != 4 or wide & (wide - 1):
        raise NotImplementedError("mesh shape")
    alone = [("wide", 1 << i) for i in reversed(range(1, (wide - 1).bit_length()))]
    near_wide, near_narrow = ("wide", 1), ("narrow", narrow - 1)
    orders = [
        alone + [near_wide, near_narrow, ("narrow", 1)],
        alone + [near_narrow, near_wide, ("narrow", 1)],
    ]
    share = chain_forward.shape[1] // narrow
    held = []
    done = []

    def swap(x, axis, step):
        return lax.ppermute(x, axis, [(i, i ^ step) for i in range(lax.axis_size(axis))])

    def gather_step(anchor):
        step = alone[len(done)]
        merged = held if len(held) == 1 else [jnp.concatenate(held, axis=0)]
        merged, anchor = lax.optimization_barrier((merged, anchor))
        held[:] = merged + [swap(m, *step) for m in merged]
        done.append(step)
        return anchor

    rim = sds((cols + 2, RIM, LANES))
    flags = sds((LEVEL3 + 1,), jnp.int32)
    flags, fields, first, second, piece = call(
        functools.partial(fine_first_kernel, sizes),
        [flags, sds((cols + 2, rows, LANES)), rim, rim, sds((2 * share // cols, cols, LANES))],
        (block, east, north, chain_forward, chain_backward),
        scratch=[
            pltpu.VMEM((2, rows, LANES), F32),
            pltpu.VMEM((2, share, LANES), F32),
            pltpu.SemaphoreType.DMA((5,)),
        ],
        specs=[HBM] * 5,
        scalars=(0,),
    )
    held.append(piece)
    gather_step(first)
    o2, o1 = exchange_narrow(first, second, route)

    half = count1 // 2
    split = sds((half, 2 * LANES, slots * LANES), BF16)
    held_tiles = [pltpu.VMEM((half, *tiles_one.shape[1:]), F32)]
    stream_sems = [pltpu.SemaphoreType.DMA((4,))]
    idx1, idx2, d1, tiles2, d2 = call(
        setup_kernel,
        [
            sds((slots, count1), jnp.int32),
            sds((slots, count2), jnp.int32),
            sds((count1, 1, LANES)),
            sds((count2, *split.shape[1:]), BF16),
            sds((count2, 1, LANES)),
        ],
        (flags, columns_one.T, live_one.T, columns_two, live_two, tiles_one, tiles_two),
        scratch=[pltpu.VMEM((slots - 1, count1), jnp.int32)] * 2
        + [pltpu.VMEM((count2, slots - 1), jnp.int32)] * 2
        + [
            pltpu.VMEM(tiles_two.shape, F32),
            pltpu.VMEM((count1, *tiles_one.shape[2:]), F32),
            pltpu.VMEM((slots, count1), jnp.int32),
            pltpu.VMEM((count2, slots), jnp.int32),
            pltpu.SMEM((count2, slots), jnp.int32),
            pltpu.SemaphoreType.DMA((6,)),
        ],
        specs=[SMEM] + [HBM] * 6,
        scalars=(0, 1),
    )
    groups1 = coarse_groups.reshape(count1, LANES)
    groups2 = coarser_groups.reshape(-1, LANES)
    o2, idx1, idx2, tiles2, d1, d2 = lax.optimization_barrier((o2, idx1, idx2, tiles2, d1, d2))

    rim = sds((cols + 2, RIM, 2 * LANES))
    ext, first, second = call(
        fine_second_kernel,
        [sds((cols + 2, rows, 2 * LANES)), rim, rim],
        (flags, fields, o2, o1),
        specs=[SMEM] + [VMEM] * 3,
    )
    if alone:
        first, second = gather_step((first, second))
    o2, o1 = exchange_wide(first, second, route)

    def split_half(i, after):
        return call(
            functools.partial(half_kernel, i),
            split,
            (tiles_one, after),
            scratch=held_tiles + stream_sems,
            specs=[HBM, VMEM],
        )

    tiles1 = split_half(0, first)
    field1 = sds((count1, cols, LANES))
    field2 = sds((count2, cols, LANES))
    more = -(-(count1 + count2) // cols)
    hold = {"t1a": tiles1, "d1": d1}
    t1 = ("t1a", "t1b")
    kept = sds((2 * cols + 3, rows + PAD, 2 * LANES))
    x1_rows = count1 + more
    keep, b1, x1 = call(
        fine_down_kernel,
        [kept, field1, sds((x1_rows, cols, LANES))],
        (flags, ext, o2, o1, fine_groups, "d1", groups1, groups2),
        scratch=[
            pltpu.VMEM((2 * cols, rows, LANES), F32),
            pltpu.VMEM(kept.shape, F32),
            pltpu.SemaphoreType.DMA((1,)),
        ],
        specs=[SMEM] + [VMEM] * 7,
        mib=16,
        us=7,
        hold=hold,
        far=(0,),
    )
    hold["b1"] = b1

    xs1 = [pltpu.VMEM((5 * count1 + 1, 8, LANES), F32)]
    xs2 = [pltpu.VMEM((5 * count2 + 1, 8, LANES), F32)]
    lead = [SMEM]

    def own_part(x):
        return call(own_kernel, field1, (tuple(hold[name] for name in t1), x), specs=[VMEM, VMEM], us=0.5)

    def smooth(level, x):
        idx, like, xs = (idx1, field1, xs1) if level == 1 else (idx2, field2, xs2)
        near = exchange(x, route)
        ins = (idx, t1 if level == 1 else ("t2",), f"d{level}", f"b{level}", x, *near)
        if level == 1:
            ins = (*ins, own_part(x))
        kernel = smooth_more_kernel if level == 1 else smooth_kernel
        return call(kernel, like, ins, xs, lead + [VMEM] * (len(ins) - 1), hold=hold), near

    while len(done) < len(alone):
        gather_step(x1)
    near = exchange(x1, route)
    hold["t1b"] = split_half(1, b1)
    maps_rows = sum(x.shape[0] for x in held)
    riding = sds((count1 + maps_rows // 2, cols, LANES))
    x2, x2_w, x2_n = call(
        functools.partial(smooth_ride_kernel, share // cols),
        [field1, riding, riding],
        (idx1, t1, "d1", "b1", x1, *near, tuple(held)),
        xs1,
        lead + [VMEM] * 9,
        hold=hold,
    )
    groups = call(
        groups_kernel,
        sds((5, count1 + count2, LANES), jnp.int32),
        (groups1, x1, *near),
        specs=[VMEM] * 6,
        us=1,
    )
    near = exchange(x2, route, wide=x2_w, second=x2_n)
    hold |= {"x2": x2, "groups": groups, "d2": d2}
    riding = sds((count1 + maps_rows, cols, LANES))
    left, scaled, scaled_w, scaled_n = call(
        residual_ride_kernel,
        [field1, field1, riding, riding],
        (idx1, t1, "d1", "b1", "x2", *near, own_part(x2), x2_w, x2_n),
        xs1,
        lead + [VMEM] * 11,
        hold=hold,
    )
    near = exchange(scaled, route, wide=scaled_w, second=scaled_n)
    maps = (scaled_n, near[2], scaled_w, near[1])
    b2, y1 = call(
        restrict_one_kernel,
        [field2, field2],
        (idx1, t1, left, groups1, "d2", scaled, *near, own_part(scaled)),
        xs1,
        lead + [VMEM] * 10,
        hold=hold,
    )

    near = exchange(y1, route)
    bundle = call(
        functools.partial(bundle_kernel, count1),
        sds((4 * maps_rows, cols, LANES)),
        (y1, *maps),
        specs=[VMEM] * 5,
        us=0.5,
    )
    maps = (bundle, lax.ppermute(bundle, "narrow", route[0]))
    tiles1 = call(
        store_kernel,
        [split, split],
        (t1, y1),
        scratch=[pltpu.SemaphoreType.DMA((2,))],
        specs=[VMEM, VMEM],
        far=(0, 1),
        hold=hold,
    )
    del hold["t1a"], hold["t1b"]
    hold |= {"b2": b2, "t2": tiles2}
    y2 = call(
        smooth_kernel, field2, (idx2, ("t2",), "d2", "b2", y1, *near), xs2, lead + [VMEM] * 8, hold=hold
    )
    near = exchange(y2, route)
    hold["y2"] = y2
    left, scaled = call(
        residual_kernel,
        [field2, field2],
        (idx2, ("t2",), "d2", "b2", "y2", *near),
        xs2,
        lead + [VMEM] * 8,
        us=1,
        hold=hold,
    )
    maps, scaled = lax.optimization_barrier((maps, scaled))
    near = exchange(scaled, route)
    chain_shape = sds((wide, 2, 2 * LANES, LANES), BF16)
    big = wide > 16
    chain = call(
        functools.partial(chain_maps_kernel, orders),
        chain_shape,
        (flags, *maps),
        specs=[SMEM] + [PLAIN if big else VMEM] * 2,
        mib=48 if big else 12,
        us=0.7,
        loose=(0,) if big else (),
    )
    if not big:
        hold["chain"] = chain
    out3 = call(
        restrict_two_kernel,
        sds((wide * narrow, cols, LANES)),
        (flags, idx2, ("t2",), left, "groups", chain_gain, scaled, *near),
        xs2,
        [SMEM, SMEM] + [VMEM] * 9,
        hold=hold,
    )
    pieces = lax.all_to_all(out3, ("wide", "narrow"), 0, 0)
    y3 = call(
        chain_kernel,
        field2,
        (flags, chain if big else "chain", pieces, idx2, ("t2",), "d2", "y2", "groups"),
        xs2 + [pltpu.VMEM((wide, cols, LANES), F32)],
        [SMEM, PLAIN if big else VMEM, VMEM, SMEM] + [VMEM] * 4,
        mib=32 if big else 12,
        us=3,
        hold=hold,
    )
    hold.pop("chain", None)
    y4, _ = smooth(2, y3)
    y5, _ = smooth(2, y4)

    for name in ("t2", "d2", "b2", "y2"):
        del hold[name]
    hold |= {"t1a": tiles1[0], "t1b": tiles1[1]}
    x3 = call(
        prolong_one_kernel,
        field1,
        (idx1, t1, "d1", "x2", "groups", y5, *exchange(y5, route)),
        xs1,
        lead + [VMEM] * 9,
        hold=hold,
    )
    del hold["x2"], hold["groups"]
    x4, _ = smooth(1, x3)
    rim = sds((cols, RIM, LANES))
    spread, first, second = call(
        fine_spread_kernel,
        [sds((cols, rows, LANES)), rim, rim],
        (flags, t1, idx1, "d1", "b1", fine_groups, x4, *exchange(x4, route), own_part(x4)),
        xs1 + [pltpu.VMEM((count1, cols, LANES), F32)],
        [SMEM, VMEM, SMEM] + [VMEM] * 9,
        us=3,
        hold=hold,
    )
    o2, o1 = exchange_narrow(first, second, route)
    rim = sds((cols, RIM, 2 * LANES))
    for name in ("t1a", "t1b", "d1", "b1"):
        del hold[name]
    ext, first, second = call(
        fine_second_kernel,
        [sds((cols, rows, 2 * LANES)), rim, rim],
        (flags, spread, o2, o1),
        specs=[SMEM] + [VMEM] * 3,
        us=1,
        hold=hold,
    )
    o2, o1 = exchange_wide(first, second, route)
    whole = sds((cols, rows, LANES))
    return call(
        fine_up_kernel,
        whole,
        (flags, keep, ext, o2, o1),
        scratch=[pltpu.VMEM(whole.shape, F32), pltpu.SemaphoreType.DMA((cols,))],
        specs=[SMEM] + [VMEM] * 4,
        far=(0,),
    )


def solution(mesh):
    tile = P(("wide", "narrow"), None, None, None)
    pair = P(("wide", "narrow"), None)
    line = P(("wide", "narrow"))
    grid = P("wide", "narrow")
    chain = P("wide", None, None)
    field = P(None, "wide", "narrow")
    in_specs = (
        field, grid, grid, grid, tile, pair, pair, line, tile, pair, pair, line, chain, chain, chain,
    )
    sizes = (mesh.shape["wide"], mesh.shape["narrow"])
    return jax.shard_map(
        functools.partial(body, sizes), mesh=mesh, in_specs=in_specs, out_specs=field, check_vma=False
    )
```
